32 devices in a mesh: seq: 8 (over z, y), ch: 4 (over x, core).
Axes of the slice: x: 2, y: 2, z: 4, core: 2. Of those that a mesh axis runs over, the one named last changes fastest.
Arguments:
- tokens: bfloat16 [16, 512, 1024], P('seq', 'ch'), may hold values from -6 to 6
- grad_out: bfloat16 [16, 512, 1024], P('seq', 'ch'), may hold values from -6 to 6
- lengths: int32 [16], P('seq'), may hold values from 64 to 512, as said below
- init_num: float32 [16, 1024], P('seq'), may hold values from -300 to 300
- init_den: float32 [16, 1024], P('seq'), may hold values from 20 to 400
- w_key: bfloat16 [1024, 1024], replicated, may hold values from -0.1875 to 0.1875
- w_value: bfloat16 [1024, 1024], replicated, may hold values from -0.1875 to 0.1875
- w_recept: bfloat16 [1024, 1024], replicated, may hold values from -0.1875 to 0.1875
- w_output: bfloat16 [1024, 1024], replicated, may hold values from -0.75 to 0.75
- w_expand: bfloat16 [1024, 4096], replicated, may hold values from -0.1875 to 0.1875
- w_contract: bfloat16 [4096, 1024], replicated, may hold values from -0.09375 to 0.09375
- w_gate: bfloat16 [1024, 1024], replicated, may hold values from -0.1875 to 0.1875
- gain_mix: float32 [1024], replicated, may hold values from 0.5 to 1.5
- bias_mix: float32 [1024], replicated, may hold values from -1.2 to 1.2
- gain_ffn: float32 [1024], replicated, may hold values from 0.5 to 1.5
- bias_ffn: float32 [1024], replicated, may hold values from -1.2 to 1.2
- mix_key: float32 [1024], replicated, may hold values from 0 to 1
- mix_value: float32 [1024], replicated, may hold values from 0 to 1
- mix_recept: float32 [1024], replicated, may hold values from 0 to 1
- blend_key: float32 [1024], replicated, may hold values from 0 to 1
- blend_gate: float32 [1024], replicated, may hold values from 0 to 1
- time_decay: float32 [1024], replicated, may hold values from -9 to -2.5
- time_first: float32 [1024], replicated, may hold values from -1 to 2
Outputs:
- mixed_out: bfloat16 [16, 512, 1024], P('seq', 'ch')
- grad_tokens: bfloat16 [16, 512, 1024], P('seq', 'ch')
- final_num: float32 [16, 1024], P('seq', 'ch')
- final_den: float32 [16, 1024], P('seq', 'ch')
- grad_w_key: float32 [1024, 1024], P('seq', 'ch')
- grad_w_value: float32 [1024, 1024], P('seq', 'ch')
- grad_w_recept: float32 [1024, 1024], P('seq', 'ch')
- grad_w_output: float32 [1024, 1024], P('seq', 'ch')
- grad_w_expand: float32 [1024, 4096], P('seq', 'ch')
- grad_w_contract: float32 [4096, 1024], P('seq', 'ch')
- grad_w_gate: float32 [1024, 1024], P('seq', 'ch')
- grad_gain_mix: float32 [1024], P(('seq', 'ch'))
- grad_bias_mix: float32 [1024], P(('seq', 'ch'))
- grad_gain_ffn: float32 [1024], P(('seq', 'ch'))
- grad_bias_ffn: float32 [1024], P(('seq', 'ch'))
- grad_mix_key: float32 [1024], P(('seq', 'ch'))
- grad_mix_value: float32 [1024], P(('seq', 'ch'))
- grad_mix_recept: float32 [1024], P(('seq', 'ch'))
- grad_blend_key: float32 [1024], P(('seq', 'ch'))
- grad_blend_gate: float32 [1024], P(('seq', 'ch'))
- grad_time_decay: float32 [1024], P(('seq', 'ch'))
- grad_time_first: float32 [1024], P(('seq', 'ch'))
The draws below stay inside these ranges and needn't reach their ends.
Inputs may be any that keep to these rules, and one draw needn't show every extreme that they name: Slot s is filled in its first lengths[s] positions. Among each 2 consecutive slots, one, drawn from the seed, is full.
All inputs are finite; a program needn't handle non-finite values.
Results may differ from the reference program's by a relative error of at most 0.02.
Values may be sent and summed in bfloat16 or wider, within the bound.
A program may use at most 192 MiB of HBM per device.

```python
import math
import jax
import jax.numpy as jnp
from jax import lax

D = 1024
FF = 4096
SEQS_GRP = 2
MINLEN = 64
SLOT = 512
SLOTS = 16


def draw_lengths(key, part):
    subkeys = jax.random.split(key, 2)
    samples = jax.random.randint(subkeys[0], (3, SLOTS), 0, SLOT - MINLEN + 1)
    shorter = MINLEN + jnp.min(samples, axis=0)
    chosen = jax.random.randint(subkeys[1], (SLOTS // SEQS_GRP, 1), 0, SEQS_GRP)
    member = lax.broadcasted_iota(jnp.int32, (SLOTS // SEQS_GRP, SEQS_GRP), 1)
    is_full = (member == chosen).reshape(SLOTS)
    return jnp.where(is_full, SLOT, shorter).astype(jnp.int32)


def block_scale(own_key, shape, cuts, least, largest):
    level = 1.0
    for axis_at, parts in cuts:
        steps = jax.random.uniform(jax.random.fold_in(jax.random.fold_in(own_key, 6), axis_at), (parts,), jnp.float32, least / len(cuts), largest / len(cuts))
        level = level * jnp.repeat(jnp.exp(steps), shape[axis_at] // parts).reshape((-1,) + (1,) * (len(shape) - 1 - axis_at))
    return level


def noise(key, shape, deviation, bound, cuts=(), held_as=jnp.bfloat16):
    level = block_scale(key, shape, cuts, -0.22, 0.18) if cuts else 1.0
    values = jax.random.normal(key, shape, jnp.float32) * deviation * level
    return jnp.minimum(jnp.maximum(values, -bound), bound).astype(held_as)


def setup_inputs(seed: int = 0) -> dict:
    splits = jax.random.split(jax.random.key(seed), 24)
    tokens = noise(splits[0], (SLOTS, SLOT, D), 1.0, 6.0, ((0, 8), (1, 4)))
    grad_out = noise(splits[1], (SLOTS, SLOT, D), 1.0, 6.0, ((0, 8), (1, 4)))
    lengths = draw_lengths(jax.random.fold_in(splits[23], 71), 0)
    init_num = noise(splits[3], (SLOTS, D), 50.0, 300.0, ((0, 8),), jnp.float32)
    init_den = jnp.clip(jnp.exp(math.log(400.0) - 2.9957323 * jax.random.uniform(splits[4], (SLOTS, D), jnp.float32) ** block_scale(splits[4], (SLOTS, D), ((0, 8),), -0.2, 0.2)), 20.0, 400.0)
    w_key = noise(splits[5], (D, D), D ** -0.5, 0.1875)
    w_value = noise(splits[6], (D, D), D ** -0.5, 0.1875)
    w_recept = noise(splits[7], (D, D), D ** -0.5, 0.1875)
    w_output = noise(splits[8], (D, D), (D // 16) ** -0.5, 0.75)
    w_expand = noise(splits[9], (D, FF), D ** -0.5, 0.1875)
    w_contract = noise(splits[10], (FF, D), FF ** -0.5, 0.09375)
    w_gate = noise(splits[11], (D, D), D ** -0.5, 0.1875)
    gain_mix = jnp.clip(1.0 + 0.1 * jax.random.normal(splits[12], (D,), jnp.float32), 0.5, 1.5)
    bias_mix = noise(splits[13], (D,), 0.2, 1.2, (), jnp.float32)
    gain_ffn = jnp.clip(1.0 + 0.1 * jax.random.normal(splits[14], (D,), jnp.float32), 0.5, 1.5)
    bias_ffn = noise(splits[15], (D,), 0.2, 1.2, (), jnp.float32)
    mix_key = jnp.clip(jax.random.uniform(splits[16], (D,), jnp.float32, 0.0, 1.0), 0.0, 1.0)
    mix_value = jnp.clip(jax.random.uniform(splits[17], (D,), jnp.float32, 0.0, 1.0), 0.0, 1.0)
    mix_recept = jnp.clip(jax.random.uniform(splits[18], (D,), jnp.float32, 0.0, 1.0), 0.0, 1.0)
    blend_key = jnp.clip(jax.random.uniform(splits[19], (D,), jnp.float32, 0.0, 1.0), 0.0, 1.0)
    blend_gate = jnp.clip(jax.random.uniform(splits[20], (D,), jnp.float32, 0.0, 1.0), 0.0, 1.0)
    time_decay = jnp.clip(jax.random.uniform(splits[21], (D,), jnp.float32, -9.0, -2.5), -9.0, -2.5)
    time_first = jnp.clip(jax.random.uniform(splits[22], (D,), jnp.float32, -1.0, 2.0), -1.0, 2.0)
    return dict(tokens=tokens, grad_out=grad_out, lengths=lengths, init_num=init_num, init_den=init_den, w_key=w_key, w_value=w_value, w_recept=w_recept, w_output=w_output, w_expand=w_expand, w_contract=w_contract, w_gate=w_gate, gain_mix=gain_mix, bias_mix=bias_mix, gain_ffn=gain_ffn, bias_ffn=bias_ffn, mix_key=mix_key, mix_value=mix_value, mix_recept=mix_recept, blend_key=blend_key, blend_gate=blend_gate, time_decay=time_decay, time_first=time_first)


@jax.custom_vjp
def low(v):
    return lax.optimization_barrier(v.astype(jnp.bfloat16)).astype(jnp.float32)

@jax.custom_vjp
def low_back(v):
    return v

def low_keep(v):
    return (low(v), None)

def low_pass(kept, grad):
    return (grad,)

def back_keep(v):
    return (v, None)

def back_low(kept, grad):
    return (low(grad),)
low.defvjp(low_keep, low_pass)
low_back.defvjp(back_keep, back_low)
EPS = 1e-05

def layer_norm(rows_in, gain, bias):
    center = rows_in - lax.optimization_barrier(jnp.mean(rows_in, axis=-1, keepdims=True))
    factor = lax.rsqrt(lax.optimization_barrier(jnp.mean(center * center, axis=-1, keepdims=True)) + EPS)
    return center * factor * gain + bias

def shifted(rows_in):
    return jnp.concatenate([jnp.zeros_like(rows_in[:, :1]), rows_in[:, :-1]], axis=1)

def blend_rows(current, earlier, weights):
    return current * weights + earlier * (1.0 - weights)

def matmul(rows_in, scaling_coefficient):
    return jnp.einsum('nsd,de->nse', rows_in, scaling_coefficient, precision=lax.Precision.HIGHEST)

def carry_update_rule(lookup_array, payload_array, occupied_lines, fading_pace, first_token_reward, opening_upper_total, opening_normalizer):

    def advance(carried, inputs_now):
        upper_accumulator, normalizer_total = carried
        current_lookup, current_payload, filled_now = inputs_now
        reward_share_term = jnp.exp(first_token_reward + current_lookup)
        layer_answer = (upper_accumulator + reward_share_term * current_payload) / (normalizer_total + reward_share_term)
        keep_factor = jnp.exp(-fading_pace * filled_now[:, None])
        scaling_coefficient = filled_now[:, None] * jnp.exp(current_lookup)
        return ((keep_factor * upper_accumulator + scaling_coefficient * current_payload, keep_factor * normalizer_total + scaling_coefficient), layer_answer)
    finals, outputs = lax.scan(advance, (opening_upper_total, opening_normalizer), (jnp.swapaxes(lookup_array, 0, 1), jnp.swapaxes(payload_array, 0, 1), jnp.swapaxes(occupied_lines, 0, 1)))
    return (jnp.swapaxes(outputs, 0, 1), finals)

def block_forward(rows_in, params, occupied_lines, opening_upper_total, opening_normalizer):
    w_key, w_value, w_recept, w_output, w_expand, w_contract, w_gate, gain_mix, bias_mix, gain_ffn, bias_ffn, mix_key, mix_value, mix_recept, blend_key, blend_gate, time_decay, time_first = params
    normed_mix = layer_norm(rows_in, gain_mix, bias_mix)
    before_mix = shifted(normed_mix)
    input_key = low(blend_rows(normed_mix, before_mix, mix_key))
    input_value = low(blend_rows(normed_mix, before_mix, mix_value))
    input_recept = low(blend_rows(normed_mix, before_mix, mix_recept))
    lookup_array = low_back(low(matmul(input_key, w_key)))
    payload_array = low_back(low(matmul(input_value, w_value)))
    recept = low_back(matmul(input_recept, w_recept))
    wkv_raw, finals = carry_update_rule(lookup_array, payload_array, occupied_lines, jnp.exp(time_decay), time_first, opening_upper_total, opening_normalizer)
    wkv_sent = low_back(low(wkv_raw))
    gated = low(jax.nn.sigmoid(recept) * wkv_sent)
    branch = low_back(matmul(gated, w_output))
    middle = rows_in + branch
    normed_ffn = layer_norm(middle, gain_ffn, bias_ffn)
    before_ffn = shifted(normed_ffn)
    input_expand = low(blend_rows(normed_ffn, before_ffn, blend_key))
    input_gate = low(blend_rows(normed_ffn, before_ffn, blend_gate))
    expanded = low_back(matmul(input_expand, w_expand))
    positive = jnp.maximum(expanded, 0.0)
    hidden = low(positive * positive)
    contracted = low_back(matmul(hidden, w_contract))
    gate_logit = low_back(matmul(input_gate, w_gate))
    layer_answer = occupied_lines[..., None] * (middle + jax.nn.sigmoid(gate_logit) * contracted)
    return (layer_answer, finals)

def reference(tokens, grad_out, lengths, init_num, init_den, w_key, w_value, w_recept, w_output, w_expand, w_contract, w_gate, gain_mix, bias_mix, gain_ffn, bias_ffn, mix_key, mix_value, mix_recept, blend_key, blend_gate, time_decay, time_first):
    params = tuple((item.astype(jnp.float32) for item in (w_key, w_value, w_recept, w_output, w_expand, w_contract, w_gate, gain_mix, bias_mix, gain_ffn, bias_ffn, mix_key, mix_value, mix_recept, blend_key, blend_gate, time_decay, time_first)))
    group_count = SLOTS // SEQS_GRP

    def regroup(array_in):
        return array_in.reshape((group_count, SEQS_GRP) + array_in.shape[1:])
    positions = jnp.arange(SLOT)

    def per_group(totals, inputs_now):
        rows_now, cot_now, lens_now, num_now, den_now = inputs_now
        occupied_lines = (positions[None, :] < lens_now[:, None]).astype(jnp.float32)

        def forward(rows_in, params_in):
            return block_forward(rows_in, params_in, occupied_lines, num_now, den_now)
        layer_answer, pull_back, finals = jax.vjp(forward, rows_now.astype(jnp.float32), params, has_aux=True)
        grad_rows, grad_params = pull_back(cot_now.astype(jnp.float32))
        totals = tuple((left + right for left, right in zip(totals, grad_params)))
        return (totals, (layer_answer.astype(jnp.bfloat16), grad_rows.astype(jnp.bfloat16), finals[0], finals[1]))
    zeros_init = tuple((jnp.zeros_like(item) for item in params))
    totals, (outputs, grad_rows, fin_num, fin_den) = lax.scan(per_group, zeros_init, (regroup(tokens), regroup(grad_out), regroup(lengths), regroup(init_num), regroup(init_den)))

    def flatten(array_in):
        return array_in.reshape((SLOTS,) + array_in.shape[2:])
    return (flatten(outputs), flatten(grad_rows), flatten(fin_num), flatten(fin_den), totals[0], totals[1], totals[2], totals[3], totals[4], totals[5], totals[6], totals[7], totals[8], totals[9], totals[10], totals[11], totals[12], totals[13], totals[14], totals[15], totals[16], totals[17])
```

```python
import functools
import math

import jax
import jax.numpy as jnp
from jax import lax
from jax.experimental import pallas as pl
from jax.experimental.pallas import tpu as pltpu
from jax.sharding import PartitionSpec as P

EPS = 1e-05
HIGH = lax.Precision.HIGHEST
WIDE_TYPE = jnp.float32
NARROW_TYPE = jnp.bfloat16


def from_behind(value, axis, steps):
    count = lax.axis_size(axis)
    initial, last = (max(0, -steps), min(count, count - steps))
    return lax.ppermute(value, axis, [(source, source + steps) for source in range(initial, last)])


def layer_norm(rows_in, gain, bias):
    center = rows_in - jnp.mean(rows_in, axis=-1, keepdims=True)
    factor = lax.rsqrt(jnp.mean(center * center, axis=-1, keepdims=True) + EPS)
    normed = center * factor
    return (normed * gain + bias, normed, factor)


def norm_back(grad_in, normed, factor, gain):
    scaled = grad_in * gain
    centered = scaled - jnp.mean(scaled, axis=-1, keepdims=True)
    return factor * (centered - normed * jnp.mean(scaled * normed, axis=-1, keepdims=True))


def blend_rows(current, earlier, weights):
    return current * weights + earlier * (1.0 - weights)


def project(rows_in, scaling_coefficient):
    flat_rows = rows_in.reshape(-1, rows_in.shape[-1])
    product = jnp.dot(flat_rows, scaling_coefficient, preferred_element_type=WIDE_TYPE)
    return product.reshape(rows_in.shape[:-1] + (scaling_coefficient.shape[1],))


def project_back(grad_in, scaling_coefficient):
    flat_rows = grad_in.reshape(-1, grad_in.shape[-1])
    product = lax.dot_general(
        flat_rows, scaling_coefficient, (((1,), (1,)), ((), ())), preferred_element_type=WIDE_TYPE
    )
    return product.reshape(grad_in.shape[:-1] + (scaling_coefficient.shape[0],))


def outer_sum(rows_in, grad_in):
    return lax.dot_general(
        rows_in.reshape(-1, rows_in.shape[-1]),
        grad_in.reshape(-1, grad_in.shape[-1]),
        (((0,), (0,)), ((), ())),
        preferred_element_type=WIDE_TYPE,
    )


def row_sum(values):
    return jnp.sum(values, axis=(0, 1))


def shift_in(rows_in, edge_rows):
    return jnp.concatenate([edge_rows, rows_in[:, :-1]], axis=1)


def shift_out(rows_in, edge_rows):
    return jnp.concatenate([rows_in[:, 1:], edge_rows], axis=1)


def weighted_value_prepare(
    incoming_key,
    incoming_value,
    incoming_count,
    preceding_count,
    occupied_lines,
    fading_pace,
    first_token_reward,
):
    slot_count, seq_span, chan_width = incoming_key.shape
    block_len = math.gcd(64, seq_span)
    block_count = seq_span // block_len
    shape_four = (slot_count, block_count, block_len, chan_width)
    exposure = (incoming_count[..., None] * fading_pace).reshape(shape_four)
    exposure_prev = (preceding_count[..., None] * fading_pace).reshape(shape_four)
    block_start = exposure_prev[:, :, 0]
    block_stop = exposure[:, :, block_len - 1]
    exponentiated_lookup = jnp.exp(incoming_key).reshape(shape_four)
    reward_share_term = jnp.exp(first_token_reward) * exponentiated_lookup
    scaling_coefficient = occupied_lines.reshape(shape_four[:3])[..., None] * exponentiated_lookup
    payload_quadruple = incoming_value.reshape(shape_four)
    paired = jnp.stack([scaling_coefficient * payload_quadruple, scaling_coefficient])
    growth = jnp.exp(exposure - block_start[:, :, None])
    shrink = jnp.exp(block_start[:, :, None] - exposure_prev)
    row_index = lax.broadcasted_iota(jnp.int32, (block_len, block_len), 0)
    col_index = lax.broadcasted_iota(jnp.int32, (block_len, block_len), 1)
    strict_lower = (col_index < row_index).astype(WIDE_TYPE)
    scaled = growth[None] * paired
    within = jnp.einsum("ab,pnjbc->pnjac", strict_lower, scaled, precision=HIGH)
    totals = jnp.exp(block_start - block_stop)[None] * jnp.sum(scaled, axis=3)
    bounds = jnp.concatenate([block_start, block_stop[:, block_count - 1 :]], axis=1)
    link_row = lax.broadcasted_iota(jnp.int32, (block_count + 1, block_count), 0)
    link_col = lax.broadcasted_iota(jnp.int32, (block_count + 1, block_count), 1)
    spread = bounds[:, :, None, :] - block_stop[:, None, :, :]
    link_mat = jnp.where(
        (link_col < link_row)[None, :, :, None], jnp.exp(-jnp.maximum(spread, 0.0)), 0.0
    )
    reached = jnp.einsum("njkc,pnkc->pnjc", link_mat, totals, precision=HIGH)
    return (
        exposure,
        exposure_prev,
        block_stop,
        bounds,
        reward_share_term,
        scaling_coefficient,
        payload_quadruple,
        shrink,
        within,
        link_mat,
        reached,
        strict_lower,
    )


def wkv_finish(ready_arguments, start_pair):
    bounds = ready_arguments[3]
    reward_share_term = ready_arguments[4]
    payload_quadruple = ready_arguments[6]
    shrink = ready_arguments[7]
    within = ready_arguments[8]
    reached = ready_arguments[10]
    block_count = shrink.shape[1]
    states = jnp.exp(-bounds)[None] * start_pair[:, :, None, :] + reached
    carried_memory = shrink[None] * (states[:, :, :block_count, None, :] + within)
    upper_accumulator = carried_memory[0] + reward_share_term * payload_quadruple
    normalizer_total = carried_memory[1] + reward_share_term
    layer_answer = upper_accumulator / normalizer_total
    flat_shape = (shrink.shape[0], shrink.shape[1] * shrink.shape[2], shrink.shape[3])
    return (
        layer_answer.reshape(flat_shape),
        states[:, :, block_count],
        (carried_memory, normalizer_total, layer_answer),
    )


def wkv_adjoint(grad_flat, ready_arguments, kept_state):
    bounds = ready_arguments[3]
    shrink = ready_arguments[7]
    carried_memory, normalizer_total, layer_answer = kept_state
    upper_total_cotangent = grad_flat.reshape(normalizer_total.shape) / normalizer_total
    adjoint = jnp.stack([upper_total_cotangent, -upper_total_cotangent * layer_answer])
    block_adj = jnp.sum(shrink[None] * adjoint, axis=3)
    block_count = shrink.shape[1]
    own_part = jnp.sum(jnp.exp(-bounds[:, :block_count])[None] * block_adj, axis=2)
    return (adjoint, block_adj, own_part)


def wkv_backward(
    ready_arguments, kept_state, adjoint, block_adj, tail_adj, fading_pace, occupied_lines
):
    (
        exposure,
        exposure_prev,
        block_stop,
        bounds,
        reward_share_term,
        scaling_coefficient,
        payload_quadruple,
        shrink,
        within,
        link_mat,
        reached,
        strict_lower,
    ) = ready_arguments
    carried_memory, normalizer_total, layer_answer = kept_state
    block_count = shrink.shape[1]
    damped = jnp.exp(exposure - block_stop[:, :, None])
    lifted = jnp.exp(block_stop[:, :, None] - exposure_prev)
    carry_in = jnp.einsum("nkjc,pnkc->pnjc", link_mat[:, :block_count], block_adj, precision=HIGH)
    carry_in = carry_in + link_mat[:, block_count][None] * tail_adj[:, :, None, :]
    inside = jnp.einsum("ab,pnjac->pnjbc", strict_lower, lifted[None] * adjoint, precision=HIGH)
    later_cotangent_carry = damped[None] * (inside + carry_in[:, :, :, None, :])
    upper_total_cotangent = adjoint[0]
    lower_sum_cotangent = adjoint[1]
    payload_cotangent = (
        upper_total_cotangent * reward_share_term + later_cotangent_carry[0] * scaling_coefficient
    )
    immediate_route = (
        upper_total_cotangent * payload_quadruple + lower_sum_cotangent
    ) * reward_share_term
    grad_key = (
        immediate_route
        + (later_cotangent_carry[0] * payload_quadruple + later_cotangent_carry[1])
        * scaling_coefficient
    )
    filled_four = occupied_lines.reshape(normalizer_total.shape[:3])[..., None]
    grad_rate = (
        -fading_pace
        * jnp.exp(-fading_pace)
        * jnp.sum(
            filled_four
            * (
                later_cotangent_carry[0] * carried_memory[0]
                + later_cotangent_carry[1] * carried_memory[1]
            ),
            axis=(0, 1, 2),
        )
    )
    grad_first = jnp.sum(immediate_route, axis=(0, 1, 2))
    flat_shape = (
        normalizer_total.shape[0],
        normalizer_total.shape[1] * normalizer_total.shape[2],
        normalizer_total.shape[3],
    )
    return (
        grad_key.reshape(flat_shape),
        payload_cotangent.reshape(flat_shape),
        grad_first,
        grad_rate,
    )


MESH = pl.DeviceIdType.MESH
AXES = "kzyx"


def axis_sizes():
    seq_size, ch_size = lax.axis_size("seq"), lax.axis_size("ch")
    return {"k": 2, "x": ch_size // 2, "y": 2, "z": seq_size // 2}


def coordinates():
    seq_at, ch_at = lax.axis_index("seq"), lax.axis_index("ch")
    return {"z": seq_at // 2, "y": seq_at % 2, "x": ch_at // 2, "k": ch_at % 2}


def device_at(place):
    return (place["z"] * 2 + place["y"], place["x"] * 2 + place["k"])


def moved(place, sizes, axis, step):
    return {**place, axis: lax.rem(place[axis] + step, sizes[axis])}


def greet(sizes, place):
    barrier = pltpu.get_barrier_semaphore()
    total = 0
    for axis in AXES:
        for step in range(1, sizes[axis]):
            there = moved(place, sizes, axis, step)
            pl.semaphore_signal(barrier, inc=1, device_id=device_at(there), device_id_type=MESH)
            total += 1
    pl.semaphore_wait(barrier, total)


class Piece:
    def __init__(self, current, order, sizes, place, landings, sends, receives):
        self.current, self.order, self.sizes, self.place = current, order, sizes, place
        self.landings, self.sends, self.receives = landings, sends, receives
        self.axes = [axis for axis in AXES if axis in order]
        self.stage = 0

    def start(self):
        axis = self.order[self.stage]
        at = self.axes.index(axis)
        self.copies = []
        for step in range(1, self.sizes[axis]):
            there = moved(self.place, self.sizes, axis, step)
            where = (slice(None),) * at + (there[axis],)
            copy = pltpu.make_async_remote_copy(
                src_ref=self.current.at[where],
                dst_ref=self.landings[self.stage].at[step - 1],
                send_sem=self.sends[self.stage][step - 1],
                recv_sem=self.receives[self.stage][step - 1],
                device_id=device_at(there),
                device_id_type=MESH,
            )
            copy.start()
            self.copies.append(copy)

    def finish(self, out_ref=None, own_ref=None):
        axis = self.order[self.stage]
        at = self.axes.index(axis)
        landing = self.landings[self.stage]
        others = self.sizes[axis] - 1
        if own_ref is None:
            own_ref = self.current.at[(slice(None),) * at + (self.place[axis],)]
        for copy in self.copies:
            copy.wait()
        remaining = [a for a in self.axes if a != axis]
        lead = tuple(self.sizes[a] for a in remaining)
        rows, columns = landing.shape[-2:]
        tile = math.gcd(rows, max(16, 32768 // columns))
        blocks = math.prod(lead)

        def add(index, carry):
            part = index % (rows // tile)
            rest = index // (rows // tile)
            where = ()
            for size in reversed(lead):
                where = (rest % size,) + where
                rest = rest // size
            where = where + (pl.ds(pl.multiple_of(part * tile, tile), tile), slice(None))
            total = own_ref[where].astype(jnp.float32)
            for other in range(others):
                total = total + landing[(other,) + where].astype(jnp.float32)
            if out_ref is None:
                landing[(0,) + where] = total.astype(jnp.bfloat16)
            else:
                out_ref[where] = total
            return carry

        lax.fori_loop(0, blocks * (rows // tile), add, 0)
        self.axes = remaining
        self.current = landing.at[0]
        self.stage += 1


def landing_shapes(order, sizes, rows, columns):
    axes = [axis for axis in AXES if axis in order]
    shapes = []
    for axis in order:
        axes = [a for a in axes if a != axis]
        shapes.append((sizes[axis] - 1,) + tuple(sizes[a] for a in axes) + (rows, columns))
    return shapes


def scatter_kernel(plan, sizes, *refs):
    count = len(plan)
    inputs, outs = refs[:count], refs[count : 2 * count]
    scratch = list(refs[2 * count :])
    place = coordinates()
    send_sems, recv_sems, own_sems = scratch[-3:]
    used = 0
    pieces, owns, loads = [], [], []
    for index, order in enumerate(plan):
        own = scratch.pop(0)
        landings = [scratch.pop(0) for _ in order]
        sends, receives = [], []
        for axis in order:
            sends.append([send_sems.at[used + s] for s in range(sizes[axis] - 1)])
            receives.append([recv_sems.at[used + s] for s in range(sizes[axis] - 1)])
            used += sizes[axis] - 1
        piece = Piece(inputs[index], order, sizes, place, landings, sends, receives)
        at = piece.axes.index(order[0])
        load = pltpu.make_async_copy(
            inputs[index].at[(slice(None),) * at + (place[order[0]],)], own, own_sems.at[index]
        )
        load.start()
        pieces.append(piece)
        owns.append(own)
        loads.append(load)
    greet(sizes, place)
    stages = len(plan[0])
    ahead = 2
    for index in range(min(ahead, count)):
        pieces[index].start()
    for turn in range(count + stages - 1):
        for stage in reversed(range(stages)):
            index = turn - stage
            if not 0 <= index < count:
                continue
            piece = pieces[index]
            if stage == 0:
                loads[index].wait()
                piece.finish(own_ref=owns[index])
                if index + ahead < count:
                    pieces[index + ahead].start()
            elif stage < stages - 1:
                piece.finish()
            else:
                piece.finish(out_ref=outs[index])
            if stage < stages - 1:
                piece.start()


def scatter_sum(terms, orders):
    sizes = axis_sizes()
    scratch, outs, total = [], [], 0
    for term, order in zip(terms, orders):
        rows, columns = term.shape[-2:]
        at = [axis for axis in AXES if axis in order].index(order[0])
        scratch.append(pltpu.VMEM(term.shape[:at] + term.shape[at + 1 :], jnp.bfloat16))
        for shape in landing_shapes(order, sizes, rows, columns):
            scratch.append(pltpu.VMEM(shape, jnp.bfloat16))
        outs.append(jax.ShapeDtypeStruct((rows, columns), jnp.float32))
        total += sum(sizes[axis] - 1 for axis in order)
    scratch += [
        pltpu.SemaphoreType.DMA((total,)),
        pltpu.SemaphoreType.DMA((total,)),
        pltpu.SemaphoreType.DMA((len(terms),)),
    ]
    return pl.pallas_call(
        functools.partial(scatter_kernel, orders, sizes),
        out_shape=outs,
        in_specs=[pl.BlockSpec(memory_space=pl.ANY)] * len(terms),
        out_specs=[pl.BlockSpec(memory_space=pltpu.VMEM)] * len(terms),
        scratch_shapes=scratch,
        compiler_params=pltpu.CompilerParams(
            collective_id=0, has_side_effects=True, vmem_limit_bytes=60 * 2**20
        ),
    )(*terms)


def by_owner(grad, sizes):
    rows = grad.shape[0] // (sizes["z"] * sizes["y"])
    columns = grad.shape[1] // (sizes["x"] * sizes["k"])
    split = grad.astype(jnp.bfloat16).reshape(
        sizes["z"], sizes["y"], rows, sizes["x"], sizes["k"], columns
    )
    return split.transpose(4, 0, 1, 3, 2, 5)


def vectors_by_owner(vectors, sizes):
    part = vectors[0].shape[0] // (sizes["z"] * sizes["y"] * sizes["x"] * sizes["k"])
    stacked = jnp.stack(vectors).reshape(
        len(vectors), sizes["z"], sizes["y"], sizes["x"], sizes["k"], part
    )
    flat = stacked.transpose(4, 1, 2, 3, 0, 5).reshape(
        sizes["k"], sizes["z"], sizes["y"], sizes["x"], len(vectors) * part
    )
    rows = 16 * -(-flat.shape[-1] // 2048)
    flat = jnp.pad(flat, ((0, 0),) * 4 + ((0, rows * 128 - flat.shape[-1]),))
    return flat.astype(jnp.bfloat16).reshape(flat.shape[:4] + (rows, 128))


def body(
    tokens,
    grad_out,
    lengths,
    init_num,
    init_den,
    w_key,
    w_value,
    w_recept,
    w_output,
    w_expand,
    w_contract,
    w_gate,
    gain_mix,
    bias_mix,
    gain_ffn,
    bias_ffn,
    mix_key,
    mix_value,
    mix_recept,
    blend_key,
    blend_gate,
    time_decay,
    time_first,
):
    slot_count, local_len, model_width = tokens.shape
    group_size = lax.axis_size("ch")
    ch_rank = lax.axis_index("ch")
    chan_width = model_width // group_size
    seq_span = local_len * group_size
    length_col = lengths[:, None]
    offset = ch_rank * local_len
    position = offset + lax.broadcasted_iota(jnp.int32, (slot_count, local_len), 1)
    occupied_lines = (position < length_col).astype(WIDE_TYPE)
    fading_pace = jnp.exp(time_decay)
    start_pair = jnp.stack([init_num, init_den])
    rows_in = tokens.astype(WIDE_TYPE)
    normed_mix, unit_mix, factor_mix = layer_norm(rows_in, gain_mix, bias_mix)
    edge_mix = from_behind(normed_mix[:, local_len - 1 :], "ch", 1)
    before_mix = shift_in(normed_mix, edge_mix)
    input_key = blend_rows(normed_mix, before_mix, mix_key).astype(NARROW_TYPE)
    input_value = blend_rows(normed_mix, before_mix, mix_value).astype(NARROW_TYPE)
    input_recept = blend_rows(normed_mix, before_mix, mix_recept).astype(NARROW_TYPE)
    lookup_array = project(input_key, w_key).astype(NARROW_TYPE)
    payload_array = project(input_value, w_value).astype(NARROW_TYPE)
    recept = project(input_recept, w_recept)
    key_cols, value_cols = (
        lax.all_to_all(lookup_array, "ch", split_axis=2, concat_axis=1, tiled=True),
        lax.all_to_all(payload_array, "ch", split_axis=2, concat_axis=1, tiled=True),
    )
    step_index = lax.broadcasted_iota(jnp.int32, (slot_count, seq_span), 1)
    incoming_count = jnp.minimum(step_index + 1, length_col).astype(WIDE_TYPE)
    preceding_count = jnp.minimum(step_index, length_col).astype(WIDE_TYPE)
    filled_cols = (step_index < length_col).astype(WIDE_TYPE)
    rate_part = lax.dynamic_slice_in_dim(fading_pace, ch_rank * chan_width, chan_width)
    first_part = lax.dynamic_slice_in_dim(time_first, ch_rank * chan_width, chan_width)
    init_part = lax.dynamic_slice_in_dim(start_pair, ch_rank * chan_width, chan_width, 2)
    ready_arguments = weighted_value_prepare(
        key_cols.astype(WIDE_TYPE),
        value_cols.astype(WIDE_TYPE),
        incoming_count,
        preceding_count,
        filled_cols,
        rate_part,
        first_part,
    )
    wkv_cols, final_pair, kept_state = wkv_finish(ready_arguments, init_part)
    wkv_rows = lax.all_to_all(
        wkv_cols.astype(NARROW_TYPE), "ch", split_axis=1, concat_axis=2, tiled=True
    )
    gate_mix = jax.nn.sigmoid(recept)
    wkv_float = wkv_rows.astype(WIDE_TYPE)
    gated = (gate_mix * wkv_float).astype(NARROW_TYPE)
    middle = rows_in + project(gated, w_output)
    normed_ffn, unit_ffn, factor_ffn = layer_norm(middle, gain_ffn, bias_ffn)
    edge_ffn = from_behind(normed_ffn[:, local_len - 1 :], "ch", 1)
    before_ffn = shift_in(normed_ffn, edge_ffn)
    input_expand = blend_rows(normed_ffn, before_ffn, blend_key).astype(NARROW_TYPE)
    input_gate = blend_rows(normed_ffn, before_ffn, blend_gate).astype(NARROW_TYPE)
    expanded = project(input_expand, w_expand)
    positive = jnp.maximum(expanded, 0.0)
    hidden = (positive * positive).astype(NARROW_TYPE)
    contracted = project(hidden, w_contract)
    gate_ffn = jax.nn.sigmoid(project(input_gate, w_gate))
    mask_three = occupied_lines[..., None]
    mixed_out = (mask_three * (middle + gate_ffn * contracted)).astype(NARROW_TYPE)
    grad_res = mask_three * grad_out.astype(WIDE_TYPE)
    grad_contracted = (grad_res * gate_ffn).astype(NARROW_TYPE)
    grad_logit = (grad_res * contracted * gate_ffn * (1.0 - gate_ffn)).astype(NARROW_TYPE)
    grad_expanded = (project_back(grad_contracted, w_contract) * 2.0 * positive).astype(NARROW_TYPE)
    grad_w_contract = outer_sum(hidden, grad_contracted)
    grad_w_expand = outer_sum(input_expand, grad_expanded)
    grad_w_gate = outer_sum(input_gate, grad_logit)
    grad_in_expand = project_back(grad_expanded, w_expand)
    grad_in_gate = project_back(grad_logit, w_gate)
    gap_ffn = normed_ffn - before_ffn
    grad_blend_key = row_sum(grad_in_expand * gap_ffn)
    grad_blend_gate = row_sum(grad_in_gate * gap_ffn)
    grad_before_ffn = grad_in_expand * (1.0 - blend_key) + grad_in_gate * (1.0 - blend_gate)
    from_next_ffn = from_behind(grad_before_ffn[:, :1], "ch", -1)
    grad_normed_ffn = (
        grad_in_expand * blend_key
        + grad_in_gate * blend_gate
        + shift_out(grad_before_ffn, from_next_ffn)
    )
    grad_gain_ffn = row_sum(grad_normed_ffn * unit_ffn)
    grad_bias_ffn = row_sum(grad_normed_ffn)
    grad_middle = grad_res + norm_back(grad_normed_ffn, unit_ffn, factor_ffn, gain_ffn)
    grad_branch = grad_middle.astype(NARROW_TYPE)
    grad_w_output = outer_sum(gated, grad_branch)
    grad_gated = project_back(grad_branch, w_output)
    grad_wkv = (grad_gated * gate_mix).astype(NARROW_TYPE)
    grad_recept = (grad_gated * wkv_float * gate_mix * (1.0 - gate_mix)).astype(NARROW_TYPE)
    grad_cols = lax.all_to_all(grad_wkv, "ch", split_axis=2, concat_axis=1, tiled=True)
    adjoint, block_adj, own_part = wkv_adjoint(
        grad_cols.astype(WIDE_TYPE), ready_arguments, kept_state
    )
    grad_key_cols, grad_value_cols, first_grad_part, rate_grad_part = wkv_backward(
        ready_arguments,
        kept_state,
        adjoint,
        block_adj,
        jnp.zeros_like(own_part),
        rate_part,
        filled_cols,
    )
    grad_key_rows, grad_value_rows = (
        lax.all_to_all(
            grad_key_cols.astype(NARROW_TYPE), "ch", split_axis=1, concat_axis=2, tiled=True
        ),
        lax.all_to_all(
            grad_value_cols.astype(NARROW_TYPE), "ch", split_axis=1, concat_axis=2, tiled=True
        ),
    )
    grad_time_decay = lax.dynamic_update_slice_in_dim(
        jnp.zeros((model_width,), WIDE_TYPE), rate_grad_part, ch_rank * chan_width, 0
    )
    grad_time_first = lax.dynamic_update_slice_in_dim(
        jnp.zeros((model_width,), WIDE_TYPE), first_grad_part, ch_rank * chan_width, 0
    )
    grad_w_key = outer_sum(input_key, grad_key_rows)
    grad_w_value = outer_sum(input_value, grad_value_rows)
    grad_w_recept = outer_sum(input_recept, grad_recept)
    grad_in_key = project_back(grad_key_rows, w_key)
    grad_in_value = project_back(grad_value_rows, w_value)
    grad_in_recept = project_back(grad_recept, w_recept)
    gap_mix = normed_mix - before_mix
    grad_mix_key = row_sum(grad_in_key * gap_mix)
    grad_mix_value = row_sum(grad_in_value * gap_mix)
    grad_mix_recept = row_sum(grad_in_recept * gap_mix)
    grad_before_mix = (
        grad_in_key * (1.0 - mix_key)
        + grad_in_value * (1.0 - mix_value)
        + grad_in_recept * (1.0 - mix_recept)
    )
    from_next_mix = from_behind(grad_before_mix[:, :1], "ch", -1)
    grad_normed_mix = (
        grad_in_key * mix_key
        + grad_in_value * mix_value
        + grad_in_recept * mix_recept
        + shift_out(grad_before_mix, from_next_mix)
    )
    grad_gain_mix = row_sum(grad_normed_mix * unit_mix)
    grad_bias_mix = row_sum(grad_normed_mix)
    grad_tokens = (grad_middle + norm_back(grad_normed_mix, unit_mix, factor_mix, gain_mix)).astype(
        NARROW_TYPE
    )
    sizes = axis_sizes()
    vectors = (
        grad_gain_mix,
        grad_bias_mix,
        grad_gain_ffn,
        grad_bias_ffn,
        grad_mix_key,
        grad_mix_value,
        grad_mix_recept,
        grad_blend_key,
        grad_blend_gate,
        grad_time_decay,
        grad_time_first,
    )
    contract_terms = by_owner(grad_w_contract, sizes)
    expand_terms = by_owner(grad_w_expand, sizes)
    half_rows = contract_terms.shape[-2] // 2
    half_columns = expand_terms.shape[-1] // 2
    terms = [
        contract_terms[..., :half_rows, :],
        expand_terms[..., :half_columns],
        contract_terms[..., half_rows:, :],
        expand_terms[..., half_columns:],
        by_owner(grad_w_gate, sizes),
        by_owner(grad_w_output, sizes),
        by_owner(grad_w_key, sizes),
        by_owner(grad_w_value, sizes),
        by_owner(grad_w_recept, sizes),
        vectors_by_owner(vectors, sizes),
    ]
    orders = ["kxyz", "kyxz", "kxyz", "kyxz", "kxyz", "kyxz", "kxyz", "kyxz", "kxyz", "kyxz"]
    sums = scatter_sum(terms, orders)
    part = model_width // (lax.axis_size("seq") * group_size)
    vector_sums = sums[9].reshape(-1)[: len(vectors) * part].reshape(len(vectors), part)
    all_sums = (
        sums[6],
        sums[7],
        sums[8],
        sums[5],
        jnp.concatenate([sums[1], sums[3]], axis=1),
        jnp.concatenate([sums[0], sums[2]], axis=0),
        sums[4],
    ) + tuple(vector_sums[i] for i in range(len(vectors)))
    return (
        mixed_out,
        grad_tokens,
        final_pair[0],
        final_pair[1],
        all_sums[0],
        all_sums[1],
        all_sums[2],
        all_sums[3],
        all_sums[4],
        all_sums[5],
        all_sums[6],
        all_sums[7],
        all_sums[8],
        all_sums[9],
        all_sums[10],
        all_sums[11],
        all_sums[12],
        all_sums[13],
        all_sums[14],
        all_sums[15],
        all_sums[16],
        all_sums[17],
    )


def solution(mesh):
    placed = (
        P("seq", "ch", None),
        P("seq", "ch", None),
        P("seq"),
        P("seq", None),
        P("seq", None),
        P(),
        P(),
        P(),
        P(),
        P(),
        P(),
        P(),
        P(),
        P(),
        P(),
        P(),
        P(),
        P(),
        P(),
        P(),
        P(),
        P(),
        P(),
    )
    return jax.shard_map(
        body,
        mesh=mesh,
        in_specs=placed,
        out_specs=(
            P("seq", "ch", None),
            P("seq", "ch", None),
            P("seq", "ch"),
            P("seq", "ch"),
            P("seq", "ch"),
            P("seq", "ch"),
            P("seq", "ch"),
            P("seq", "ch"),
            P("seq", "ch"),
            P("seq", "ch"),
            P("seq", "ch"),
            P(("seq", "ch")),
            P(("seq", "ch")),
            P(("seq", "ch")),
            P(("seq", "ch")),
            P(("seq", "ch")),
            P(("seq", "ch")),
            P(("seq", "ch")),
            P(("seq", "ch")),
            P(("seq", "ch")),
            P(("seq", "ch")),
            P(("seq", "ch")),
        ),
        check_vma=False,
    )
```

```python
import functools
import math

import jax
import jax.numpy as jnp
from jax import lax
from jax.experimental import pallas as pl
from jax.experimental.pallas import tpu as pltpu
from jax.sharding import PartitionSpec as P

EPS = 1e-05
MESH = pl.DeviceIdType.MESH
AXES = "zyx"
F32 = jnp.float32
BF16 = jnp.bfloat16
TILE = 16
WIDE = 256
SLOTS_OF_WEIGHTS = 3

NN = (((1,), (0,)), ((), ()))
NT = (((1,), (1,)), ((), ()))
TN = (((0,), (0,)), ((), ()))


def dot(left, right, how):
    return lax.dot_general(left, right, how, preferred_element_type=F32)


def axis_sizes():
    seq_size, ch_size = lax.axis_size("seq"), lax.axis_size("ch")
    return {"k": 2, "x": ch_size // 2, "y": 2, "z": seq_size // 2}


def coordinates():
    seq_at, ch_at = lax.axis_index("seq"), lax.axis_index("ch")
    return {"z": seq_at // 2, "y": seq_at % 2, "x": ch_at // 2, "k": ch_at % 2}


def device_at(place):
    return (place["z"] * 2 + place["y"], place["x"] * 2 + place["k"])


def moved(place, sizes, axis, step):
    return {**place, axis: lax.rem(place[axis] + step, sizes[axis])}


class Copies:
    def __init__(self, sends, receives):
        self.sends, self.receives, self.used = sends, receives, 0
        self.open = []

    def start(self, source, target, device):
        copy = pltpu.make_async_remote_copy(
            src_ref=source,
            dst_ref=target,
            send_sem=self.sends.at[self.used],
            recv_sem=self.receives.at[self.used],
            device_id=device,
            device_id_type=MESH,
        )
        self.used += 1
        copy.start()
        return copy


class Piece:
    def __init__(self, make, order, sizes, place, copies, held, landings, out_ref):
        self.make, self.order, self.sizes, self.place = make, order, sizes, place
        self.remote, self.held, self.landings, self.out_ref = copies, held, landings, out_ref
        self.axes = list(AXES)
        self.stage = 0
        self.copies = []

    def start(self):
        axis = self.order[self.stage]
        at = self.axes.index(axis)
        for step in range(1, self.sizes[axis]):
            there = moved(self.place, self.sizes, axis, step)
            if self.stage == 0:

                def keep(where, value, slot=step - 1):
                    self.held[(slot,) + where] = value.astype(BF16)

                self.make(there[axis], keep)
                source = self.held.at[step - 1]
            else:
                source = self.landings[self.stage - 1].at[
                    (0,) + (slice(None),) * at + (there[axis],)
                ]
            self.copies.append(
                self.remote.start(
                    source, self.landings[self.stage].at[step - 1], device_at(there)
                )
            )

    def finish(self):
        axis = self.order[self.stage]
        at = self.axes.index(axis)
        landing = self.landings[self.stage]
        others = self.sizes[axis] - 1
        for copy in self.copies:
            copy.wait()
        self.copies = []
        remaining = [a for a in self.axes if a != axis]
        if self.stage == 0:

            def add(where, value):
                for other in range(others):
                    value = value + landing[(other,) + where].astype(F32)
                landing[(0,) + where] = value.astype(BF16)

            self.make(self.place[axis], add)
        else:
            own = self.landings[self.stage - 1].at[
                (0,) + (slice(None),) * at + (self.place[axis],)
            ]
            lead = tuple(self.sizes[a] for a in remaining)
            rows, columns = landing.shape[-2:]
            tile = math.gcd(rows, max(16, 32768 // columns))
            parts = rows // tile

            def add_tile(index, carry):
                part, rest = index % parts, index // parts
                where = ()
                for size in reversed(lead):
                    where = (rest % size,) + where
                    rest = rest // size
                spot = pl.ds(pl.multiple_of(part * tile, tile), tile)
                where = where + (spot, slice(None))
                total = own[where].astype(F32)
                for other in range(others):
                    total = total + landing[(other,) + where].astype(F32)
                if remaining:
                    landing[(0,) + where] = total.astype(BF16)
                else:
                    self.out_ref[where] = total
                return carry

            lax.fori_loop(0, math.prod(lead) * parts, add_tile, 0)
        self.axes = remaining
        self.stage += 1

    def advance(self):
        self.finish()
        if self.axes:
            self.start()


class Plan:
    def __init__(self, tokens, w_expand):
        self.slots, self.length, self.width = tokens.shape
        self.hidden = w_expand.shape[1]
        self.sizes = sizes = axis_sizes()
        self.seq, self.ch = sizes["z"] * 2, sizes["x"] * 2
        self.rows = self.slots * self.length
        rows, width, hidden = self.rows, self.width, self.hidden
        self.narrow = width // self.ch
        self.broad = hidden // self.ch
        self.short = width // self.seq
        self.tall = hidden // self.seq
        half = sizes["x"] * self.narrow
        self.pieces = []
        cuts = 2 if (self.tall // 2) % 128 == 0 else 1
        self.contract_cuts = cuts
        for _ in range(cuts):
            self.pieces.append(("contract", "yxz", self.tall // cuts, self.narrow))
        cuts = 2 if (self.broad // 2) % 128 == 0 else 1
        self.expand_cuts = cuts
        for _ in range(cuts):
            self.pieces.append(("expand", "xyz", self.short, self.broad // cuts))
        first_z = "zxy" if (2 * self.short) % 128 == 0 else "xyz"
        for name, order in (
            ("gate", first_z),
            ("output", "xyz"),
            ("key", first_z),
            ("value", "xyz"),
            ("recept", "xyz"),
        ):
            self.pieces.append((name, order, self.short, self.narrow))
        vmem = pltpu.VMEM
        shapes = {
            "panels": vmem((SLOTS_OF_WEIGHTS, width, width), BF16),
            "both_hidden": vmem((2 * rows, hidden), BF16),
            "grad_expanded": vmem((rows, hidden), BF16),
            "their_expanded": vmem((rows, hidden // 2), BF16),
            "key": vmem((rows, width), BF16),
            "value": vmem((rows, width), BF16),
            "edges_out": vmem((4, 8, width), F32),
            "edges_in": vmem((4, 8, width), F32),
            "sums_out": vmem((2, 8, width), F32),
            "sums_in": vmem((2, self.ch - 1, 8, width), F32),
            "states": vmem((8, width), F32),
            "finals": vmem((8, width), F32),
            "later": vmem((8, width), F32),
            "factor_ffn": vmem((rows, 128), F32),
            "vector_in": vmem((self.count_vector_slots(), 16, width), F32),
        }
        for name in ("expand", "gate", "output", "key", "value", "recept"):
            shapes["both_" + name] = vmem((2 * rows, width), BF16)
        for name in ("contract", "gate", "output", "key", "value", "recept"):
            shapes["back_" + name] = vmem((2 * rows, half), BF16)
        for index in range(4):
            shapes["rows_" + str(index)] = vmem((rows, width), BF16)
        for name in ("middle", "total", "sigmoid", "num", "den", "unit", "gap"):
            shapes["wide_" + name] = vmem((rows, width), F32)
        copies = 64 + 4 * self.ch
        for index, (name, order, height, breadth) in enumerate(self.pieces):
            axes = [axis for axis in AXES if axis != order[0]]
            lead = tuple(sizes[a] for a in axes)
            shapes["held_" + str(index)] = vmem(
                (sizes[order[0]] - 1,) + lead + (height, breadth), BF16
            )
            axes = list(AXES)
            for stage, axis in enumerate(order):
                axes.remove(axis)
                shape = (sizes[axis] - 1,) + tuple(sizes[a] for a in axes) + (height, breadth)
                shapes["landing_" + str(index) + "_" + str(stage)] = vmem(shape, BF16)
                copies += sizes[axis] - 1
        copies += self.count_vector_slots()
        shapes["sends"] = pltpu.SemaphoreType.DMA((copies,))
        shapes["receives"] = pltpu.SemaphoreType.DMA((copies,))
        shapes["panel_sems"] = pltpu.SemaphoreType.DMA((SLOTS_OF_WEIGHTS,))
        self.shapes = shapes

    def count_vector_slots(self):
        return sum(size - 1 for size in self.sizes.values())


INPUTS = (
    "tokens",
    "grad_out",
    "lengths",
    "init_num",
    "init_den",
    "w_key",
    "w_value",
    "w_recept",
    "w_output",
    "w_expand",
    "w_contract",
    "w_gate",
    "gain_mix",
    "bias_mix",
    "gain_ffn",
    "bias_ffn",
    "mix_key",
    "mix_value",
    "mix_recept",
    "blend_key",
    "blend_gate",
    "time_decay",
    "time_first",
)
OUTPUTS = (
    "mixed_out",
    "grad_tokens",
    "final",
    "grad_key",
    "grad_value",
    "grad_recept",
    "grad_output",
    "grad_expand",
    "grad_contract",
    "grad_gate",
    "vectors",
)
VECTORS = (
    "gain_mix",
    "bias_mix",
    "gain_ffn",
    "bias_ffn",
    "mix_key",
    "mix_value",
    "mix_recept",
    "blend_key",
    "blend_gate",
    "time_decay",
    "time_first",
)


class Panels:
    def __init__(self, sources, ref, sems):
        self.sources, self.ref, self.sems = sources, ref, sems
        self.used = 0
        for index in range(min(SLOTS_OF_WEIGHTS, len(sources))):
            self.copy(index).start()

    def copy(self, index):
        slot = index % SLOTS_OF_WEIGHTS
        return pltpu.make_async_copy(self.sources[index], self.ref.at[slot], self.sems.at[slot])

    def take(self):
        self.copy(self.used).wait()
        return self.ref.at[self.used % SLOTS_OF_WEIGHTS]

    def release(self):
        index = self.used + SLOTS_OF_WEIGHTS
        if index < len(self.sources):
            self.copy(index).start()
        self.used += 1


def layer_kernel(plan, *all_refs):
    inputs = dict(zip(INPUTS, all_refs))
    outputs = dict(zip(OUTPUTS, all_refs[len(INPUTS) :]))
    held = dict(zip(plan.shapes, all_refs[len(INPUTS) + len(OUTPUTS) :]))
    sizes = plan.sizes
    place = coordinates()
    ch_at = lax.axis_index("ch")
    seq_at = lax.axis_index("seq")
    slots, length, width, rows = plan.slots, plan.length, plan.width, plan.rows
    hidden, ch_size = plan.hidden, plan.ch
    panel_count = hidden // width
    tokens, grad_out, lengths = inputs["tokens"], inputs["grad_out"], inputs["lengths"]
    first_rows = slice(0, rows)
    last_rows = slice(rows, 2 * rows)

    w_expand, w_contract = inputs["w_expand"], inputs["w_contract"]

    def expand_panel(index):
        return w_expand.at[:, pl.ds(index * width, width)]

    def contract_panel(index):
        return w_contract.at[pl.ds(index * width, width), :]

    order = [inputs["w_key"], inputs["w_value"], inputs["w_recept"], inputs["w_output"]]
    for index in range(panel_count):
        order += [expand_panel(index), contract_panel(index)]
    order += [inputs["w_gate"]]
    order += [contract_panel(index) for index in range(panel_count)]
    order += [expand_panel(index) for index in range(panel_count)]
    order += [inputs["w_gate"], inputs["w_output"]]
    order += [inputs["w_key"], inputs["w_value"], inputs["w_recept"]]
    panels = Panels(order, held["panels"], held["panel_sems"])

    barrier = pltpu.get_barrier_semaphore()
    greeted = 0
    for step in range(1, ch_size):
        pl.semaphore_signal(
            barrier,
            inc=1,
            device_id=(seq_at, lax.rem(ch_at + step, ch_size)),
            device_id_type=MESH,
        )
        greeted += 1
    for axis in "yz":
        for step in range(1, sizes[axis]):
            there = device_at(moved(place, sizes, axis, step))
            pl.semaphore_signal(barrier, inc=1, device_id=there, device_id_type=MESH)
            greeted += 1
    copies = Copies(held["sends"], held["receives"])
    partner = device_at({**place, "k": 1 - place["k"]})
    after = (seq_at, lax.rem(ch_at + 1, ch_size))
    before = (seq_at, lax.rem(ch_at + ch_size - 1, ch_size))

    filled_here = [
        jnp.clip(lengths[slot] - ch_at * length, 0, length) for slot in range(slots)
    ]
    vectors = outputs["vectors"]
    vectors[...] = jnp.zeros_like(vectors)

    def add_vector(name, value):
        at = VECTORS.index(name)
        vectors[at : at + 1, :] += jnp.sum(value, axis=0, keepdims=True)

    def normalize(value):
        center = value - jnp.mean(value, axis=-1, keepdims=True)
        factor = lax.rsqrt(jnp.mean(center * center, axis=-1, keepdims=True) + EPS)
        return center * factor, factor

    def blend(current, earlier, weights):
        return current * weights + earlier * (1.0 - weights)

    def tiles_of(slot, index):
        return pl.ds(pl.multiple_of(slot * length + index * TILE, TILE), TILE)

    row_in_tile = lax.broadcasted_iota(jnp.int32, (TILE, width), 0)

    def shift_down(value, carry):
        return jnp.where(row_in_tile == 0, carry, pltpu.roll(value, 1, 0))

    def shift_up(value, carry):
        return jnp.where(row_in_tile == TILE - 1, carry, pltpu.roll(value, TILE - 1, 0))

    steps_in_slot = length // TILE

    def matmul(left, panel, how, use, left_columns=None):
        def step(index, carry):
            columns = pl.ds(pl.multiple_of(index * WIDE, WIDE), WIDE)
            right = panel[:, columns] if how is NN else panel[columns, :]
            source = left[...] if left_columns is None else left[:, left_columns]
            use(columns, dot(source, right, how))
            return carry

        lax.fori_loop(0, width // WIDE, step, 0)

    def counts(slot, shape, offset):
        at = lax.broadcasted_iota(jnp.int32, shape, 0) + offset
        earlier = jnp.minimum(at, filled_here[slot]).astype(F32)
        upto = jnp.minimum(at + 1, filled_here[slot]).astype(F32)
        return earlier, upto, at < filled_here[slot]

    def tall_mask(columns):
        at = lax.broadcasted_iota(jnp.int32, (rows, columns), 0)
        inside = at < filled_here[0]
        for slot in range(1, slots):
            shifted = at - slot * length
            inside = inside | ((shifted >= 0) & (shifted < filled_here[slot]))
        return inside

    edges_out, edges_in = held["edges_out"], held["edges_in"]
    edges_out[...] = jnp.zeros_like(edges_out)
    for slot in range(slots):
        last = tokens[slot * length + length - TILE : slot * length + length, :].astype(F32)
        edges_out[0, slot : slot + 1, :] = last[TILE - 1 :, :]
    pl.semaphore_wait(barrier, greeted)
    edge_copy = copies.start(edges_out.at[0], edges_in.at[0], after)

    gain_mix, bias_mix = inputs["gain_mix"], inputs["bias_mix"]
    keep_edge = jnp.where(ch_at > 0, 1.0, 0.0)
    keep_next = jnp.where(ch_at < ch_size - 1, 1.0, 0.0)

    edge_copy.wait()
    edge_unit, _ = normalize(edges_in[0])
    edges_in[0] = (edge_unit * gain_mix[...] + bias_mix[...]) * keep_edge
    mixes = [inputs["mix_key"], inputs["mix_value"], inputs["mix_recept"]]
    both_mix = [held["both_key"], held["both_value"], held["both_recept"]]
    for slot in range(slots):

        def mix_step(index, carry, slot=slot):
            spot = tiles_of(slot, index)
            unit, _ = normalize(tokens[spot, :].astype(F32))
            normed = unit * gain_mix[...] + bias_mix[...]
            earlier = shift_down(normed, carry)
            for weights, target in zip(mixes, both_mix):
                target[spot, :] = blend(normed, earlier, weights[...]).astype(BF16)
            return normed[TILE - 1 :, :]

        lax.fori_loop(0, steps_in_slot, mix_step, edges_in[0, slot : slot + 1, :])
    exchanges = {}
    for name in ("key", "value", "recept"):
        ref = held["both_" + name]
        exchanges[name] = [
            copies.start(ref.at[pl.ds(0, rows), :], ref.at[pl.ds(rows, rows), :], partner)
        ]

    key_ref, value_ref = held["key"], held["value"]
    wide = {
        name: held["wide_" + name]
        for name in ("middle", "total", "sigmoid", "num", "den", "unit", "gap")
    }

    def own(name):
        return held["both_" + name].at[pl.ds(0, rows), :]

    def store_key(columns, product):
        key_ref[:, columns] = product.astype(BF16)

    def store_value(columns, product):
        value_ref[:, columns] = product.astype(BF16)

    matmul(own("key"), panels.take(), NN, store_key)
    panels.release()
    matmul(own("value"), panels.take(), NN, store_value)
    panels.release()

    time_decay, time_first = inputs["time_decay"], inputs["time_first"]
    square = (length, 3 * length)
    at_row = lax.broadcasted_iota(jnp.int32, square, 0)
    at_column = lax.rem(lax.broadcasted_iota(jnp.int32, square, 1), length)
    lower = jnp.where(at_column < at_row, 1.0, 0.0).astype(BF16)
    upper = jnp.where(at_column > at_row, 1.0, 0.0).astype(BF16)

    def triangle(matrix, value):
        high = value.astype(BF16)
        rest = value - high.astype(F32)
        middle = rest.astype(BF16)
        low = (rest - middle.astype(F32)).astype(BF16)
        return dot(matrix, jnp.concatenate([high, middle, low], axis=0), NN)

    sums_out, sums_in = held["sums_out"], held["sums_in"]
    sums_out[...] = jnp.zeros_like(sums_out)
    for slot in range(slots):

        def local_step(index, carry, slot=slot):
            columns = pl.ds(pl.multiple_of(index * WIDE, WIDE), WIDE)
            spot = pl.ds(slot * length, length)
            rate = jnp.exp(time_decay[:, columns])
            earlier, upto, filled = counts(slot, (length, WIDE), 0)
            stop = rate * filled_here[slot].astype(F32)
            keys = key_ref[spot, columns].astype(F32)
            weight = jnp.where(filled, jnp.exp(rate * upto - stop) * jnp.exp(keys), 0.0)
            payload = weight * value_ref[spot, columns].astype(F32)
            raised = jnp.exp(stop - rate * earlier)
            wide["num"][spot, columns] = raised * triangle(lower, payload)
            wide["den"][spot, columns] = raised * triangle(lower, weight)
            sums_out[0, slot : slot + 1, columns] = jnp.sum(payload, axis=0, keepdims=True)
            at = slots + slot
            sums_out[0, at : at + 1, columns] = jnp.sum(weight, axis=0, keepdims=True)
            return carry

        lax.fori_loop(0, width // WIDE, local_step, 0)

    def share(which):
        return [
            copies.start(
                sums_out.at[which],
                sums_in.at[which, step - 1],
                (seq_at, lax.rem(ch_at + step, ch_size)),
            )
            for step in range(1, ch_size)
        ]

    sum_copies = share(0)

    def store_sigmoid(columns, product):
        wide["sigmoid"][:, columns] = jax.nn.sigmoid(product)

    matmul(own("recept"), panels.take(), NN, store_sigmoid)
    panels.release()
    for copy in sum_copies:
        copy.wait()

    rate_row = jnp.exp(time_decay[...])
    states, finals = held["states"], held["finals"]
    states[...] = jnp.zeros_like(states)
    finals[...] = jnp.zeros_like(finals)
    for slot in range(slots):
        size = lengths[slot]
        reached = jnp.minimum(size, ch_at * length)
        for pair, initial in enumerate((inputs["init_num"], inputs["init_den"])):
            at = pair * slots + slot
            start_row = initial[slot : slot + 1, :]
            state = jnp.exp(-rate_row * reached.astype(F32)) * start_row
            final = jnp.exp(-rate_row * size.astype(F32)) * start_row
            for step in range(ch_size):
                source = lax.rem(ch_at + ch_size - step, ch_size)
                done = jnp.minimum(size, (source + 1) * length)
                term = (
                    sums_out[0, at : at + 1, :]
                    if step == 0
                    else sums_in[0, step - 1, at : at + 1, :]
                )
                final = final + jnp.exp(-rate_row * (size - done).astype(F32)) * term
                if step:
                    gone = jnp.maximum(reached - done, 0).astype(F32)
                    state = state + jnp.where(source < ch_at, jnp.exp(-rate_row * gone) * term, 0.0)
            states[at : at + 1, :] = state
            finals[at : at + 1, :] = final
    own_columns = pl.ds(pl.multiple_of(ch_at * plan.narrow, plan.narrow), plan.narrow)
    outputs["final"][...] = finals[:, own_columns]

    both_output = held["both_output"]
    for slot in range(slots):

        def wkv_step(index, carry, slot=slot):
            spot = tiles_of(slot, index)
            earlier, _, _ = counts(slot, (TILE, width), index * TILE)
            faded = jnp.exp(-rate_row * earlier)
            num = wide["num"][spot, :] + faded * states[slot : slot + 1, :]
            den = wide["den"][spot, :] + faded * states[slots + slot : slots + slot + 1, :]
            wide["num"][spot, :] = num
            wide["den"][spot, :] = den
            bonus = jnp.exp(time_first[...] + key_ref[spot, :].astype(F32))
            wkv = (num + bonus * value_ref[spot, :].astype(F32)) / (den + bonus)
            sent = wkv.astype(BF16).astype(F32)
            both_output[spot, :] = (wide["sigmoid"][spot, :] * sent).astype(BF16)
            return carry

        lax.fori_loop(0, steps_in_slot, wkv_step, 0)
    exchanges["output"] = [
        copies.start(
            both_output.at[pl.ds(0, rows), :], both_output.at[pl.ds(rows, rows), :], partner
        )
    ]

    def store_middle(columns, product):
        wide["middle"][:, columns] = tokens[:, columns].astype(F32) + product

    matmul(own("output"), panels.take(), NN, store_middle)
    panels.release()

    gain_ffn, bias_ffn = inputs["gain_ffn"], inputs["bias_ffn"]
    factor_ffn = held["factor_ffn"]
    for slot in range(slots):
        last = wide["middle"][slot * length + length - TILE : slot * length + length, :]
        unit, _ = normalize(last)
        edges_out[1, slot : slot + 1, :] = (unit * gain_ffn[...] + bias_ffn[...])[TILE - 1 :, :]
    edge_copy = copies.start(edges_out.at[1], edges_in.at[1], after)

    def unit_step(index, carry):
        spot = pl.ds(pl.multiple_of(index * TILE, TILE), TILE)
        unit, factor = normalize(wide["middle"][spot, :])
        wide["unit"][spot, :] = unit
        factor_ffn[spot, :] = jnp.broadcast_to(factor, (TILE, 128))
        return carry

    lax.fori_loop(0, rows // TILE, unit_step, 0)
    edge_copy.wait()
    blends = [inputs["blend_key"], inputs["blend_gate"]]
    both_blend = [held["both_expand"], held["both_gate"]]
    for slot in range(slots):

        def blend_step(index, carry, slot=slot):
            spot = tiles_of(slot, index)
            normed = wide["unit"][spot, :] * gain_ffn[...] + bias_ffn[...]
            earlier = shift_down(normed, carry)
            wide["gap"][spot, :] = normed - earlier
            for weights, target in zip(blends, both_blend):
                target[spot, :] = blend(normed, earlier, weights[...]).astype(BF16)
            return normed[TILE - 1 :, :]

        lax.fori_loop(
            0, steps_in_slot, blend_step, edges_in[1, slot : slot + 1, :] * keep_edge
        )
    for name in ("expand", "gate"):
        ref = held["both_" + name]
        exchanges[name] = [
            copies.start(ref.at[pl.ds(0, rows), :], ref.at[pl.ds(rows, rows), :], partner)
        ]

    both_hidden = held["both_hidden"]
    exchanges["hidden"] = []
    for index in range(panel_count):

        def store_hidden(columns, product, index=index):
            positive = jnp.maximum(product, 0.0)
            start = pl.multiple_of(columns.start + index * width, WIDE)
            both_hidden[first_rows, pl.ds(start, WIDE)] = (positive * positive).astype(BF16)

        matmul(own("expand"), panels.take(), NN, store_hidden)
        panels.release()
        part = pl.ds(index * width, width)
        exchanges["hidden"].append(
            copies.start(
                both_hidden.at[pl.ds(0, rows), part],
                both_hidden.at[pl.ds(rows, rows), part],
                partner,
            )
        )

        def add_contracted(columns, product, index=index):
            if index:
                product = product + wide["total"][:, columns]
            wide["total"][:, columns] = product

        matmul(both_hidden.at[pl.ds(0, rows), part], panels.take(), NN, add_contracted)
        panels.release()

    grad_contracted, grad_logit = held["rows_0"], held["rows_1"]

    def finish_forward(columns, product):
        gate = jax.nn.sigmoid(product)
        contracted = wide["total"][:, columns]
        inside = tall_mask(WIDE)
        mixed = wide["middle"][:, columns] + gate * contracted
        outputs["mixed_out"][:, columns] = jnp.where(inside, mixed, 0.0).astype(BF16)
        grad = jnp.where(inside, grad_out[:, columns].astype(F32), 0.0)
        grad_contracted[:, columns] = (grad * gate).astype(BF16)
        grad_logit[:, columns] = (grad * contracted * gate * (1.0 - gate)).astype(BF16)

    matmul(own("gate"), panels.take(), NN, finish_forward)
    panels.release()

    def hand_over(name, source):
        target = held["back_" + name]
        part = plan.narrow
        exchanges["back_" + name] = []
        for x_at in range(sizes["x"]):
            theirs = pl.multiple_of((x_at * 2 + 1 - place["k"]) * part, part)
            mine = pl.multiple_of((x_at * 2 + place["k"]) * part, part)
            spot = pl.ds(x_at * part, part)
            exchanges["back_" + name].append(
                copies.start(
                    source.at[:, pl.ds(theirs, part)],
                    target.at[pl.ds(rows, rows), spot],
                    partner,
                )
            )
            target[first_rows, spot] = source[:, pl.ds(mine, part)]

    def settle(*wanted):
        for name in wanted:
            for copy in exchanges.pop(name):
                copy.wait()

    height = min(256, width)
    owners = height // plan.short

    def emit_owners(emit, tile, value):
        for owner in range(owners):
            part = value[owner * plan.short : (owner + 1) * plan.short, :]
            emit((tile * (owners // 2) + owner // 2, owner % 2), part)

    def square_maker(name, first):
        lefts, rights = held["both_" + name], held["back_" + name]

        def by_x(x_at, emit):
            spot = pl.ds(pl.multiple_of(x_at * plan.narrow, plan.narrow), plan.narrow)

            def step(tile, carry):
                left = lefts[:, pl.ds(pl.multiple_of(tile * height, height), height)]
                emit_owners(emit, tile, dot(left, rights[:, spot], TN))
                return carry

            lax.fori_loop(0, width // height, step, 0)

        def by_z(z_at, emit):
            part = 2 * plan.short
            left = lefts[:, pl.ds(pl.multiple_of(z_at * part, part), part)]
            value = dot(left, rights[...], TN)
            for y_at in range(2):
                for x_at in range(sizes["x"]):
                    emit(
                        (y_at, x_at),
                        value[
                            y_at * plan.short : (y_at + 1) * plan.short,
                            x_at * plan.narrow : (x_at + 1) * plan.narrow,
                        ],
                    )

        return by_x if first == "x" else by_z

    def contract_maker(cut):
        part = plan.tall // plan.contract_cuts

        def make(y_at, emit):
            def step(z_at, carry):
                start = (z_at * 2 + y_at) * plan.tall + cut * part
                left = both_hidden[:, pl.ds(pl.multiple_of(start, part), part)]
                value = dot(left, held["back_contract"][...], TN)
                for x_at in range(sizes["x"]):
                    emit(
                        (z_at, x_at),
                        value[:, x_at * plan.narrow : (x_at + 1) * plan.narrow],
                    )
                return carry

            lax.fori_loop(0, sizes["z"], step, 0)

        return make

    grad_expanded, their_expanded = held["grad_expanded"], held["their_expanded"]

    def expand_maker(cut):
        part = plan.broad // plan.expand_cuts

        def make(x_at, emit):
            mine = pl.ds(
                pl.multiple_of((x_at * 2 + place["k"]) * plan.broad + cut * part, part), part
            )
            theirs = pl.ds(pl.multiple_of(x_at * plan.broad + cut * part, part), part)

            def step(tile, carry):
                spot = pl.ds(pl.multiple_of(tile * height, height), height)
                left = held["both_expand"]
                value = dot(left[first_rows, spot], grad_expanded[:, mine], TN)
                value = value + dot(left[last_rows, spot], their_expanded[:, theirs], TN)
                emit_owners(emit, tile, value)
                return carry

            lax.fori_loop(0, width // height, step, 0)

        return make

    pieces = {}
    seen = {}
    for index, (name, order_of, tall, broad) in enumerate(plan.pieces):
        cut = seen.get(name, 0)
        seen[name] = cut + 1
        out_ref = outputs["grad_" + name]
        if name == "contract":
            make = contract_maker(cut)
            out_ref = out_ref.at[pl.ds(cut * tall, tall), :]
        elif name == "expand":
            make = expand_maker(cut)
            out_ref = out_ref.at[:, pl.ds(cut * broad, broad)]
        else:
            make = square_maker(name, order_of[0])
        landings = [
            held["landing_" + str(index) + "_" + str(stage)] for stage in range(len(order_of))
        ]
        pieces[name + str(cut)] = Piece(
            make, order_of, sizes, place, copies, held["held_" + str(index)], landings, out_ref
        )
    contract_names = ["contract" + str(cut) for cut in range(plan.contract_cuts)]
    expand_names = ["expand" + str(cut) for cut in range(plan.expand_cuts)]

    hand_over("contract", grad_contracted)
    hand_over("gate", grad_logit)
    settle("hidden", "back_contract")
    for name in contract_names:
        pieces[name].start()

    for index in range(panel_count):

        def store_expanded(columns, product, index=index):
            start = pl.multiple_of(columns.start + index * width, WIDE)
            spot = pl.ds(start, WIDE)
            positive = jnp.sqrt(both_hidden[first_rows, spot].astype(F32))
            grad_expanded[:, spot] = (product * 2.0 * positive).astype(BF16)

        matmul(grad_contracted, panels.take(), NT, store_expanded)
        panels.release()
    exchanges["expanded"] = []
    for x_at in range(sizes["x"]):
        theirs = pl.multiple_of((x_at * 2 + 1 - place["k"]) * plan.broad, plan.broad)
        exchanges["expanded"].append(
            copies.start(
                grad_expanded.at[:, pl.ds(theirs, plan.broad)],
                their_expanded.at[:, pl.ds(x_at * plan.broad, plan.broad)],
                partner,
            )
        )
    for index in range(panel_count):

        def add_expand(columns, product, index=index):
            if index:
                product = product + wide["total"][:, columns]
            wide["total"][:, columns] = product

        matmul(
            grad_expanded,
            panels.take(),
            NT,
            add_expand,
            left_columns=pl.ds(index * width, width),
        )
        panels.release()

    def store_gate(columns, product):
        wide["middle"][:, columns] = product

    matmul(grad_logit, panels.take(), NT, store_gate)
    panels.release()

    for slot in range(slots):
        spot = slice(slot * length, slot * length + TILE)
        edge = wide["total"][spot, :] * (1.0 - blends[0][...])
        edge = edge + wide["middle"][spot, :] * (1.0 - blends[1][...])
        edges_out[2, slot : slot + 1, :] = edge[:1, :]
    edge_copy = copies.start(edges_out.at[2], edges_in.at[2], before)
    settle("expand", "expanded")
    for name in expand_names:
        pieces[name].start()
    settle("gate", "back_gate")
    pieces["gate0"].start()
    edge_copy.wait()

    grad_branch = held["rows_2"]
    for slot in range(slots):

        def ffn_back_step(index, carry, slot=slot):
            spot = tiles_of(slot, steps_in_slot - 1 - index)
            at = (steps_in_slot - 1 - index) * TILE
            in_expand, in_gate = wide["total"][spot, :], wide["middle"][spot, :]
            gap = wide["gap"][spot, :]
            unit = wide["unit"][spot, :]
            add_vector("blend_key", in_expand * gap)
            add_vector("blend_gate", in_gate * gap)
            weight_key, weight_gate = blends[0][...], blends[1][...]
            earlier = in_expand * (1.0 - weight_key) + in_gate * (1.0 - weight_gate)
            grad_normed = (
                in_expand * weight_key + in_gate * weight_gate + shift_up(earlier, carry)
            )
            add_vector("gain_ffn", grad_normed * unit)
            add_vector("bias_ffn", grad_normed)
            scaled = grad_normed * gain_ffn[...]
            centered = scaled - jnp.mean(scaled, axis=-1, keepdims=True)
            centered = centered - unit * jnp.mean(scaled * unit, axis=-1, keepdims=True)
            _, _, filled = counts(slot, (TILE, width), at)
            grad = jnp.where(filled, grad_out[spot, :].astype(F32), 0.0)
            grad = grad + factor_ffn[spot, :1] * centered
            wide["total"][spot, :] = grad
            grad_branch[spot, :] = grad.astype(BF16)
            return earlier[:1, :]

        lax.fori_loop(
            0, steps_in_slot, ffn_back_step, edges_in[2, slot : slot + 1, :] * keep_next
        )

    hand_over("output", grad_branch)
    grad_recept = held["rows_3"]

    def gated_back(columns, product):
        gate = wide["sigmoid"][:, columns]
        bonus = jnp.exp(time_first[:, columns] + key_ref[:, columns].astype(F32))
        norm = wide["den"][:, columns] + bonus
        wkv = (wide["num"][:, columns] + bonus * value_ref[:, columns].astype(F32)) / norm
        sent = wkv.astype(BF16).astype(F32)
        grad_wkv = (product * gate).astype(BF16).astype(F32)
        grad_recept[:, columns] = (product * sent * gate * (1.0 - gate)).astype(BF16)
        upper_part = grad_wkv / norm
        wide["middle"][:, columns] = upper_part
        wide["gap"][:, columns] = -upper_part * wkv

    matmul(grad_branch, panels.take(), NT, gated_back)
    panels.release()

    for slot in range(slots):

        def adjoint_step(index, carry, slot=slot):
            columns = pl.ds(pl.multiple_of(index * WIDE, WIDE), WIDE)
            spot = pl.ds(slot * length, length)
            rate = jnp.exp(time_decay[:, columns])
            earlier, upto, _ = counts(slot, (length, WIDE), 0)
            faded = jnp.exp(-rate * earlier)
            raised = jnp.exp(rate * upto)
            for pair, (source, target) in enumerate((("middle", "sigmoid"), ("gap", "unit"))):
                terms = faded * wide[source][spot, columns]
                wide[target][spot, columns] = raised * triangle(upper, terms)
                at = pair * slots + slot
                sums_out[1, at : at + 1, columns] = jnp.sum(terms, axis=0, keepdims=True)
            return carry

        lax.fori_loop(0, width // WIDE, adjoint_step, 0)
    sum_copies = share(1)
    settle("output", "back_output")
    pieces["output0"].start()
    for copy in sum_copies:
        copy.wait()
    later = held["later"]
    later[...] = jnp.zeros_like(later)
    for slot in range(slots):
        size = lengths[slot]
        done = jnp.minimum(size, (ch_at + 1) * length)
        for pair in range(2):
            at = pair * slots + slot
            total = jnp.zeros((1, width), F32)
            for step in range(1, ch_size):
                source = lax.rem(ch_at + ch_size - step, ch_size)
                reached = jnp.minimum(size, source * length)
                gone = jnp.maximum(reached - done, 0).astype(F32)
                term = sums_in[1, step - 1, at : at + 1, :]
                total = total + jnp.where(source > ch_at, jnp.exp(-rate_row * gone) * term, 0.0)
            later[at : at + 1, :] = total

    grad_key, grad_value = held["rows_0"], held["rows_1"]
    for slot in range(slots):

        def wkv_back_step(index, carry, slot=slot):
            spot = tiles_of(slot, index)
            _, upto, filled = counts(slot, (TILE, width), index * TILE)
            left = filled_here[slot].astype(F32) - upto
            faded = jnp.exp(-rate_row * left)
            adj_num = wide["sigmoid"][spot, :] + faded * later[slot : slot + 1, :]
            adj_den = wide["unit"][spot, :] + faded * later[slots + slot : slots + slot + 1, :]
            keys, values = key_ref[spot, :].astype(F32), value_ref[spot, :].astype(F32)
            bonus = jnp.exp(time_first[...] + keys)
            weight = jnp.where(filled, jnp.exp(keys), 0.0)
            upper_part, lower_part = wide["middle"][spot, :], wide["gap"][spot, :]
            direct = (upper_part * values + lower_part) * bonus
            grad_value[spot, :] = (upper_part * bonus + weight * adj_num).astype(BF16)
            grad_key[spot, :] = (direct + weight * (adj_num * values + adj_den)).astype(BF16)
            add_vector("time_first", direct)
            decay = adj_num * wide["num"][spot, :] + adj_den * wide["den"][spot, :]
            add_vector("time_decay", jnp.where(filled, decay, 0.0))
            return carry

        lax.fori_loop(0, steps_in_slot, wkv_back_step, 0)
    decay_at = VECTORS.index("time_decay")
    vectors[decay_at : decay_at + 1, :] *= -rate_row * jnp.exp(-rate_row)

    hand_over("key", grad_key)
    hand_over("value", grad_value)
    hand_over("recept", grad_recept)

    def keeper(name):
        def keep(columns, product):
            wide[name][:, columns] = product

        return keep

    for source, name in ((grad_key, "sigmoid"), (grad_value, "unit"), (grad_recept, "gap")):
        matmul(source, panels.take(), NT, keeper(name))
        panels.release()
    in_names = ("sigmoid", "unit", "gap")
    for slot in range(slots):
        spot = slice(slot * length, slot * length + TILE)
        edge = jnp.zeros((TILE, width), F32)
        for name, weights in zip(in_names, mixes):
            edge = edge + wide[name][spot, :] * (1.0 - weights[...])
        edges_out[3, slot : slot + 1, :] = edge[:1, :]
    edge_copy = copies.start(edges_out.at[3], edges_in.at[3], before)
    for name in ("key", "value", "recept"):
        settle(name, "back_" + name)
        pieces[name + "0"].start()

    for slot in range(slots):

        def again_step(index, carry, slot=slot):
            spot = tiles_of(slot, index)
            unit, _ = normalize(tokens[spot, :].astype(F32))
            normed = unit * gain_mix[...] + bias_mix[...]
            wide["num"][spot, :] = unit
            wide["den"][spot, :] = normed - shift_down(normed, carry)
            return normed[TILE - 1 :, :]

        lax.fori_loop(0, steps_in_slot, again_step, edges_in[0, slot : slot + 1, :])
    edge_copy.wait()
    vector_names = ("mix_key", "mix_value", "mix_recept")
    for slot in range(slots):

        def mix_back_step(index, carry, slot=slot):
            spot = tiles_of(slot, steps_in_slot - 1 - index)
            _, factor = normalize(tokens[spot, :].astype(F32))
            unit, gap = wide["num"][spot, :], wide["den"][spot, :]
            earlier = jnp.zeros((TILE, width), F32)
            grad_normed = jnp.zeros((TILE, width), F32)
            for name, weights, vector in zip(in_names, mixes, vector_names):
                grad = wide[name][spot, :]
                add_vector(vector, grad * gap)
                earlier = earlier + grad * (1.0 - weights[...])
                grad_normed = grad_normed + grad * weights[...]
            grad_normed = grad_normed + shift_up(earlier, carry)
            add_vector("gain_mix", grad_normed * unit)
            add_vector("bias_mix", grad_normed)
            scaled = grad_normed * gain_mix[...]
            centered = scaled - jnp.mean(scaled, axis=-1, keepdims=True)
            centered = centered - unit * jnp.mean(scaled * unit, axis=-1, keepdims=True)
            grad = wide["total"][spot, :] + factor * centered
            outputs["grad_tokens"][spot, :] = grad.astype(BF16)
            return earlier[:1, :]

        lax.fori_loop(
            0, steps_in_slot, mix_back_step, edges_in[3, slot : slot + 1, :] * keep_next
        )

    vector_in = held["vector_in"]
    vector_slot = 0

    def start_vectors(axis):
        nonlocal vector_slot
        found = []
        for step in range(1, sizes[axis]):
            there = device_at(moved(place, sizes, axis, step))
            found.append(copies.start(vectors, vector_in.at[vector_slot], there))
            vector_slot += 1
        return found

    def finish_vectors(found):
        for copy in found:
            copy.wait()
        for at in range(vector_slot - len(found), vector_slot):
            vectors[...] += vector_in[at]

    squares = ["gate0", "output0", "key0", "value0", "recept0"]
    rounds = contract_names[:1] + expand_names[:1] + ["gate0"]
    rounds += contract_names[1:] + expand_names[1:]
    rounds += ["output0", "key0", "value0", "recept0"]
    for turn in range(3):
        axis = "kxy"[turn]
        found = start_vectors(axis)
        for name in rounds:
            pieces[name].advance()
        finish_vectors(found)
    finish_vectors(start_vectors("z"))


def body(*arguments):
    values = dict(zip(INPUTS, arguments))
    plan = Plan(values["tokens"], values["w_expand"])
    rows, width = plan.rows, plan.width
    operands, specs = [], []
    for name in INPUTS:
        value = values[name]
        space = pltpu.VMEM
        if name in ("tokens", "grad_out"):
            value = value.reshape(rows, width)
        elif name == "lengths":
            space = pltpu.SMEM
        elif name.startswith("w_"):
            space = pl.ANY
        elif value.ndim == 1:
            value = value.reshape(1, width)
        operands.append(value)
        specs.append(pl.BlockSpec(memory_space=space))
    outs = {
        "mixed_out": ((rows, width), BF16),
        "grad_tokens": ((rows, width), BF16),
        "final": ((8, plan.narrow), F32),
        "grad_key": ((plan.short, plan.narrow), F32),
        "grad_value": ((plan.short, plan.narrow), F32),
        "grad_recept": ((plan.short, plan.narrow), F32),
        "grad_output": ((plan.short, plan.narrow), F32),
        "grad_expand": ((plan.short, plan.broad), F32),
        "grad_contract": ((plan.tall, plan.narrow), F32),
        "grad_gate": ((plan.short, plan.narrow), F32),
        "vectors": ((16, width), F32),
    }
    results = pl.pallas_call(
        functools.partial(layer_kernel, plan),
        out_shape=[jax.ShapeDtypeStruct(*outs[name]) for name in OUTPUTS],
        in_specs=specs,
        out_specs=[pl.BlockSpec(memory_space=pltpu.VMEM)] * len(OUTPUTS),
        scratch_shapes=list(plan.shapes.values()),
        compiler_params=pltpu.CompilerParams(
            collective_id=0, has_side_effects=True, vmem_limit_bytes=62 * 2**20
        ),
    )(*operands)
    got = dict(zip(OUTPUTS, results))
    shape = values["tokens"].shape
    part = width // (plan.seq * plan.ch)
    at = (lax.axis_index("seq") * plan.ch + lax.axis_index("ch")) * part
    vectors = lax.dynamic_slice_in_dim(got["vectors"], at, part, 1)
    slots = plan.slots
    return (
        got["mixed_out"].reshape(shape),
        got["grad_tokens"].reshape(shape),
        got["final"][:slots],
        got["final"][slots : 2 * slots],
        got["grad_key"],
        got["grad_value"],
        got["grad_recept"],
        got["grad_output"],
        got["grad_expand"],
        got["grad_contract"],
        got["grad_gate"],
    ) + tuple(vectors[index] for index in range(len(VECTORS)))


def solution(mesh):
    split, copied = P("seq", "ch", None), P()
    placed = (split, split, P("seq"), P("seq", None), P("seq", None)) + (copied,) * 18
    both = P("seq", "ch")
    return jax.shard_map(
        body,
        mesh=mesh,
        in_specs=placed,
        out_specs=(split, split) + (both,) * 9 + (P(("seq", "ch")),) * 11,
        check_vma=False,
    )
```

```python
import functools
import math

import jax
import jax.numpy as jnp
from jax import lax
from jax.experimental import pallas as pl
from jax.experimental.pallas import tpu as pltpu
from jax.sharding import PartitionSpec as P

EPS = 1e-05
MESH = pl.DeviceIdType.MESH
AXES = "hlyx"
F32 = jnp.float32
BF16 = jnp.bfloat16
TILE = 64
WIDE = 256
SLOTS_OF_WEIGHTS = 3

ORDERS = {
    "c0": "xylh",
    "c1": "yxlh",
    "c2": "lxyh",
    "c3": "yxlh",
    "e0": "xylh",
    "e1": "yxlh",
    "e2": "lyxh",
    "e3": "lxyh",
    "g": "lyxh",
    "o": "xylh",
    "k": "yxlh",
    "v": "xylh",
    "r": "yxlh",
}
PUMPS = (
    (),
    ("c0", "c1", "c2"),
    ("c3", "e0", "e2"),
    ("g", "c0", "c1", "c2"),
    (),
    ("e1", "e3", "o", "c3", "c0", "c1", "c2"),
)

NN = (((1,), (0,)), ((), ()))
NT = (((1,), (1,)), ((), ()))
TN = (((0,), (0,)), ((), ()))


def dot(left, right, how):
    return lax.dot_general(left, right, how, preferred_element_type=F32)


def axis_sizes():
    seq_size, ch_size = lax.axis_size("seq"), lax.axis_size("ch")
    return {"k": 2, "x": ch_size // 2, "y": 2, "l": 2, "h": seq_size // 4}


def coordinates():
    seq_at, ch_at = lax.axis_index("seq"), lax.axis_index("ch")
    return {
        "h": seq_at // 4,
        "l": seq_at // 2 % 2,
        "y": seq_at % 2,
        "x": ch_at // 2,
        "k": ch_at % 2,
    }


def device_at(place):
    return (place["h"] * 4 + place["l"] * 2 + place["y"], place["x"] * 2 + place["k"])


def moved(place, sizes, axis, step):
    return {**place, axis: lax.rem(place[axis] + step, sizes[axis])}


class Copies:
    def __init__(self, sends, receives):
        self.sends, self.receives, self.used = sends, receives, 0
        self.open = []

    def start(self, source, target, device):
        copy = pltpu.make_async_remote_copy(
            src_ref=source,
            dst_ref=target,
            send_sem=self.sends.at[self.used],
            recv_sem=self.receives.at[self.used],
            device_id=device,
            device_id_type=MESH,
        )
        self.used += 1
        copy.start()
        return copy


class Piece:
    def __init__(self, make, order, sizes, place, copies, held, landings, out_ref):
        self.make, self.order, self.sizes, self.place = make, order, sizes, place
        self.remote, self.held, self.landings, self.out_ref = copies, held, landings, out_ref
        self.axes = list(AXES)
        self.stage = 0
        self.copies = []

    def start(self):
        axis = self.order[self.stage]
        at = self.axes.index(axis)
        for step in range(1, self.sizes[axis]):
            there = moved(self.place, self.sizes, axis, step)
            if self.stage == 0:

                def keep(where, value, slot=step - 1):
                    self.held[(slot,) + where] = value.astype(BF16)

                self.make(there[axis], keep)
                source = self.held.at[step - 1]
            else:
                source = self.landings[self.stage - 1].at[
                    (0,) + (slice(None),) * at + (there[axis],)
                ]
            self.copies.append(
                self.remote.start(
                    source, self.landings[self.stage].at[step - 1], device_at(there)
                )
            )

    def finish(self):
        axis = self.order[self.stage]
        at = self.axes.index(axis)
        landing = self.landings[self.stage]
        others = self.sizes[axis] - 1
        for copy in self.copies:
            copy.wait()
        self.copies = []
        remaining = [a for a in self.axes if a != axis]
        if self.stage == 0:

            def add(where, value):
                for other in range(others):
                    value = value + landing[(other,) + where].astype(F32)
                landing[(0,) + where] = value.astype(BF16)

            self.make(self.place[axis], add)
        else:
            own = self.landings[self.stage - 1].at[
                (0,) + (slice(None),) * at + (self.place[axis],)
            ]
            lead = tuple(self.sizes[a] for a in remaining)
            rows, columns = landing.shape[-2:]
            tile = math.gcd(rows, max(16, 32768 // columns))
            parts = rows // tile

            def add_tile(index, carry):
                part, rest = index % parts, index // parts
                where = ()
                for size in reversed(lead):
                    where = (rest % size,) + where
                    rest = rest // size
                spot = pl.ds(pl.multiple_of(part * tile, tile), tile)
                where = where + (spot, slice(None))
                total = own[where].astype(F32)
                for other in range(others):
                    total = total + landing[(other,) + where].astype(F32)
                if remaining:
                    landing[(0,) + where] = total.astype(BF16)
                else:
                    self.out_ref[where] = total
                return carry

            lax.fori_loop(0, math.prod(lead) * parts, add_tile, 0)
        self.axes = remaining
        self.stage += 1

    def advance(self):
        self.finish()
        if self.axes:
            self.start()


class Plan:
    def __init__(self, tokens, w_expand):
        self.slots, self.length, self.width = tokens.shape
        self.hidden = w_expand.shape[1]
        self.sizes = sizes = axis_sizes()
        self.seq, self.ch = sizes["h"] * 4, sizes["x"] * 2
        self.rows = self.slots * self.length
        rows, width, hidden = self.rows, self.width, self.hidden
        self.narrow = width // self.ch
        self.broad = hidden // self.ch
        self.short = width // self.seq
        self.tall = hidden // self.seq
        half = sizes["x"] * self.narrow
        self.pieces = []
        cuts = 4 if (self.tall // 4) % 128 == 0 else 1
        part = self.tall // cuts
        for cut in range(cuts):
            self.pieces.append(("contract", "c" + str(cut), part, cut * part, self.narrow, 0))
        cuts = 4 if (self.broad // 4) % 128 == 0 else 1
        part = self.broad // cuts
        for cut in range(cuts):
            self.pieces.append(("expand", "e" + str(cut), self.short, 0, part, cut * part))
        for name in ("gate", "output", "key", "value", "recept"):
            self.pieces.append((name, name[0], self.short, 0, self.narrow, 0))
        self.orders = {
            piece[1]: ORDERS[piece[1]] if piece[2] % 128 == 0 else "xylh" for piece in self.pieces
        }
        vmem = pltpu.VMEM
        shapes = {
            "panels": vmem((SLOTS_OF_WEIGHTS, width, width), BF16),
            "both_hidden": vmem((2 * rows, hidden), BF16),
            "grad_expanded": vmem((rows, hidden), BF16),
            "their_expanded": vmem((rows, hidden // 2), BF16),
            "key": vmem((rows, width), BF16),
            "value": vmem((rows, width), BF16),
            "edges_out": vmem((4, 8, width), F32),
            "edges_in": vmem((4, 8, width), F32),
            "sums_out": vmem((2, 8, width), F32),
            "sums_in": vmem((2, self.ch - 1, 8, width), F32),
            "states": vmem((8, width), F32),
            "finals": vmem((8, width), F32),
            "later": vmem((8, width), F32),
            "factor_ffn": vmem((rows, 128), F32),
            "vector_in": vmem((self.count_vector_slots(), 16, width), F32),
        }
        for name in ("expand", "gate", "output", "key", "value", "recept"):
            shapes["both_" + name] = vmem((2 * rows, width), BF16)
        for name in ("contract", "gate", "output", "key", "value", "recept"):
            shapes["back_" + name] = vmem((2 * rows, half), BF16)
        for index in range(4):
            shapes["rows_" + str(index)] = vmem((rows, width), BF16)
        for name in ("middle", "total", "sigmoid", "num", "den", "unit", "gap"):
            shapes["wide_" + name] = vmem((rows, width), F32)
        copies = 64 + 4 * self.ch
        for name, short_name, height, _, breadth, _ in self.pieces:
            order = self.orders[short_name]
            axes = [axis for axis in AXES if axis != order[0]]
            lead = tuple(sizes[a] for a in axes)
            shapes["held_" + short_name] = vmem(
                (sizes[order[0]] - 1,) + lead + (height, breadth), BF16
            )
            axes = list(AXES)
            for stage, axis in enumerate(order):
                axes.remove(axis)
                shape = (sizes[axis] - 1,) + tuple(sizes[a] for a in axes) + (height, breadth)
                shapes["landing_" + short_name + str(stage)] = vmem(shape, BF16)
                copies += sizes[axis] - 1
        copies += self.count_vector_slots()
        shapes["sends"] = pltpu.SemaphoreType.DMA((copies,))
        shapes["receives"] = pltpu.SemaphoreType.DMA((copies,))
        shapes["panel_sems"] = pltpu.SemaphoreType.DMA((SLOTS_OF_WEIGHTS,))
        self.shapes = shapes

    def count_vector_slots(self):
        return sum(size - 1 for size in self.sizes.values())


INPUTS = (
    "tokens",
    "grad_out",
    "lengths",
    "init_num",
    "init_den",
    "w_key",
    "w_value",
    "w_recept",
    "w_output",
    "w_expand",
    "w_contract",
    "w_gate",
    "gain_mix",
    "bias_mix",
    "gain_ffn",
    "bias_ffn",
    "mix_key",
    "mix_value",
    "mix_recept",
    "blend_key",
    "blend_gate",
    "time_decay",
    "time_first",
)
OUTPUTS = (
    "mixed_out",
    "grad_tokens",
    "final",
    "grad_key",
    "grad_value",
    "grad_recept",
    "grad_output",
    "grad_expand",
    "grad_contract",
    "grad_gate",
    "vectors",
)
VECTORS = (
    "gain_mix",
    "bias_mix",
    "gain_ffn",
    "bias_ffn",
    "mix_key",
    "mix_value",
    "mix_recept",
    "blend_key",
    "blend_gate",
    "time_decay",
    "time_first",
)


class Panels:
    def __init__(self, sources, ref, sems):
        self.sources, self.ref, self.sems = sources, ref, sems
        self.used = 0
        for index in range(min(SLOTS_OF_WEIGHTS, len(sources))):
            self.copy(index).start()

    def copy(self, index):
        slot = index % SLOTS_OF_WEIGHTS
        return pltpu.make_async_copy(self.sources[index], self.ref.at[slot], self.sems.at[slot])

    def take(self):
        self.copy(self.used).wait()
        return self.ref.at[self.used % SLOTS_OF_WEIGHTS]

    def release(self):
        index = self.used + SLOTS_OF_WEIGHTS
        if index < len(self.sources):
            self.copy(index).start()
        self.used += 1


def layer_kernel(plan, *all_refs):
    inputs = dict(zip(INPUTS, all_refs))
    outputs = dict(zip(OUTPUTS, all_refs[len(INPUTS) :]))
    held = dict(zip(plan.shapes, all_refs[len(INPUTS) + len(OUTPUTS) :]))
    sizes = plan.sizes
    place = coordinates()
    ch_at = lax.axis_index("ch")
    seq_at = lax.axis_index("seq")
    slots, length, width, rows = plan.slots, plan.length, plan.width, plan.rows
    hidden, ch_size = plan.hidden, plan.ch
    panel_count = hidden // width
    tokens, grad_out, lengths = inputs["tokens"], inputs["grad_out"], inputs["lengths"]
    first_rows = slice(0, rows)
    last_rows = slice(rows, 2 * rows)

    w_expand, w_contract = inputs["w_expand"], inputs["w_contract"]

    def expand_panel(index):
        return w_expand.at[:, pl.ds(index * width, width)]

    def contract_panel(index):
        return w_contract.at[pl.ds(index * width, width), :]

    order = [inputs["w_key"], inputs["w_value"], inputs["w_recept"], inputs["w_output"]]
    for index in range(panel_count):
        order += [expand_panel(index), contract_panel(index)]
    order += [inputs["w_gate"]]
    order += [contract_panel(index) for index in range(panel_count)]
    order += [expand_panel(index) for index in range(panel_count)]
    order += [inputs["w_gate"], inputs["w_output"]]
    order += [inputs["w_key"], inputs["w_value"], inputs["w_recept"]]
    panels = Panels(order, held["panels"], held["panel_sems"])

    barrier = pltpu.get_barrier_semaphore()
    greeted = 0
    for step in range(1, ch_size):
        pl.semaphore_signal(
            barrier,
            inc=1,
            device_id=(seq_at, lax.rem(ch_at + step, ch_size)),
            device_id_type=MESH,
        )
        greeted += 1
    for axis in "ylh":
        for step in range(1, sizes[axis]):
            there = device_at(moved(place, sizes, axis, step))
            pl.semaphore_signal(barrier, inc=1, device_id=there, device_id_type=MESH)
            greeted += 1
    copies = Copies(held["sends"], held["receives"])
    partner = device_at({**place, "k": 1 - place["k"]})
    after = (seq_at, lax.rem(ch_at + 1, ch_size))
    before = (seq_at, lax.rem(ch_at + ch_size - 1, ch_size))

    filled_here = [
        jnp.clip(lengths[slot] - ch_at * length, 0, length) for slot in range(slots)
    ]
    vectors = outputs["vectors"]
    vectors[...] = jnp.zeros_like(vectors)

    def add_vector(name, value):
        at = VECTORS.index(name)
        vectors[at : at + 1, :] += jnp.sum(value, axis=0, keepdims=True)

    def normalize(value):
        center = value - jnp.mean(value, axis=-1, keepdims=True)
        factor = lax.rsqrt(jnp.mean(center * center, axis=-1, keepdims=True) + EPS)
        return center * factor, factor

    def blend(current, earlier, weights):
        return current * weights + earlier * (1.0 - weights)

    def tiles_of(slot, index):
        return pl.ds(pl.multiple_of(slot * length + index * TILE, TILE), TILE)

    row_in_tile = lax.broadcasted_iota(jnp.int32, (TILE, width), 0)

    def shift_down(value, carry):
        return jnp.where(row_in_tile == 0, carry, pltpu.roll(value, 1, 0))

    def shift_up(value, carry):
        return jnp.where(row_in_tile == TILE - 1, carry, pltpu.roll(value, TILE - 1, 0))

    steps_in_slot = length // TILE

    def matmul(left, panel, how, use, left_columns=None):
        def step(index, carry):
            columns = pl.ds(pl.multiple_of(index * WIDE, WIDE), WIDE)
            right = panel[:, columns] if how is NN else panel[columns, :]
            source = left[...] if left_columns is None else left[:, left_columns]
            use(columns, dot(source, right, how))
            return carry

        lax.fori_loop(0, width // WIDE, step, 0)

    def counts(slot, shape, offset):
        at = lax.broadcasted_iota(jnp.int32, shape, 0) + offset
        earlier = jnp.minimum(at, filled_here[slot]).astype(F32)
        upto = jnp.minimum(at + 1, filled_here[slot]).astype(F32)
        return earlier, upto, at < filled_here[slot]

    def tall_mask(columns):
        at = lax.broadcasted_iota(jnp.int32, (rows, columns), 0)
        inside = at < filled_here[0]
        for slot in range(1, slots):
            shifted = at - slot * length
            inside = inside | ((shifted >= 0) & (shifted < filled_here[slot]))
        return inside

    edges_out, edges_in = held["edges_out"], held["edges_in"]
    edges_out[...] = jnp.zeros_like(edges_out)
    for slot in range(slots):
        last = tokens[slot * length + length - TILE : slot * length + length, :].astype(F32)
        edges_out[0, slot : slot + 1, :] = last[TILE - 1 :, :]
    pl.semaphore_wait(barrier, greeted)
    edge_copy = copies.start(edges_out.at[0], edges_in.at[0], after)

    gain_mix, bias_mix = inputs["gain_mix"], inputs["bias_mix"]
    keep_edge = jnp.where(ch_at > 0, 1.0, 0.0)
    keep_next = jnp.where(ch_at < ch_size - 1, 1.0, 0.0)

    edge_copy.wait()
    edge_unit, _ = normalize(edges_in[0])
    edges_in[0] = (edge_unit * gain_mix[...] + bias_mix[...]) * keep_edge
    mixes = [inputs["mix_key"], inputs["mix_value"], inputs["mix_recept"]]
    both_mix = [held["both_key"], held["both_value"], held["both_recept"]]
    for slot in range(slots):

        def mix_step(index, carry, slot=slot):
            spot = tiles_of(slot, index)
            unit, _ = normalize(tokens[spot, :].astype(F32))
            normed = unit * gain_mix[...] + bias_mix[...]
            earlier = shift_down(normed, carry)
            for weights, target in zip(mixes, both_mix):
                target[spot, :] = blend(normed, earlier, weights[...]).astype(BF16)
            return normed[TILE - 1 :, :]

        lax.fori_loop(0, steps_in_slot, mix_step, edges_in[0, slot : slot + 1, :])
    exchanges = {}
    for name in ("key", "value", "recept"):
        ref = held["both_" + name]
        exchanges[name] = [
            copies.start(ref.at[pl.ds(0, rows), :], ref.at[pl.ds(rows, rows), :], partner)
        ]

    key_ref, value_ref = held["key"], held["value"]
    wide = {
        name: held["wide_" + name]
        for name in ("middle", "total", "sigmoid", "num", "den", "unit", "gap")
    }

    def own(name):
        return held["both_" + name].at[pl.ds(0, rows), :]

    def store_key(columns, product):
        key_ref[:, columns] = product.astype(BF16)

    def store_value(columns, product):
        value_ref[:, columns] = product.astype(BF16)

    matmul(own("key"), panels.take(), NN, store_key)
    panels.release()
    matmul(own("value"), panels.take(), NN, store_value)
    panels.release()

    time_decay, time_first = inputs["time_decay"], inputs["time_first"]
    square = (length, 3 * length)
    at_row = lax.broadcasted_iota(jnp.int32, square, 0)
    at_column = lax.rem(lax.broadcasted_iota(jnp.int32, square, 1), length)
    lower = jnp.where(at_column < at_row, 1.0, 0.0).astype(BF16)
    upper = jnp.where(at_column > at_row, 1.0, 0.0).astype(BF16)

    def triangle(matrix, value):
        high = value.astype(BF16)
        rest = value - high.astype(F32)
        middle = rest.astype(BF16)
        low = (rest - middle.astype(F32)).astype(BF16)
        return dot(matrix, jnp.concatenate([high, middle, low], axis=0), NN)

    sums_out, sums_in = held["sums_out"], held["sums_in"]
    sums_out[...] = jnp.zeros_like(sums_out)
    for slot in range(slots):

        def local_step(index, carry, slot=slot):
            columns = pl.ds(pl.multiple_of(index * WIDE, WIDE), WIDE)
            spot = pl.ds(slot * length, length)
            rate = jnp.exp(time_decay[:, columns])
            earlier, upto, filled = counts(slot, (length, WIDE), 0)
            stop = rate * filled_here[slot].astype(F32)
            keys = key_ref[spot, columns].astype(F32)
            weight = jnp.where(filled, jnp.exp(rate * upto - stop) * jnp.exp(keys), 0.0)
            payload = weight * value_ref[spot, columns].astype(F32)
            raised = jnp.exp(stop - rate * earlier)
            wide["num"][spot, columns] = raised * triangle(lower, payload)
            wide["den"][spot, columns] = raised * triangle(lower, weight)
            sums_out[0, slot : slot + 1, columns] = jnp.sum(payload, axis=0, keepdims=True)
            at = slots + slot
            sums_out[0, at : at + 1, columns] = jnp.sum(weight, axis=0, keepdims=True)
            return carry

        lax.fori_loop(0, width // WIDE, local_step, 0)

    def share(which):
        return [
            copies.start(
                sums_out.at[which],
                sums_in.at[which, step - 1],
                (seq_at, lax.rem(ch_at + step, ch_size)),
            )
            for step in range(1, ch_size)
        ]

    sum_copies = share(0)

    def store_sigmoid(columns, product):
        wide["sigmoid"][:, columns] = jax.nn.sigmoid(product)

    matmul(own("recept"), panels.take(), NN, store_sigmoid)
    panels.release()
    for copy in sum_copies:
        copy.wait()

    rate_row = jnp.exp(time_decay[...])
    states, finals = held["states"], held["finals"]
    states[...] = jnp.zeros_like(states)
    finals[...] = jnp.zeros_like(finals)
    for slot in range(slots):
        size = lengths[slot]
        reached = jnp.minimum(size, ch_at * length)
        for pair, initial in enumerate((inputs["init_num"], inputs["init_den"])):
            at = pair * slots + slot
            start_row = initial[slot : slot + 1, :]
            state = jnp.exp(-rate_row * reached.astype(F32)) * start_row
            final = jnp.exp(-rate_row * size.astype(F32)) * start_row
            for step in range(ch_size):
                source = lax.rem(ch_at + ch_size - step, ch_size)
                done = jnp.minimum(size, (source + 1) * length)
                term = (
                    sums_out[0, at : at + 1, :]
                    if step == 0
                    else sums_in[0, step - 1, at : at + 1, :]
                )
                final = final + jnp.exp(-rate_row * (size - done).astype(F32)) * term
                if step:
                    gone = jnp.maximum(reached - done, 0).astype(F32)
                    state = state + jnp.where(source < ch_at, jnp.exp(-rate_row * gone) * term, 0.0)
            states[at : at + 1, :] = state
            finals[at : at + 1, :] = final
    own_columns = pl.ds(pl.multiple_of(ch_at * plan.narrow, plan.narrow), plan.narrow)
    outputs["final"][...] = finals[:, own_columns]

    both_output = held["both_output"]
    for slot in range(slots):

        def wkv_step(index, carry, slot=slot):
            spot = tiles_of(slot, index)
            earlier, _, _ = counts(slot, (TILE, width), index * TILE)
            faded = jnp.exp(-rate_row * earlier)
            num = wide["num"][spot, :] + faded * states[slot : slot + 1, :]
            den = wide["den"][spot, :] + faded * states[slots + slot : slots + slot + 1, :]
            wide["num"][spot, :] = num
            wide["den"][spot, :] = den
            bonus = jnp.exp(time_first[...] + key_ref[spot, :].astype(F32))
            wkv = (num + bonus * value_ref[spot, :].astype(F32)) / (den + bonus)
            sent = wkv.astype(BF16).astype(F32)
            both_output[spot, :] = (wide["sigmoid"][spot, :] * sent).astype(BF16)
            return carry

        lax.fori_loop(0, steps_in_slot, wkv_step, 0)
    exchanges["output"] = [
        copies.start(
            both_output.at[pl.ds(0, rows), :], both_output.at[pl.ds(rows, rows), :], partner
        )
    ]

    def store_middle(columns, product):
        wide["middle"][:, columns] = tokens[:, columns].astype(F32) + product

    matmul(own("output"), panels.take(), NN, store_middle)
    panels.release()

    gain_ffn, bias_ffn = inputs["gain_ffn"], inputs["bias_ffn"]
    factor_ffn = held["factor_ffn"]
    for slot in range(slots):
        last = wide["middle"][slot * length + length - TILE : slot * length + length, :]
        unit, _ = normalize(last)
        edges_out[1, slot : slot + 1, :] = (unit * gain_ffn[...] + bias_ffn[...])[TILE - 1 :, :]
    edge_copy = copies.start(edges_out.at[1], edges_in.at[1], after)

    def unit_step(index, carry):
        spot = pl.ds(pl.multiple_of(index * TILE, TILE), TILE)
        unit, factor = normalize(wide["middle"][spot, :])
        wide["unit"][spot, :] = unit
        factor_ffn[spot, :] = jnp.broadcast_to(factor, (TILE, 128))
        return carry

    lax.fori_loop(0, rows // TILE, unit_step, 0)
    edge_copy.wait()
    blends = [inputs["blend_key"], inputs["blend_gate"]]
    both_blend = [held["both_expand"], held["both_gate"]]
    for slot in range(slots):

        def blend_step(index, carry, slot=slot):
            spot = tiles_of(slot, index)
            normed = wide["unit"][spot, :] * gain_ffn[...] + bias_ffn[...]
            earlier = shift_down(normed, carry)
            wide["gap"][spot, :] = normed - earlier
            for weights, target in zip(blends, both_blend):
                target[spot, :] = blend(normed, earlier, weights[...]).astype(BF16)
            return normed[TILE - 1 :, :]

        lax.fori_loop(
            0, steps_in_slot, blend_step, edges_in[1, slot : slot + 1, :] * keep_edge
        )
    for name in ("expand", "gate"):
        ref = held["both_" + name]
        exchanges[name] = [
            copies.start(ref.at[pl.ds(0, rows), :], ref.at[pl.ds(rows, rows), :], partner)
        ]

    both_hidden = held["both_hidden"]
    exchanges["hidden"] = []
    for index in range(panel_count):

        def store_hidden(columns, product, index=index):
            positive = jnp.maximum(product, 0.0)
            start = pl.multiple_of(columns.start + index * width, WIDE)
            both_hidden[first_rows, pl.ds(start, WIDE)] = (positive * positive).astype(BF16)

        matmul(own("expand"), panels.take(), NN, store_hidden)
        panels.release()
        part = pl.ds(index * width, width)
        exchanges["hidden"].append(
            copies.start(
                both_hidden.at[pl.ds(0, rows), part],
                both_hidden.at[pl.ds(rows, rows), part],
                partner,
            )
        )

        def add_contracted(columns, product, index=index):
            if index:
                product = product + wide["total"][:, columns]
            wide["total"][:, columns] = product

        matmul(both_hidden.at[pl.ds(0, rows), part], panels.take(), NN, add_contracted)
        panels.release()

    grad_contracted, grad_logit = held["rows_0"], held["rows_1"]

    def finish_forward(columns, product):
        gate = jax.nn.sigmoid(product)
        contracted = wide["total"][:, columns]
        inside = tall_mask(WIDE)
        mixed = wide["middle"][:, columns] + gate * contracted
        outputs["mixed_out"][:, columns] = jnp.where(inside, mixed, 0.0).astype(BF16)
        grad = jnp.where(inside, grad_out[:, columns].astype(F32), 0.0)
        grad_contracted[:, columns] = (grad * gate).astype(BF16)
        grad_logit[:, columns] = (grad * contracted * gate * (1.0 - gate)).astype(BF16)

    matmul(own("gate"), panels.take(), NN, finish_forward)
    panels.release()

    def hand_over(name, source):
        target = held["back_" + name]
        part = plan.narrow
        exchanges["back_" + name] = []
        for x_at in range(sizes["x"]):
            theirs = pl.multiple_of((x_at * 2 + 1 - place["k"]) * part, part)
            mine = pl.multiple_of((x_at * 2 + place["k"]) * part, part)
            spot = pl.ds(x_at * part, part)
            exchanges["back_" + name].append(
                copies.start(
                    source.at[:, pl.ds(theirs, part)],
                    target.at[pl.ds(rows, rows), spot],
                    partner,
                )
            )
            target[first_rows, spot] = source[:, pl.ds(mine, part)]

    def settle(*wanted):
        for name in wanted:
            for copy in exchanges.pop(name):
                copy.wait()

    grad_expanded, their_expanded = held["grad_expanded"], held["their_expanded"]

    def maker(piece):
        name, short_name, height, row_cut, breadth, column_cut = piece
        first = plan.orders[short_name][0]
        left = held["both_" + ("hidden" if name == "contract" else name)]
        row_step = plan.tall if name == "contract" else plan.short
        if name == "expand":
            rights = (
                (
                    first_rows,
                    grad_expanded,
                    lambda at: (at * 2 + place["k"]) * plan.broad + column_cut,
                ),
                (last_rows, their_expanded, lambda at: at * plan.broad + column_cut),
            )
        else:
            rights = ((slice(None), held["back_" + name], lambda at: at * plan.narrow),)

        def along(axis, coordinate):
            return [coordinate] if axis == first else range(sizes[axis])

        def make(coordinate, emit):
            places = [(l, y) for l in along("l", coordinate) for y in along("y", coordinate)]
            columns = along("x", coordinate)

            def step(h, carry):
                starts = [((h * 2 + l) * 2 + y) * row_step + row_cut for l, y in places]
                spans = [(start, height) for start in starts]
                if row_step == height and first in "xl":
                    spans = [(starts[0], len(starts) * height)]
                value = None
                for part, right, column_of in rights:
                    a = [
                        left[part, pl.ds(pl.multiple_of(start, math.gcd(span, 512)), span)]
                        for start, span in spans
                    ]
                    b = [
                        right[:, pl.ds(pl.multiple_of(column_of(x), breadth), breadth)]
                        for x in columns
                    ]
                    a = jnp.concatenate(a, axis=1) if len(a) > 1 else a[0]
                    b = jnp.concatenate(b, axis=1) if len(b) > 1 else b[0]
                    product = dot(a, b, TN)
                    value = product if value is None else value + product
                for index, (l, y) in enumerate(places):
                    rows_of = value[index * height : (index + 1) * height, :]
                    for x in columns:
                        at = 0 if first == "x" else x
                        block = rows_of[:, at * breadth : (at + 1) * breadth]
                        where = {"h": h, "l": l, "y": y, "x": x}
                        emit(tuple(where[a] for a in AXES if a != first), block)
                return carry

            lax.fori_loop(0, sizes["h"], step, 0)

        return make

    pieces = {}
    for piece in plan.pieces:
        name, short_name, height, row_cut, breadth, column_cut = piece
        order_of = plan.orders[short_name]
        out_ref = outputs["grad_" + name].at[
            pl.ds(row_cut, height), pl.ds(column_cut, breadth)
        ]
        landings = [held["landing_" + short_name + str(stage)] for stage in range(len(order_of))]
        pieces[short_name] = Piece(
            maker(piece),
            order_of,
            sizes,
            place,
            copies,
            held["held_" + short_name],
            landings,
            out_ref,
        )

    def start_pieces(prefix):
        for short_name, piece in pieces.items():
            if short_name.startswith(prefix):
                piece.start()

    def pump(point):
        for short_name in PUMPS[point]:
            piece = pieces.get(short_name)
            if piece is not None and piece.copies:
                piece.advance()

    hand_over("contract", grad_contracted)
    hand_over("gate", grad_logit)
    settle("hidden", "back_contract")
    start_pieces("c")

    for index in range(panel_count):

        def store_expanded(columns, product, index=index):
            start = pl.multiple_of(columns.start + index * width, WIDE)
            spot = pl.ds(start, WIDE)
            positive = jnp.sqrt(both_hidden[first_rows, spot].astype(F32))
            grad_expanded[:, spot] = (product * 2.0 * positive).astype(BF16)

        matmul(grad_contracted, panels.take(), NT, store_expanded)
        panels.release()
    exchanges["expanded"] = []
    for x_at in range(sizes["x"]):
        theirs = pl.multiple_of((x_at * 2 + 1 - place["k"]) * plan.broad, plan.broad)
        exchanges["expanded"].append(
            copies.start(
                grad_expanded.at[:, pl.ds(theirs, plan.broad)],
                their_expanded.at[:, pl.ds(x_at * plan.broad, plan.broad)],
                partner,
            )
        )
    for index in range(panel_count):

        def add_expand(columns, product, index=index):
            if index:
                product = product + wide["total"][:, columns]
            wide["total"][:, columns] = product

        matmul(
            grad_expanded,
            panels.take(),
            NT,
            add_expand,
            left_columns=pl.ds(index * width, width),
        )
        panels.release()

    settle("expand", "expanded")
    start_pieces("e")

    def store_gate(columns, product):
        wide["middle"][:, columns] = product

    matmul(grad_logit, panels.take(), NT, store_gate)
    panels.release()

    for slot in range(slots):
        spot = slice(slot * length, slot * length + TILE)
        edge = wide["total"][spot, :] * (1.0 - blends[0][...])
        edge = edge + wide["middle"][spot, :] * (1.0 - blends[1][...])
        edges_out[2, slot : slot + 1, :] = edge[:1, :]
    edge_copy = copies.start(edges_out.at[2], edges_in.at[2], before)
    settle("gate", "back_gate")
    start_pieces("g")
    pump(0)
    edge_copy.wait()

    grad_branch = held["rows_2"]
    for slot in range(slots):

        def ffn_back_step(index, carry, slot=slot):
            spot = tiles_of(slot, steps_in_slot - 1 - index)
            at = (steps_in_slot - 1 - index) * TILE
            in_expand, in_gate = wide["total"][spot, :], wide["middle"][spot, :]
            gap = wide["gap"][spot, :]
            unit = wide["unit"][spot, :]
            add_vector("blend_key", in_expand * gap)
            add_vector("blend_gate", in_gate * gap)
            weight_key, weight_gate = blends[0][...], blends[1][...]
            earlier = in_expand * (1.0 - weight_key) + in_gate * (1.0 - weight_gate)
            grad_normed = (
                in_expand * weight_key + in_gate * weight_gate + shift_up(earlier, carry)
            )
            add_vector("gain_ffn", grad_normed * unit)
            add_vector("bias_ffn", grad_normed)
            scaled = grad_normed * gain_ffn[...]
            centered = scaled - jnp.mean(scaled, axis=-1, keepdims=True)
            centered = centered - unit * jnp.mean(scaled * unit, axis=-1, keepdims=True)
            _, _, filled = counts(slot, (TILE, width), at)
            grad = jnp.where(filled, grad_out[spot, :].astype(F32), 0.0)
            grad = grad + factor_ffn[spot, :1] * centered
            wide["total"][spot, :] = grad
            grad_branch[spot, :] = grad.astype(BF16)
            return earlier[:1, :]

        lax.fori_loop(
            0, steps_in_slot, ffn_back_step, edges_in[2, slot : slot + 1, :] * keep_next
        )

    hand_over("output", grad_branch)
    pump(1)
    grad_recept = held["rows_3"]

    def gated_back(columns, product):
        gate = wide["sigmoid"][:, columns]
        bonus = jnp.exp(time_first[:, columns] + key_ref[:, columns].astype(F32))
        norm = wide["den"][:, columns] + bonus
        wkv = (wide["num"][:, columns] + bonus * value_ref[:, columns].astype(F32)) / norm
        sent = wkv.astype(BF16).astype(F32)
        grad_wkv = (product * gate).astype(BF16).astype(F32)
        grad_recept[:, columns] = (product * sent * gate * (1.0 - gate)).astype(BF16)
        upper_part = grad_wkv / norm
        wide["middle"][:, columns] = upper_part
        wide["gap"][:, columns] = -upper_part * wkv

    matmul(grad_branch, panels.take(), NT, gated_back)
    panels.release()

    for slot in range(slots):

        def adjoint_step(index, carry, slot=slot):
            columns = pl.ds(pl.multiple_of(index * WIDE, WIDE), WIDE)
            spot = pl.ds(slot * length, length)
            rate = jnp.exp(time_decay[:, columns])
            earlier, upto, _ = counts(slot, (length, WIDE), 0)
            faded = jnp.exp(-rate * earlier)
            raised = jnp.exp(rate * upto)
            for pair, (source, target) in enumerate((("middle", "sigmoid"), ("gap", "unit"))):
                terms = faded * wide[source][spot, columns]
                wide[target][spot, columns] = raised * triangle(upper, terms)
                at = pair * slots + slot
                sums_out[1, at : at + 1, columns] = jnp.sum(terms, axis=0, keepdims=True)
            return carry

        lax.fori_loop(0, width // WIDE, adjoint_step, 0)
    sum_copies = share(1)
    settle("output", "back_output")
    start_pieces("o")
    pump(2)
    for copy in sum_copies:
        copy.wait()
    later = held["later"]
    later[...] = jnp.zeros_like(later)
    for slot in range(slots):
        size = lengths[slot]
        done = jnp.minimum(size, (ch_at + 1) * length)
        for pair in range(2):
            at = pair * slots + slot
            total = jnp.zeros((1, width), F32)
            for step in range(1, ch_size):
                source = lax.rem(ch_at + ch_size - step, ch_size)
                reached = jnp.minimum(size, source * length)
                gone = jnp.maximum(reached - done, 0).astype(F32)
                term = sums_in[1, step - 1, at : at + 1, :]
                total = total + jnp.where(source > ch_at, jnp.exp(-rate_row * gone) * term, 0.0)
            later[at : at + 1, :] = total

    grad_key, grad_value = held["rows_0"], held["rows_1"]
    for slot in range(slots):

        def wkv_back_step(index, carry, slot=slot):
            spot = tiles_of(slot, index)
            _, upto, filled = counts(slot, (TILE, width), index * TILE)
            left = filled_here[slot].astype(F32) - upto
            faded = jnp.exp(-rate_row * left)
            adj_num = wide["sigmoid"][spot, :] + faded * later[slot : slot + 1, :]
            adj_den = wide["unit"][spot, :] + faded * later[slots + slot : slots + slot + 1, :]
            keys, values = key_ref[spot, :].astype(F32), value_ref[spot, :].astype(F32)
            bonus = jnp.exp(time_first[...] + keys)
            weight = jnp.where(filled, jnp.exp(keys), 0.0)
            upper_part, lower_part = wide["middle"][spot, :], wide["gap"][spot, :]
            direct = (upper_part * values + lower_part) * bonus
            grad_value[spot, :] = (upper_part * bonus + weight * adj_num).astype(BF16)
            grad_key[spot, :] = (direct + weight * (adj_num * values + adj_den)).astype(BF16)
            add_vector("time_first", direct)
            decay = adj_num * wide["num"][spot, :] + adj_den * wide["den"][spot, :]
            add_vector("time_decay", jnp.where(filled, decay, 0.0))
            return carry

        lax.fori_loop(0, steps_in_slot, wkv_back_step, 0)
    decay_at = VECTORS.index("time_decay")
    vectors[decay_at : decay_at + 1, :] *= -rate_row * jnp.exp(-rate_row)

    hand_over("key", grad_key)
    hand_over("value", grad_value)
    hand_over("recept", grad_recept)
    pump(3)

    def keeper(name):
        def keep(columns, product):
            wide[name][:, columns] = product

        return keep

    for source, name in ((grad_key, "sigmoid"), (grad_value, "unit"), (grad_recept, "gap")):
        matmul(source, panels.take(), NT, keeper(name))
        panels.release()
    in_names = ("sigmoid", "unit", "gap")
    for slot in range(slots):
        spot = slice(slot * length, slot * length + TILE)
        edge = jnp.zeros((TILE, width), F32)
        for name, weights in zip(in_names, mixes):
            edge = edge + wide[name][spot, :] * (1.0 - weights[...])
        edges_out[3, slot : slot + 1, :] = edge[:1, :]
    edge_copy = copies.start(edges_out.at[3], edges_in.at[3], before)
    for name in ("key", "value", "recept"):
        settle(name, "back_" + name)
        start_pieces(name[0])
    pump(4)

    for slot in range(slots):

        def again_step(index, carry, slot=slot):
            spot = tiles_of(slot, index)
            unit, _ = normalize(tokens[spot, :].astype(F32))
            normed = unit * gain_mix[...] + bias_mix[...]
            wide["num"][spot, :] = unit
            wide["den"][spot, :] = normed - shift_down(normed, carry)
            return normed[TILE - 1 :, :]

        lax.fori_loop(0, steps_in_slot, again_step, edges_in[0, slot : slot + 1, :])
    edge_copy.wait()
    vector_names = ("mix_key", "mix_value", "mix_recept")
    for slot in range(slots):

        def mix_back_step(index, carry, slot=slot):
            spot = tiles_of(slot, steps_in_slot - 1 - index)
            _, factor = normalize(tokens[spot, :].astype(F32))
            unit, gap = wide["num"][spot, :], wide["den"][spot, :]
            earlier = jnp.zeros((TILE, width), F32)
            grad_normed = jnp.zeros((TILE, width), F32)
            for name, weights, vector in zip(in_names, mixes, vector_names):
                grad = wide[name][spot, :]
                add_vector(vector, grad * gap)
                earlier = earlier + grad * (1.0 - weights[...])
                grad_normed = grad_normed + grad * weights[...]
            grad_normed = grad_normed + shift_up(earlier, carry)
            add_vector("gain_mix", grad_normed * unit)
            add_vector("bias_mix", grad_normed)
            scaled = grad_normed * gain_mix[...]
            centered = scaled - jnp.mean(scaled, axis=-1, keepdims=True)
            centered = centered - unit * jnp.mean(scaled * unit, axis=-1, keepdims=True)
            grad = wide["total"][spot, :] + factor * centered
            outputs["grad_tokens"][spot, :] = grad.astype(BF16)
            return earlier[:1, :]

        lax.fori_loop(
            0, steps_in_slot, mix_back_step, edges_in[3, slot : slot + 1, :] * keep_next
        )

    vector_in = held["vector_in"]
    vector_slot = 0

    def start_vectors(axis):
        nonlocal vector_slot
        found = []
        for step in range(1, sizes[axis]):
            there = device_at(moved(place, sizes, axis, step))
            found.append(copies.start(vectors, vector_in.at[vector_slot], there))
            vector_slot += 1
        return found

    def finish_vectors(found):
        for copy in found:
            copy.wait()
        for at in range(vector_slot - len(found), vector_slot):
            vectors[...] += vector_in[at]

    found = start_vectors("k")
    pump(5)
    finish_vectors(found)
    found = start_vectors("x")
    later_axes = ["y", "l", "h"]
    while any(piece.copies for piece in pieces.values()):
        for stage in range(len(AXES)):
            waiting = [p for p in pieces.values() if p.copies and p.stage == stage]
            if waiting:
                break
        for piece in waiting:
            piece.advance()
        finish_vectors(found)
        found = start_vectors(later_axes.pop(0)) if later_axes else []
    finish_vectors(found)
    for axis in later_axes:
        finish_vectors(start_vectors(axis))


def place_outputs(plan, *refs):
    count = len(OUTPUTS)
    for source, target in zip(refs[: count - 1], refs[count:]):
        target[...] = source[...]
    part = plan.width // (plan.seq * plan.ch)
    at = (lax.axis_index("seq") * plan.ch + lax.axis_index("ch")) * part
    turned = pltpu.roll(refs[count - 1][...], lax.rem(plan.width - at, plan.width), 1)
    for index, target in enumerate(refs[2 * count - 1 :]):
        target[...] = turned[index : index + 1, :part]


def body(*arguments):
    values = dict(zip(INPUTS, arguments))
    plan = Plan(values["tokens"], values["w_expand"])
    rows, width = plan.rows, plan.width
    operands, specs = [], []
    for name in INPUTS:
        value = values[name]
        space = pltpu.VMEM
        if name in ("tokens", "grad_out"):
            value = value.reshape(rows, width)
        elif name == "lengths":
            space = pltpu.SMEM
        elif name.startswith("w_"):
            space = pl.ANY
        elif value.ndim == 1:
            value = value.reshape(1, width)
        operands.append(value)
        specs.append(pl.BlockSpec(memory_space=space))
    outs = {
        "mixed_out": ((rows, width), BF16),
        "grad_tokens": ((rows, width), BF16),
        "final": ((8, plan.narrow), F32),
        "grad_key": ((plan.short, plan.narrow), F32),
        "grad_value": ((plan.short, plan.narrow), F32),
        "grad_recept": ((plan.short, plan.narrow), F32),
        "grad_output": ((plan.short, plan.narrow), F32),
        "grad_expand": ((plan.short, plan.broad), F32),
        "grad_contract": ((plan.tall, plan.narrow), F32),
        "grad_gate": ((plan.short, plan.narrow), F32),
        "vectors": ((16, width), F32),
    }
    results = pl.pallas_call(
        functools.partial(layer_kernel, plan),
        out_shape=[jax.ShapeDtypeStruct(*outs[name]) for name in OUTPUTS],
        in_specs=specs,
        out_specs=[pl.BlockSpec(memory_space=pltpu.VMEM)] * len(OUTPUTS),
        scratch_shapes=list(plan.shapes.values()),
        compiler_params=pltpu.CompilerParams(
            collective_id=0, has_side_effects=True, vmem_limit_bytes=62 * 2**20
        ),
    )(*operands)
    part = width // (plan.seq * plan.ch)
    shapes = [outs[name] for name in OUTPUTS[:-1]] + [((1, part), F32)] * len(VECTORS)
    results = pl.pallas_call(
        functools.partial(place_outputs, plan),
        out_shape=[jax.ShapeDtypeStruct(*shape) for shape in shapes],
        in_specs=[pl.BlockSpec(memory_space=pltpu.VMEM)] * len(OUTPUTS),
        out_specs=[pl.BlockSpec(memory_space=pltpu.VMEM)] * len(shapes),
    )(*results)
    got = dict(zip(OUTPUTS[:-1], results))
    vectors = results[len(OUTPUTS) - 1 :]
    shape = values["tokens"].shape
    slots = plan.slots
    return (
        got["mixed_out"].reshape(shape),
        got["grad_tokens"].reshape(shape),
        got["final"][:slots],
        got["final"][slots : 2 * slots],
        got["grad_key"],
        got["grad_value"],
        got["grad_recept"],
        got["grad_output"],
        got["grad_expand"],
        got["grad_contract"],
        got["grad_gate"],
    ) + tuple(vector.reshape(part) for vector in vectors)


def solution(mesh):
    split, copied = P("seq", "ch", None), P()
    placed = (split, split, P("seq"), P("seq", None), P("seq", None)) + (copied,) * 18
    both = P("seq", "ch")
    return jax.shard_map(
        body,
        mesh=mesh,
        in_specs=placed,
        out_specs=(split, split) + (both,) * 9 + (P(("seq", "ch")),) * 11,
        check_vma=False,
    )
```

```python
import functools
import math

import jax
import jax.numpy as jnp
from jax import lax
from jax.experimental import pallas as pl
from jax.experimental.pallas import tpu as pltpu
from jax.sharding import PartitionSpec as P

EPS = 1e-05
MESH = pl.DeviceIdType.MESH
AXES = "hlyx"
F32 = jnp.float32
BF16 = jnp.bfloat16
TILE = 64
WIDE = 256
MATMUL_WIDE = 512
SLOTS_OF_WEIGHTS = 3

ORDERS = {
    "c0": "xlyh",
    "c1": "ylhx",
    "c2": "lxyh",
    "c3": "xylh",
    "e0": "lxyh",
    "e1": "ylxh",
    "e2": "xylh",
    "e3": "ylxh",
    "g": "ylxh",
    "o": "xylh",
    "k": "xylh",
    "v": "xylh",
    "r": "xylh",
}
PUMPS = (
    (),
    (
        "c0", "c1",
    ),
    (
        "e1",
    ),
    (
        "c3",
    ),
    (
        "c0",
    ),
    (
        "e2", "c1", "e3",
    ),
    (),
    (
        "c2", "e0", "e1", "o", "c1", "g", "e3", "c3", "c0", "r", "!", "g", "*", "c3", "e2", "c0",
        "c3", "o", "k", "e2", "o", "r", "e2", "o", "k", "v", "r", "k", "c2", "r", "v", "k", "c2",
        "e0", "v", "e1", "c2", "c1", "e0", "v", "e3", "e1", "g", "*", "e0", "e3", "g", "*",
    ),
)

NN = (((1,), (0,)), ((), ()))
NT = (((1,), (1,)), ((), ()))
TN = (((0,), (0,)), ((), ()))


def dot(left, right, how):
    return lax.dot_general(left, right, how, preferred_element_type=F32)


def axis_sizes():
    seq_size, ch_size = lax.axis_size("seq"), lax.axis_size("ch")
    return {"k": 2, "x": ch_size // 2, "y": 2, "l": 2, "h": seq_size // 4}


def coordinates():
    seq_at, ch_at = lax.axis_index("seq"), lax.axis_index("ch")
    return {
        "h": seq_at // 4,
        "l": seq_at // 2 % 2,
        "y": seq_at % 2,
        "x": ch_at // 2,
        "k": ch_at % 2,
    }


def device_at(place):
    return (place["h"] * 4 + place["l"] * 2 + place["y"], place["x"] * 2 + place["k"])


def moved(place, sizes, axis, step):
    return {**place, axis: lax.rem(place[axis] + step, sizes[axis])}


class Copies:
    def __init__(self, sends, receives):
        self.sends, self.receives, self.used = sends, receives, 0
        self.open = []

    def start(self, source, target, device):
        copy = pltpu.make_async_remote_copy(
            src_ref=source,
            dst_ref=target,
            send_sem=self.sends.at[self.used],
            recv_sem=self.receives.at[self.used],
            device_id=device,
            device_id_type=MESH,
        )
        self.used += 1
        copy.start()
        return copy


class Piece:
    def __init__(self, make, order, sizes, place, copies, held, landings, out_ref):
        self.make, self.order, self.sizes, self.place = make, order, sizes, place
        self.remote, self.held, self.landings, self.out_ref = copies, held, landings, out_ref
        self.axes = list(AXES)
        self.stage = 0
        self.copies = []

    def start(self):
        axis = self.order[self.stage]
        at = self.axes.index(axis)
        for step in range(1, self.sizes[axis]):
            there = moved(self.place, self.sizes, axis, step)
            if self.stage == 0:

                def keep(where, value, slot=step - 1):
                    self.held[(slot,) + where] = value.astype(BF16)

                self.make(there[axis], keep)
                source = self.held.at[step - 1]
            else:
                source = self.landings[self.stage - 1].at[
                    (0,) + (slice(None),) * at + (there[axis],)
                ]
            self.copies.append(
                self.remote.start(
                    source, self.landings[self.stage].at[step - 1], device_at(there)
                )
            )

    def finish(self):
        axis = self.order[self.stage]
        at = self.axes.index(axis)
        landing = self.landings[self.stage]
        others = self.sizes[axis] - 1
        for copy in self.copies:
            copy.wait()
        self.copies = []
        remaining = [a for a in self.axes if a != axis]
        if self.stage == 0:

            def add(where, value):
                for other in range(others):
                    value = value + landing[(other,) + where].astype(F32)
                landing[(0,) + where] = value.astype(BF16)

            self.make(self.place[axis], add)
        else:
            own = self.landings[self.stage - 1].at[
                (0,) + (slice(None),) * at + (self.place[axis],)
            ]
            lead = tuple(self.sizes[a] for a in remaining)
            rows, columns = landing.shape[-2:]
            tile = math.gcd(rows, max(16, 32768 // columns))
            parts = rows // tile

            def add_tile(index, carry):
                part, rest = index % parts, index // parts
                where = ()
                for size in reversed(lead):
                    where = (rest % size,) + where
                    rest = rest // size
                spot = pl.ds(pl.multiple_of(part * tile, tile), tile)
                where = where + (spot, slice(None))
                total = own[where].astype(F32)
                for other in range(others):
                    total = total + landing[(other,) + where].astype(F32)
                if remaining:
                    landing[(0,) + where] = total.astype(BF16)
                else:
                    self.out_ref[where] = total
                return carry

            lax.fori_loop(0, math.prod(lead) * parts, add_tile, 0)
        self.axes = remaining
        self.stage += 1

    def advance(self):
        self.finish()
        if self.axes:
            self.start()


class Plan:
    def __init__(self, tokens, w_expand):
        self.slots, self.length, self.width = tokens.shape
        self.hidden = w_expand.shape[1]
        self.sizes = sizes = axis_sizes()
        self.seq, self.ch = sizes["h"] * 4, sizes["x"] * 2
        self.rows = self.slots * self.length
        rows, width, hidden = self.rows, self.width, self.hidden
        self.narrow = width // self.ch
        self.broad = hidden // self.ch
        self.short = width // self.seq
        self.tall = hidden // self.seq
        self.vector_span = self.short if self.short % 128 == 0 else width
        half = sizes["x"] * self.narrow
        self.pieces = []
        cuts = 4 if (self.tall // 4) % 128 == 0 else 1
        part = self.tall // cuts
        for cut in range(cuts):
            self.pieces.append(("contract", "c" + str(cut), part, cut * part, self.narrow, 0))
        cuts = 4 if (self.broad // 4) % 128 == 0 else 1
        part = self.broad // cuts
        for cut in range(cuts):
            self.pieces.append(("expand", "e" + str(cut), self.short, 0, part, cut * part))
        for name in ("gate", "output", "key", "value", "recept"):
            self.pieces.append((name, name[0], self.short, 0, self.narrow, 0))
        self.orders = {
            piece[1]: ORDERS[piece[1]] if piece[2] % 128 == 0 else "xylh" for piece in self.pieces
        }
        vmem = pltpu.VMEM
        shapes = {
            "panels": vmem((SLOTS_OF_WEIGHTS, width, width), BF16),
            "both_hidden": vmem((2 * rows, hidden), BF16),
            "grad_expanded": vmem((rows, hidden), BF16),
            "their_expanded": vmem((rows, hidden // 2), BF16),
            "key": vmem((rows, width), BF16),
            "value": vmem((rows, width), BF16),
            "edges_out": vmem((4, 8, width), F32),
            "edges_in": vmem((4, 8, width), F32),
            "sums_out": vmem((2, 8, width), F32),
            "sums_in": vmem((2, self.ch - 1, 8, width), F32),
            "states": vmem((8, width), F32),
            "finals": vmem((8, width), F32),
            "later": vmem((8, width), F32),
            "factor_ffn": vmem((rows, 128), F32),
            "vectors": vmem((16, width), F32),
            "vector_in": vmem((self.count_vector_slots(), 16, width), F32),
            "vector_parts": vmem((self.seq - 1, 16, self.vector_span), F32),
        }
        for name in ("expand", "gate", "output", "key", "value", "recept"):
            shapes["both_" + name] = vmem((2 * rows, width), BF16)
        for name in ("contract", "gate", "output", "key", "value", "recept"):
            shapes["back_" + name] = vmem((2 * rows, half), BF16)
        for index in range(4):
            shapes["rows_" + str(index)] = vmem((rows, width), BF16)
        for name in ("middle", "total", "sigmoid", "num", "den", "unit", "gap"):
            shapes["wide_" + name] = vmem((rows, width), F32)
        copies = 64 + 4 * self.ch
        for name, short_name, height, _, breadth, _ in self.pieces:
            order = self.orders[short_name]
            axes = [axis for axis in AXES if axis != order[0]]
            lead = tuple(sizes[a] for a in axes)
            shapes["held_" + short_name] = vmem(
                (sizes[order[0]] - 1,) + lead + (height, breadth), BF16
            )
            axes = list(AXES)
            for stage, axis in enumerate(order):
                axes.remove(axis)
                shape = (sizes[axis] - 1,) + tuple(sizes[a] for a in axes) + (height, breadth)
                shapes["landing_" + short_name + str(stage)] = vmem(shape, BF16)
                copies += sizes[axis] - 1
        copies += self.count_vector_slots() + self.seq
        shapes["sends"] = pltpu.SemaphoreType.DMA((copies,))
        shapes["receives"] = pltpu.SemaphoreType.DMA((copies,))
        shapes["panel_sems"] = pltpu.SemaphoreType.DMA((SLOTS_OF_WEIGHTS,))
        self.shapes = shapes

    def count_vector_slots(self):
        axes = "kx" if self.vector_span < self.width else "kxylh"
        return sum(self.sizes[axis] - 1 for axis in axes)


INPUTS = (
    "tokens",
    "grad_out",
    "lengths",
    "init_num",
    "init_den",
    "w_key",
    "w_value",
    "w_recept",
    "w_output",
    "w_expand",
    "w_contract",
    "w_gate",
    "gain_mix",
    "bias_mix",
    "gain_ffn",
    "bias_ffn",
    "mix_key",
    "mix_value",
    "mix_recept",
    "blend_key",
    "blend_gate",
    "time_decay",
    "time_first",
)
OUTPUTS = (
    "mixed_out",
    "grad_tokens",
    "final",
    "grad_key",
    "grad_value",
    "grad_recept",
    "grad_output",
    "grad_expand",
    "grad_contract",
    "grad_gate",
    "vectors",
)
VECTORS = (
    "gain_mix",
    "bias_mix",
    "gain_ffn",
    "bias_ffn",
    "mix_key",
    "mix_value",
    "mix_recept",
    "blend_key",
    "blend_gate",
    "time_decay",
    "time_first",
)


class Panels:
    def __init__(self, sources, ref, sems):
        self.sources, self.ref, self.sems = sources, ref, sems
        self.used = 0
        for index in range(min(SLOTS_OF_WEIGHTS, len(sources))):
            self.copy(index).start()

    def copy(self, index):
        slot = index % SLOTS_OF_WEIGHTS
        return pltpu.make_async_copy(self.sources[index], self.ref.at[slot], self.sems.at[slot])

    def take(self):
        self.copy(self.used).wait()
        return self.ref.at[self.used % SLOTS_OF_WEIGHTS]

    def release(self):
        index = self.used + SLOTS_OF_WEIGHTS
        if index < len(self.sources):
            self.copy(index).start()
        self.used += 1


def layer_kernel(plan, *all_refs):
    inputs = dict(zip(INPUTS, all_refs))
    outputs = dict(zip(OUTPUTS, all_refs[len(INPUTS) :]))
    held = dict(zip(plan.shapes, all_refs[len(INPUTS) + len(OUTPUTS) :]))
    sizes = plan.sizes
    place = coordinates()
    ch_at = lax.axis_index("ch")
    seq_at = lax.axis_index("seq")
    slots, length, width, rows = plan.slots, plan.length, plan.width, plan.rows
    hidden, ch_size = plan.hidden, plan.ch
    panel_count = hidden // width
    tokens, grad_out, lengths = inputs["tokens"], inputs["grad_out"], inputs["lengths"]
    first_rows = slice(0, rows)
    last_rows = slice(rows, 2 * rows)

    w_expand, w_contract = inputs["w_expand"], inputs["w_contract"]

    def expand_panel(index):
        return w_expand.at[:, pl.ds(index * width, width)]

    def contract_panel(index):
        return w_contract.at[pl.ds(index * width, width), :]

    order = [inputs["w_key"], inputs["w_value"], inputs["w_recept"], inputs["w_output"]]
    for index in range(panel_count):
        order += [expand_panel(index), contract_panel(index)]
    order += [inputs["w_gate"]]
    order += [contract_panel(index) for index in range(panel_count)]
    order += [expand_panel(index) for index in range(panel_count)]
    order += [inputs["w_gate"], inputs["w_output"]]
    order += [inputs["w_key"], inputs["w_value"], inputs["w_recept"]]
    panels = Panels(order, held["panels"], held["panel_sems"])

    barrier = pltpu.get_barrier_semaphore()
    greeted = 0
    for step in range(1, ch_size):
        pl.semaphore_signal(
            barrier,
            inc=1,
            device_id=(seq_at, lax.rem(ch_at + step, ch_size)),
            device_id_type=MESH,
        )
        greeted += 1
    for step in range(1, plan.seq):
        pl.semaphore_signal(
            barrier,
            inc=1,
            device_id=(lax.rem(seq_at + step, plan.seq), ch_at),
            device_id_type=MESH,
        )
        greeted += 1
    copies = Copies(held["sends"], held["receives"])
    partner = device_at({**place, "k": 1 - place["k"]})
    after = (seq_at, lax.rem(ch_at + 1, ch_size))
    before = (seq_at, lax.rem(ch_at + ch_size - 1, ch_size))

    filled_here = [
        jnp.clip(lengths[slot] - ch_at * length, 0, length) for slot in range(slots)
    ]
    vectors = held["vectors"]
    vectors[...] = jnp.zeros_like(vectors)

    def add_vector(name, value):
        at = VECTORS.index(name)
        vectors[at : at + 1, :] += jnp.sum(value, axis=0, keepdims=True)

    def normalize(value):
        center = value - jnp.mean(value, axis=-1, keepdims=True)
        factor = lax.rsqrt(jnp.mean(center * center, axis=-1, keepdims=True) + EPS)
        return center * factor, factor

    def blend(current, earlier, weights):
        return current * weights + earlier * (1.0 - weights)

    def tiles_of(slot, index):
        return pl.ds(pl.multiple_of(slot * length + index * TILE, TILE), TILE)

    row_in_tile = lax.broadcasted_iota(jnp.int32, (TILE, width), 0)

    def shift_down(value, carry):
        return jnp.where(row_in_tile == 0, carry, pltpu.roll(value, 1, 0))

    def shift_up(value, carry):
        return jnp.where(row_in_tile == TILE - 1, carry, pltpu.roll(value, TILE - 1, 0))

    steps_in_slot = length // TILE

    def matmul(left, panel, how, use, left_columns=None):
        def step(index, carry):
            columns = pl.ds(pl.multiple_of(index * MATMUL_WIDE, MATMUL_WIDE), MATMUL_WIDE)
            right = panel[:, columns] if how is NN else panel[columns, :]
            source = left[...] if left_columns is None else left[:, left_columns]
            use(columns, dot(source, right, how))
            return carry

        lax.fori_loop(0, width // MATMUL_WIDE, step, 0)

    def counts(slot, shape, offset):
        at = lax.broadcasted_iota(jnp.int32, shape, 0) + offset
        earlier = jnp.minimum(at, filled_here[slot]).astype(F32)
        upto = jnp.minimum(at + 1, filled_here[slot]).astype(F32)
        return earlier, upto, at < filled_here[slot]

    def tall_mask(columns):
        at = lax.broadcasted_iota(jnp.int32, (rows, columns), 0)
        inside = at < filled_here[0]
        for slot in range(1, slots):
            shifted = at - slot * length
            inside = inside | ((shifted >= 0) & (shifted < filled_here[slot]))
        return inside

    edges_out, edges_in = held["edges_out"], held["edges_in"]
    edges_out[...] = jnp.zeros_like(edges_out)
    for slot in range(slots):
        last = tokens[slot * length + length - 16 : slot * length + length, :].astype(F32)
        edges_out[0, slot : slot + 1, :] = last[15:, :]
    pl.semaphore_wait(barrier, greeted)
    edge_copy = copies.start(edges_out.at[0], edges_in.at[0], after)

    gain_mix, bias_mix = inputs["gain_mix"], inputs["bias_mix"]
    keep_edge = jnp.where(ch_at > 0, 1.0, 0.0)
    keep_next = jnp.where(ch_at < ch_size - 1, 1.0, 0.0)

    mixes = [inputs["mix_key"], inputs["mix_value"], inputs["mix_recept"]]
    both_mix = [held["both_key"], held["both_value"], held["both_recept"]]

    def last_row_before(slot, index):
        return pl.ds(pl.multiple_of(slot * length + index * TILE - 16, 16), 16)

    def mix_tile(slot, index, carry):
        spot = tiles_of(slot, index)
        unit, _ = normalize(tokens[spot, :].astype(F32))
        normed = unit * gain_mix[...] + bias_mix[...]
        earlier = shift_down(normed, carry)
        for weights, target in zip(mixes, both_mix):
            target[spot, :] = blend(normed, earlier, weights[...]).astype(BF16)

    def mix_carry(slot, index):
        unit, _ = normalize(tokens[last_row_before(slot, index), :].astype(F32))
        return (unit * gain_mix[...] + bias_mix[...])[15:, :]

    for slot in range(slots):

        def mix_step(index, carry, slot=slot):
            mix_tile(slot, index, mix_carry(slot, index))
            return carry

        lax.fori_loop(1, steps_in_slot, mix_step, 0)
    edge_copy.wait()
    edge_unit, _ = normalize(edges_in[0])
    edges_in[0] = (edge_unit * gain_mix[...] + bias_mix[...]) * keep_edge
    for slot in range(slots):
        mix_tile(slot, 0, edges_in[0, slot : slot + 1, :])
    exchanges = {}
    for name in ("key", "value", "recept"):
        ref = held["both_" + name]
        exchanges[name] = [
            copies.start(ref.at[pl.ds(0, rows), :], ref.at[pl.ds(rows, rows), :], partner)
        ]

    key_ref, value_ref = held["key"], held["value"]
    wide = {
        name: held["wide_" + name]
        for name in ("middle", "total", "sigmoid", "num", "den", "unit", "gap")
    }

    def own(name):
        return held["both_" + name].at[pl.ds(0, rows), :]

    def store_key(columns, product):
        key_ref[:, columns] = product.astype(BF16)

    def store_value(columns, product):
        value_ref[:, columns] = product.astype(BF16)

    matmul(own("key"), panels.take(), NN, store_key)
    panels.release()
    matmul(own("value"), panels.take(), NN, store_value)
    panels.release()

    time_decay, time_first = inputs["time_decay"], inputs["time_first"]
    square = (length, 3 * length)
    at_row = lax.broadcasted_iota(jnp.int32, square, 0)
    at_column = lax.rem(lax.broadcasted_iota(jnp.int32, square, 1), length)
    lower = jnp.where(at_column < at_row, 1.0, 0.0).astype(BF16)
    upper = jnp.where(at_column > at_row, 1.0, 0.0).astype(BF16)

    def triangle(matrix, value):
        high = value.astype(BF16)
        rest = value - high.astype(F32)
        middle = rest.astype(BF16)
        low = (rest - middle.astype(F32)).astype(BF16)
        return dot(matrix, jnp.concatenate([high, middle, low], axis=0), NN)

    sums_out, sums_in = held["sums_out"], held["sums_in"]
    sums_out[...] = jnp.zeros_like(sums_out)
    for slot in range(slots):

        def local_step(index, carry, slot=slot):
            columns = pl.ds(pl.multiple_of(index * WIDE, WIDE), WIDE)
            spot = pl.ds(slot * length, length)
            rate = jnp.exp(time_decay[:, columns])
            earlier, upto, filled = counts(slot, (length, WIDE), 0)
            stop = rate * filled_here[slot].astype(F32)
            keys = key_ref[spot, columns].astype(F32)
            weight = jnp.where(filled, jnp.exp(rate * upto - stop) * jnp.exp(keys), 0.0)
            payload = weight * value_ref[spot, columns].astype(F32)
            raised = jnp.exp(stop - rate * earlier)
            wide["num"][spot, columns] = raised * triangle(lower, payload)
            wide["den"][spot, columns] = raised * triangle(lower, weight)
            sums_out[0, slot : slot + 1, columns] = jnp.sum(payload, axis=0, keepdims=True)
            at = slots + slot
            sums_out[0, at : at + 1, columns] = jnp.sum(weight, axis=0, keepdims=True)
            return carry

        lax.fori_loop(0, width // WIDE, local_step, 0)

    def share(which):
        return [
            copies.start(
                sums_out.at[which],
                sums_in.at[which, step - 1],
                (seq_at, lax.rem(ch_at + step, ch_size)),
            )
            for step in range(1, ch_size)
        ]

    sum_copies = share(0)

    def store_sigmoid(columns, product):
        wide["sigmoid"][:, columns] = jax.nn.sigmoid(product)

    matmul(own("recept"), panels.take(), NN, store_sigmoid)
    panels.release()
    for copy in sum_copies:
        copy.wait()

    rate_row = jnp.exp(time_decay[...])
    states, finals = held["states"], held["finals"]
    states[...] = jnp.zeros_like(states)
    finals[...] = jnp.zeros_like(finals)
    for slot in range(slots):
        size = lengths[slot]
        reached = jnp.minimum(size, ch_at * length)
        for pair, initial in enumerate((inputs["init_num"], inputs["init_den"])):
            at = pair * slots + slot
            start_row = initial[slot : slot + 1, :]
            state = jnp.exp(-rate_row * reached.astype(F32)) * start_row
            final = jnp.exp(-rate_row * size.astype(F32)) * start_row
            for step in range(ch_size):
                source = lax.rem(ch_at + ch_size - step, ch_size)
                done = jnp.minimum(size, (source + 1) * length)
                term = (
                    sums_out[0, at : at + 1, :]
                    if step == 0
                    else sums_in[0, step - 1, at : at + 1, :]
                )
                final = final + jnp.exp(-rate_row * (size - done).astype(F32)) * term
                if step:
                    gone = jnp.maximum(reached - done, 0).astype(F32)
                    state = state + jnp.where(source < ch_at, jnp.exp(-rate_row * gone) * term, 0.0)
            states[at : at + 1, :] = state
            finals[at : at + 1, :] = final
    own_columns = pl.ds(pl.multiple_of(ch_at * plan.narrow, plan.narrow), plan.narrow)
    outputs["final"][...] = finals[:, own_columns]

    both_output = held["both_output"]
    for slot in range(slots):

        def wkv_step(index, carry, slot=slot):
            spot = tiles_of(slot, index)
            earlier, _, _ = counts(slot, (TILE, width), index * TILE)
            faded = jnp.exp(-rate_row * earlier)
            num = wide["num"][spot, :] + faded * states[slot : slot + 1, :]
            den = wide["den"][spot, :] + faded * states[slots + slot : slots + slot + 1, :]
            wide["num"][spot, :] = num
            wide["den"][spot, :] = den
            bonus = jnp.exp(time_first[...] + key_ref[spot, :].astype(F32))
            wkv = (num + bonus * value_ref[spot, :].astype(F32)) / (den + bonus)
            sent = wkv.astype(BF16).astype(F32)
            both_output[spot, :] = (wide["sigmoid"][spot, :] * sent).astype(BF16)
            return carry

        lax.fori_loop(0, steps_in_slot, wkv_step, 0)
    exchanges["output"] = [
        copies.start(
            both_output.at[pl.ds(0, rows), :], both_output.at[pl.ds(rows, rows), :], partner
        )
    ]

    def store_middle(columns, product):
        wide["middle"][:, columns] = tokens[:, columns].astype(F32) + product

    matmul(own("output"), panels.take(), NN, store_middle)
    panels.release()

    gain_ffn, bias_ffn = inputs["gain_ffn"], inputs["bias_ffn"]
    factor_ffn = held["factor_ffn"]
    for slot in range(slots):
        last = wide["middle"][slot * length + length - 8 : slot * length + length, :]
        unit, _ = normalize(last)
        edges_out[1, slot : slot + 1, :] = (unit * gain_ffn[...] + bias_ffn[...])[7:, :]
    edge_copy = copies.start(edges_out.at[1], edges_in.at[1], after)

    def unit_step(index, carry):
        spot = pl.ds(pl.multiple_of(index * TILE, TILE), TILE)
        unit, factor = normalize(wide["middle"][spot, :])
        wide["unit"][spot, :] = unit
        factor_ffn[spot, :] = jnp.broadcast_to(factor, (TILE, 128))
        return carry

    lax.fori_loop(0, rows // TILE, unit_step, 0)
    blends = [inputs["blend_key"], inputs["blend_gate"]]
    both_blend = [held["both_expand"], held["both_gate"]]

    def blend_tile(slot, index, carry):
        spot = tiles_of(slot, index)
        normed = wide["unit"][spot, :] * gain_ffn[...] + bias_ffn[...]
        earlier = shift_down(normed, carry)
        wide["gap"][spot, :] = normed - earlier
        for weights, target in zip(blends, both_blend):
            target[spot, :] = blend(normed, earlier, weights[...]).astype(BF16)

    for slot in range(slots):

        def blend_step(index, carry, slot=slot):
            last = wide["unit"][last_row_before(slot, index), :][15:, :]
            blend_tile(slot, index, last * gain_ffn[...] + bias_ffn[...])
            return carry

        lax.fori_loop(1, steps_in_slot, blend_step, 0)
    edge_copy.wait()
    for slot in range(slots):
        blend_tile(slot, 0, edges_in[1, slot : slot + 1, :] * keep_edge)
    for name in ("expand", "gate"):
        ref = held["both_" + name]
        exchanges[name] = [
            copies.start(ref.at[pl.ds(0, rows), :], ref.at[pl.ds(rows, rows), :], partner)
        ]

    both_hidden = held["both_hidden"]
    exchanges["hidden"] = []
    for index in range(panel_count):

        def store_hidden(columns, product, index=index):
            positive = jnp.maximum(product, 0.0)
            start = pl.multiple_of(columns.start + index * width, MATMUL_WIDE)
            both_hidden[first_rows, pl.ds(start, MATMUL_WIDE)] = (positive * positive).astype(BF16)

        matmul(own("expand"), panels.take(), NN, store_hidden)
        panels.release()
        part = pl.ds(index * width, width)
        exchanges["hidden"].append(
            copies.start(
                both_hidden.at[pl.ds(0, rows), part],
                both_hidden.at[pl.ds(rows, rows), part],
                partner,
            )
        )

        def add_contracted(columns, product, index=index):
            if index:
                product = product + wide["total"][:, columns]
            wide["total"][:, columns] = product

        matmul(both_hidden.at[pl.ds(0, rows), part], panels.take(), NN, add_contracted)
        panels.release()

    grad_contracted, grad_logit = held["rows_0"], held["rows_1"]

    def finish_forward(columns, product):
        gate = jax.nn.sigmoid(product)
        contracted = wide["total"][:, columns]
        inside = tall_mask(MATMUL_WIDE)
        mixed = wide["middle"][:, columns] + gate * contracted
        outputs["mixed_out"][:, columns] = jnp.where(inside, mixed, 0.0).astype(BF16)
        grad = jnp.where(inside, grad_out[:, columns].astype(F32), 0.0)
        grad_contracted[:, columns] = (grad * gate).astype(BF16)
        grad_logit[:, columns] = (grad * contracted * gate * (1.0 - gate)).astype(BF16)

    matmul(own("gate"), panels.take(), NN, finish_forward)
    panels.release()

    def hand_over(name, source):
        target = held["back_" + name]
        part = plan.narrow
        exchanges["back_" + name] = []
        for x_at in range(sizes["x"]):
            theirs = pl.multiple_of((x_at * 2 + 1 - place["k"]) * part, part)
            mine = pl.multiple_of((x_at * 2 + place["k"]) * part, part)
            spot = pl.ds(x_at * part, part)
            exchanges["back_" + name].append(
                copies.start(
                    source.at[:, pl.ds(theirs, part)],
                    target.at[pl.ds(rows, rows), spot],
                    partner,
                )
            )
            target[first_rows, spot] = source[:, pl.ds(mine, part)]

    def settle(*wanted):
        for name in wanted:
            for copy in exchanges.pop(name):
                copy.wait()

    grad_expanded, their_expanded = held["grad_expanded"], held["their_expanded"]

    def maker(piece):
        name, short_name, height, row_cut, breadth, column_cut = piece
        first = plan.orders[short_name][0]
        left = held["both_" + ("hidden" if name == "contract" else name)]
        row_step = plan.tall if name == "contract" else plan.short
        if name == "expand":
            rights = (
                (
                    first_rows,
                    grad_expanded,
                    lambda at: (at * 2 + place["k"]) * plan.broad + column_cut,
                ),
                (last_rows, their_expanded, lambda at: at * plan.broad + column_cut),
            )
        else:
            rights = ((slice(None), held["back_" + name], lambda at: at * plan.narrow),)

        def along(axis, coordinate):
            return [coordinate] if axis == first else range(sizes[axis])

        def make(coordinate, emit):
            places = [(l, y) for l in along("l", coordinate) for y in along("y", coordinate)]
            columns = along("x", coordinate)

            def step(h, carry):
                starts = [((h * 2 + l) * 2 + y) * row_step + row_cut for l, y in places]
                spans = [(start, height) for start in starts]
                if row_step == height and first in "xl":
                    spans = [(starts[0], len(starts) * height)]
                value = None
                for part, right, column_of in rights:
                    a = [
                        left[part, pl.ds(pl.multiple_of(start, math.gcd(span, 512)), span)]
                        for start, span in spans
                    ]
                    b = [
                        right[:, pl.ds(pl.multiple_of(column_of(x), breadth), breadth)]
                        for x in columns
                    ]
                    a = jnp.concatenate(a, axis=1) if len(a) > 1 else a[0]
                    b = jnp.concatenate(b, axis=1) if len(b) > 1 else b[0]
                    product = dot(a, b, TN)
                    value = product if value is None else value + product
                for index, (l, y) in enumerate(places):
                    rows_of = value[index * height : (index + 1) * height, :]
                    for x in columns:
                        at = 0 if first == "x" else x
                        block = rows_of[:, at * breadth : (at + 1) * breadth]
                        where = {"h": h, "l": l, "y": y, "x": x}
                        emit(tuple(where[a] for a in AXES if a != first), block)
                return carry

            lax.fori_loop(0, sizes["h"], step, 0)

        return make

    pieces = {}
    for piece in plan.pieces:
        name, short_name, height, row_cut, breadth, column_cut = piece
        order_of = plan.orders[short_name]
        out_ref = outputs["grad_" + name].at[
            pl.ds(row_cut, height), pl.ds(column_cut, breadth)
        ]
        landings = [held["landing_" + short_name + str(stage)] for stage in range(len(order_of))]
        pieces[short_name] = Piece(
            maker(piece),
            order_of,
            sizes,
            place,
            copies,
            held["held_" + short_name],
            landings,
            out_ref,
        )

    def start_pieces(prefix):
        for short_name, piece in pieces.items():
            if short_name.startswith(prefix):
                piece.start()

    vector_in = held["vector_in"]
    vector_parts = held["vector_parts"]
    span = plan.vector_span
    scattered = span < width
    vector_queue = {"left": list("kxs" if scattered else "kxylh"), "open": [], "slot": 0}

    def part_of(index):
        return vectors.at[:, pl.ds(pl.multiple_of(index * span, span), span)]

    def start_vectors():
        axis = vector_queue["left"].pop(0)
        if axis == "s":
            for step in range(1, plan.seq):
                there = lax.rem(seq_at + step, plan.seq)
                target = vector_parts.at[step - 1]
                copy = copies.start(part_of(there), target, (there, ch_at))
                vector_queue["open"].append((copy, None))
            return
        for step in range(1, sizes[axis]):
            there = device_at(moved(place, sizes, axis, step))
            copy = copies.start(vectors, vector_in.at[vector_queue["slot"]], there)
            vector_queue["open"].append((copy, vector_queue["slot"]))
            vector_queue["slot"] += 1

    def pump_vectors():
        found, vector_queue["open"] = vector_queue["open"], []
        for copy, _ in found:
            copy.wait()
        for _, slot in found:
            if slot is not None:
                vectors[...] += vector_in[slot]
        if vector_queue["left"]:
            start_vectors()
        elif found:
            total = part_of(seq_at)[...] if scattered else vectors[...]
            for step in range(plan.seq - 1 if scattered else 0):
                total = total + vector_parts[step]
            outputs["vectors"][...] = total

    def pump(point, finish_mix=None):
        for short_name in PUMPS[point]:
            if short_name == "!":
                finish_mix()
                continue
            if short_name == "*":
                pump_vectors()
                continue
            piece = pieces.get(short_name)
            if piece is not None and piece.copies:
                piece.advance()

    hand_over("contract", grad_contracted)
    hand_over("gate", grad_logit)
    settle("hidden", "back_contract")
    start_pieces("c")

    for index in range(panel_count):

        def store_expanded(columns, product, index=index):
            start = pl.multiple_of(columns.start + index * width, MATMUL_WIDE)
            spot = pl.ds(start, MATMUL_WIDE)
            positive = jnp.sqrt(both_hidden[first_rows, spot].astype(F32))
            grad_expanded[:, spot] = (product * 2.0 * positive).astype(BF16)

        matmul(grad_contracted, panels.take(), NT, store_expanded)
        panels.release()
    pump(0)
    exchanges["expanded"] = []
    for x_at in range(sizes["x"]):
        theirs = pl.multiple_of((x_at * 2 + 1 - place["k"]) * plan.broad, plan.broad)
        exchanges["expanded"].append(
            copies.start(
                grad_expanded.at[:, pl.ds(theirs, plan.broad)],
                their_expanded.at[:, pl.ds(x_at * plan.broad, plan.broad)],
                partner,
            )
        )
    for index in range(panel_count):

        def add_expand(columns, product, index=index):
            if index:
                product = product + wide["total"][:, columns]
            wide["total"][:, columns] = product

        matmul(
            grad_expanded,
            panels.take(),
            NT,
            add_expand,
            left_columns=pl.ds(index * width, width),
        )
        panels.release()

    def store_gate(columns, product):
        wide["middle"][:, columns] = product

    matmul(grad_logit, panels.take(), NT, store_gate)
    panels.release()

    for slot in range(slots):
        spot = slice(slot * length, slot * length + 8)
        edge = wide["total"][spot, :] * (1.0 - blends[0][...])
        edge = edge + wide["middle"][spot, :] * (1.0 - blends[1][...])
        edges_out[2, slot : slot + 1, :] = edge[:1, :]
    edge_copy = copies.start(edges_out.at[2], edges_in.at[2], before)
    settle("expand", "expanded")
    start_pieces("e")
    settle("gate", "back_gate")
    start_pieces("g")
    pump(1)
    grad_branch = held["rows_2"]

    def first_row_after(slot, index):
        return pl.ds(pl.multiple_of(slot * length + (index + 1) * TILE, 8), 8)

    def ffn_back_earlier(spot):
        earlier = wide["total"][spot, :] * (1.0 - blends[0][...])
        return earlier + wide["middle"][spot, :] * (1.0 - blends[1][...])

    def ffn_back_tile(slot, index, carry):
        spot = tiles_of(slot, index)
        in_expand, in_gate = wide["total"][spot, :], wide["middle"][spot, :]
        gap = wide["gap"][spot, :]
        unit = wide["unit"][spot, :]
        add_vector("blend_key", in_expand * gap)
        add_vector("blend_gate", in_gate * gap)
        earlier = ffn_back_earlier(spot)
        grad_normed = in_expand * blends[0][...] + in_gate * blends[1][...]
        grad_normed = grad_normed + shift_up(earlier, carry)
        add_vector("gain_ffn", grad_normed * unit)
        add_vector("bias_ffn", grad_normed)
        scaled = grad_normed * gain_ffn[...]
        centered = scaled - jnp.mean(scaled, axis=-1, keepdims=True)
        centered = centered - unit * jnp.mean(scaled * unit, axis=-1, keepdims=True)
        _, _, filled = counts(slot, (TILE, width), index * TILE)
        grad = jnp.where(filled, grad_out[spot, :].astype(F32), 0.0)
        grad = grad + factor_ffn[spot, :1] * centered
        wide["total"][spot, :] = grad
        grad_branch[spot, :] = grad.astype(BF16)

    for slot in range(slots):

        def ffn_back_step(index, carry, slot=slot):
            ffn_back_tile(slot, index, ffn_back_earlier(first_row_after(slot, index))[:1, :])
            return carry

        lax.fori_loop(0, steps_in_slot - 1, ffn_back_step, 0)
    edge_copy.wait()
    for slot in range(slots):
        ffn_back_tile(slot, steps_in_slot - 1, edges_in[2, slot : slot + 1, :] * keep_next)

    hand_over("output", grad_branch)
    pump(2)
    grad_recept = held["rows_3"]

    def gated_back(columns, product):
        gate = wide["sigmoid"][:, columns]
        bonus = jnp.exp(time_first[:, columns] + key_ref[:, columns].astype(F32))
        norm = wide["den"][:, columns] + bonus
        wkv = (wide["num"][:, columns] + bonus * value_ref[:, columns].astype(F32)) / norm
        sent = wkv.astype(BF16).astype(F32)
        grad_wkv = (product * gate).astype(BF16).astype(F32)
        grad_recept[:, columns] = (product * sent * gate * (1.0 - gate)).astype(BF16)
        upper_part = grad_wkv / norm
        wide["middle"][:, columns] = upper_part
        wide["gap"][:, columns] = -upper_part * wkv

    matmul(grad_branch, panels.take(), NT, gated_back)
    panels.release()
    hand_over("recept", grad_recept)
    pump(3)

    for slot in range(slots):

        def adjoint_step(index, carry, slot=slot):
            columns = pl.ds(pl.multiple_of(index * WIDE, WIDE), WIDE)
            spot = pl.ds(slot * length, length)
            rate = jnp.exp(time_decay[:, columns])
            earlier, upto, _ = counts(slot, (length, WIDE), 0)
            faded = jnp.exp(-rate * earlier)
            raised = jnp.exp(rate * upto)
            for pair, (source, target) in enumerate((("middle", "sigmoid"), ("gap", "unit"))):
                terms = faded * wide[source][spot, columns]
                wide[target][spot, columns] = raised * triangle(upper, terms)
                at = pair * slots + slot
                sums_out[1, at : at + 1, columns] = jnp.sum(terms, axis=0, keepdims=True)
            return carry

        lax.fori_loop(0, width // WIDE, adjoint_step, 0)
    sum_copies = share(1)
    settle("output", "back_output")
    start_pieces("o")
    settle("recept", "back_recept")
    start_pieces("r")
    pump(4)
    for copy in sum_copies:
        copy.wait()
    later = held["later"]
    later[...] = jnp.zeros_like(later)
    for slot in range(slots):
        size = lengths[slot]
        done = jnp.minimum(size, (ch_at + 1) * length)
        for pair in range(2):
            at = pair * slots + slot
            total = jnp.zeros((1, width), F32)
            for step in range(1, ch_size):
                source = lax.rem(ch_at + ch_size - step, ch_size)
                reached = jnp.minimum(size, source * length)
                gone = jnp.maximum(reached - done, 0).astype(F32)
                term = sums_in[1, step - 1, at : at + 1, :]
                total = total + jnp.where(source > ch_at, jnp.exp(-rate_row * gone) * term, 0.0)
            later[at : at + 1, :] = total

    grad_key, grad_value = held["rows_0"], held["rows_1"]
    for slot in range(slots):

        def wkv_back_step(index, carry, slot=slot):
            spot = tiles_of(slot, index)
            _, upto, filled = counts(slot, (TILE, width), index * TILE)
            left = filled_here[slot].astype(F32) - upto
            faded = jnp.exp(-rate_row * left)
            adj_num = wide["sigmoid"][spot, :] + faded * later[slot : slot + 1, :]
            adj_den = wide["unit"][spot, :] + faded * later[slots + slot : slots + slot + 1, :]
            keys, values = key_ref[spot, :].astype(F32), value_ref[spot, :].astype(F32)
            bonus = jnp.exp(time_first[...] + keys)
            weight = jnp.where(filled, jnp.exp(keys), 0.0)
            upper_part, lower_part = wide["middle"][spot, :], wide["gap"][spot, :]
            direct = (upper_part * values + lower_part) * bonus
            grad_value[spot, :] = (upper_part * bonus + weight * adj_num).astype(BF16)
            grad_key[spot, :] = (direct + weight * (adj_num * values + adj_den)).astype(BF16)
            add_vector("time_first", direct)
            decay = adj_num * wide["num"][spot, :] + adj_den * wide["den"][spot, :]
            add_vector("time_decay", jnp.where(filled, decay, 0.0))
            return carry

        lax.fori_loop(0, steps_in_slot, wkv_back_step, 0)
    decay_at = VECTORS.index("time_decay")
    vectors[decay_at : decay_at + 1, :] *= -rate_row * jnp.exp(-rate_row)

    hand_over("key", grad_key)
    hand_over("value", grad_value)
    pump(5)

    def keeper(name):
        def keep(columns, product):
            wide[name][:, columns] = product

        return keep

    for source, name in ((grad_key, "sigmoid"), (grad_value, "unit"), (grad_recept, "gap")):
        matmul(source, panels.take(), NT, keeper(name))
        panels.release()
    in_names = ("sigmoid", "unit", "gap")
    for slot in range(slots):
        spot = slice(slot * length, slot * length + 8)
        edge = jnp.zeros((8, width), F32)
        for name, weights in zip(in_names, mixes):
            edge = edge + wide[name][spot, :] * (1.0 - weights[...])
        edges_out[3, slot : slot + 1, :] = edge[:1, :]
    edge_copy = copies.start(edges_out.at[3], edges_in.at[3], before)
    for name in ("key", "value"):
        settle(name, "back_" + name)
        start_pieces(name[0])
    pump(6)

    in_carry = [edges_in[0, slot : slot + 1, :] for slot in range(slots)]
    vector_names = ("mix_key", "mix_value", "mix_recept")

    def mix_back_earlier(spot):
        earlier = wide[in_names[0]][spot, :] * (1.0 - mixes[0][...])
        for name, weights in zip(in_names[1:], mixes[1:]):
            earlier = earlier + wide[name][spot, :] * (1.0 - weights[...])
        return earlier

    def mix_back_tile(slot, index, before_row, after_row):
        spot = tiles_of(slot, index)
        unit, factor = normalize(tokens[spot, :].astype(F32))
        normed = unit * gain_mix[...] + bias_mix[...]
        gap = normed - shift_down(normed, before_row)
        grad_normed = shift_up(mix_back_earlier(spot), after_row)
        for name, weights, vector in zip(in_names, mixes, vector_names):
            grad = wide[name][spot, :]
            add_vector(vector, grad * gap)
            grad_normed = grad_normed + grad * weights[...]
        add_vector("gain_mix", grad_normed * unit)
        add_vector("bias_mix", grad_normed)
        scaled = grad_normed * gain_mix[...]
        centered = scaled - jnp.mean(scaled, axis=-1, keepdims=True)
        centered = centered - unit * jnp.mean(scaled * unit, axis=-1, keepdims=True)
        grad = wide["total"][spot, :] + factor * centered
        outputs["grad_tokens"][spot, :] = grad.astype(BF16)

    def next_row(slot, index):
        return mix_back_earlier(first_row_after(slot, index))[:1, :]

    last_tile = steps_in_slot - 1
    for slot in range(slots):

        def mix_back_step(index, carry, slot=slot):
            mix_back_tile(slot, index, mix_carry(slot, index), next_row(slot, index))
            return carry

        lax.fori_loop(1, last_tile, mix_back_step, 0)
        if last_tile:
            mix_back_tile(slot, 0, in_carry[slot], next_row(slot, 0))
    def finish_mix():
        edge_copy.wait()
        for slot in range(slots):
            after_row = edges_in[3, slot : slot + 1, :] * keep_next
            before_row = mix_carry(slot, last_tile) if last_tile else in_carry[slot]
            mix_back_tile(slot, last_tile, before_row, after_row)
        start_vectors()

    pump(7, finish_mix)
    while any(piece.copies for piece in pieces.values()):
        for piece in pieces.values():
            if piece.copies:
                piece.advance()
    while vector_queue["open"]:
        pump_vectors()


def place_outputs(plan, *refs):
    count = len(OUTPUTS)
    for source, target in zip(refs[: count - 1], refs[count:]):
        target[...] = source[...]
    part = plan.width // (plan.seq * plan.ch)
    at = lax.axis_index("ch") * part
    span = plan.vector_span
    if span == plan.width:
        at = at + lax.axis_index("seq") * plan.short
    turned = pltpu.roll(refs[count - 1][...], lax.rem(span - at, span), 1)
    for index, target in enumerate(refs[2 * count - 1 :]):
        target[...] = turned[index : index + 1, :part]


def body(*arguments):
    values = dict(zip(INPUTS, arguments))
    plan = Plan(values["tokens"], values["w_expand"])
    rows, width = plan.rows, plan.width
    operands, specs = [], []
    for name in INPUTS:
        value = values[name]
        space = pltpu.VMEM
        if name in ("tokens", "grad_out"):
            value = value.reshape(rows, width)
        elif name == "lengths":
            space = pltpu.SMEM
        elif name.startswith("w_"):
            space = pl.ANY
        elif value.ndim == 1:
            value = value.reshape(1, width)
        operands.append(value)
        specs.append(pl.BlockSpec(memory_space=space))
    outs = {
        "mixed_out": ((rows, width), BF16),
        "grad_tokens": ((rows, width), BF16),
        "final": ((8, plan.narrow), F32),
        "grad_key": ((plan.short, plan.narrow), F32),
        "grad_value": ((plan.short, plan.narrow), F32),
        "grad_recept": ((plan.short, plan.narrow), F32),
        "grad_output": ((plan.short, plan.narrow), F32),
        "grad_expand": ((plan.short, plan.broad), F32),
        "grad_contract": ((plan.tall, plan.narrow), F32),
        "grad_gate": ((plan.short, plan.narrow), F32),
        "vectors": ((16, plan.vector_span), F32),
    }
    results = pl.pallas_call(
        functools.partial(layer_kernel, plan),
        out_shape=[jax.ShapeDtypeStruct(*outs[name]) for name in OUTPUTS],
        in_specs=specs,
        out_specs=[pl.BlockSpec(memory_space=pltpu.VMEM)] * len(OUTPUTS),
        scratch_shapes=list(plan.shapes.values()),
        compiler_params=pltpu.CompilerParams(
            collective_id=0, has_side_effects=True, vmem_limit_bytes=63 * 2**20
        ),
    )(*operands)
    part = width // (plan.seq * plan.ch)
    shapes = [outs[name] for name in OUTPUTS[:-1]] + [((1, part), F32)] * len(VECTORS)
    results = pl.pallas_call(
        functools.partial(place_outputs, plan),
        out_shape=[jax.ShapeDtypeStruct(*shape) for shape in shapes],
        in_specs=[pl.BlockSpec(memory_space=pltpu.VMEM)] * len(OUTPUTS),
        out_specs=[pl.BlockSpec(memory_space=pltpu.VMEM)] * len(shapes),
    )(*results)
    got = dict(zip(OUTPUTS[:-1], results))
    vectors = results[len(OUTPUTS) - 1 :]
    shape = values["tokens"].shape
    slots = plan.slots
    return (
        got["mixed_out"].reshape(shape),
        got["grad_tokens"].reshape(shape),
        got["final"][:slots],
        got["final"][slots : 2 * slots],
        got["grad_key"],
        got["grad_value"],
        got["grad_recept"],
        got["grad_output"],
        got["grad_expand"],
        got["grad_contract"],
        got["grad_gate"],
    ) + tuple(vector.reshape(part) for vector in vectors)


def solution(mesh):
    split, copied = P("seq", "ch", None), P()
    placed = (split, split, P("seq"), P("seq", None), P("seq", None)) + (copied,) * 18
    both = P("seq", "ch")
    return jax.shard_map(
        body,
        mesh=mesh,
        in_specs=placed,
        out_specs=(split, split) + (both,) * 9 + (P(("seq", "ch")),) * 11,
        check_vma=False,
    )
```

```python
import functools
import math

import jax
import jax.numpy as jnp
from jax import lax
from jax.experimental import pallas as pl
from jax.experimental.pallas import tpu as pltpu
from jax.sharding import PartitionSpec as P

EPS = 1e-05
MESH = pl.DeviceIdType.MESH
AXES = "hlyx"
F32 = jnp.float32
BF16 = jnp.bfloat16
TILE = 64
WIDE = 256
MATMUL_WIDE = 512
SLOTS_OF_WEIGHTS = 3

ORDERS = {
    "c0": "ylhx",
    "c1": "lyxh",
    "c2": "yxlh",
    "c3": "xylh",
    "e0": "lyh",
    "e1": "lyh",
    "e2": "ylh",
    "e3": "ylh",
    "g": "lyxh",
    "o": "xylh",
    "k": "xylh",
    "v": "xylh",
    "r": "yxlh",
}
PUMPS = (
    (),
    (
        "c0", "c1",
    ),
    (
        "c3", "E0", "c2", "g",
    ),
    (),
    (
        "E1", "c1",
    ),
    (
        "c0", "c2", "c3",
    ),
    (
        "e0", "E2", "g", "e1",
    ),
    (
        "E3", "c0", "c2", "r", "c3", "e0", "c2", "o", "c3", "c1", "!", "e2", "e0", "*", "e1", "c1",
        "e2", "e3", "e1", "k", "e2", "o", "e3", "o", "k", "e3", "v", "o", "g", "c0", "k", "v", "g",
        "r", "k", "*", "v", "r", "*", "v", "r",
    ),
)

NN = (((1,), (0,)), ((), ()))
NT = (((1,), (1,)), ((), ()))
TN = (((0,), (0,)), ((), ()))


def dot(left, right, how):
    return lax.dot_general(left, right, how, preferred_element_type=F32)


def axis_sizes():
    seq_size, ch_size = lax.axis_size("seq"), lax.axis_size("ch")
    return {"k": 2, "x": ch_size // 2, "y": 2, "l": 2, "h": seq_size // 4}


def coordinates():
    seq_at, ch_at = lax.axis_index("seq"), lax.axis_index("ch")
    return {
        "h": seq_at // 4,
        "l": seq_at // 2 % 2,
        "y": seq_at % 2,
        "x": ch_at // 2,
        "k": ch_at % 2,
    }


def device_at(place):
    return (place["h"] * 4 + place["l"] * 2 + place["y"], place["x"] * 2 + place["k"])


def moved(place, sizes, axis, step):
    return {**place, axis: lax.rem(place[axis] + step, sizes[axis])}


class Copies:
    def __init__(self, sends, receives):
        self.sends, self.receives, self.used = sends, receives, 0
        self.open = []

    def start(self, source, target, device):
        copy = pltpu.make_async_remote_copy(
            src_ref=source,
            dst_ref=target,
            send_sem=self.sends.at[self.used],
            recv_sem=self.receives.at[self.used],
            device_id=device,
            device_id_type=MESH,
        )
        self.used += 1
        copy.start()
        return copy


class Piece:
    def __init__(self, make, order, sizes, place, copies, held, landings, out_ref):
        self.make, self.order, self.sizes, self.place = make, order, sizes, place
        self.remote, self.held, self.landings, self.out_ref = copies, held, landings, out_ref
        self.axes = [axis for axis in AXES if axis in order]
        self.stage = 0
        self.copies = []

    def start(self):
        axis = self.order[self.stage]
        at = self.axes.index(axis)
        for step in range(1, self.sizes[axis]):
            there = moved(self.place, self.sizes, axis, step)
            if self.stage == 0:

                def keep(where, value, slot=step - 1):
                    self.held[(slot,) + where] = value.astype(BF16)

                self.make(there[axis], keep)
                source = self.held.at[step - 1]
            else:
                source = self.landings[self.stage - 1].at[
                    (0,) + (slice(None),) * at + (there[axis],)
                ]
            self.copies.append(
                self.remote.start(
                    source, self.landings[self.stage].at[step - 1], device_at(there)
                )
            )

    def finish(self):
        axis = self.order[self.stage]
        at = self.axes.index(axis)
        landing = self.landings[self.stage]
        others = self.sizes[axis] - 1
        for copy in self.copies:
            copy.wait()
        self.copies = []
        remaining = [a for a in self.axes if a != axis]
        if self.stage == 0:

            def add(where, value):
                for other in range(others):
                    value = value + landing[(other,) + where].astype(F32)
                landing[(0,) + where] = value.astype(BF16)

            self.make(self.place[axis], add)
        else:
            own = self.landings[self.stage - 1].at[
                (0,) + (slice(None),) * at + (self.place[axis],)
            ]
            lead = tuple(self.sizes[a] for a in remaining)
            rows, columns = landing.shape[-2:]
            tile = math.gcd(rows, max(16, 32768 // columns))
            parts = rows // tile

            def add_tile(index, carry):
                part, rest = index % parts, index // parts
                where = ()
                for size in reversed(lead):
                    where = (rest % size,) + where
                    rest = rest // size
                spot = pl.ds(pl.multiple_of(part * tile, tile), tile)
                where = where + (spot, slice(None))
                total = own[where].astype(F32)
                for other in range(others):
                    total = total + landing[(other,) + where].astype(F32)
                if remaining:
                    landing[(0,) + where] = total.astype(BF16)
                else:
                    self.out_ref[where] = total
                return carry

            lax.fori_loop(0, math.prod(lead) * parts, add_tile, 0)
        self.axes = remaining
        self.stage += 1

    def advance(self):
        self.finish()
        if self.axes:
            self.start()


class Plan:
    def __init__(self, tokens, w_expand):
        self.slots, self.length, self.width = tokens.shape
        self.hidden = w_expand.shape[1]
        self.sizes = sizes = axis_sizes()
        self.seq, self.ch = sizes["h"] * 4, sizes["x"] * 2
        self.rows = self.slots * self.length
        rows, width, hidden = self.rows, self.width, self.hidden
        self.narrow = width // self.ch
        self.broad = hidden // self.ch
        self.short = width // self.seq
        self.tall = hidden // self.seq
        self.vector_span = self.short if self.short % 128 == 0 else width
        half = sizes["x"] * self.narrow
        self.pieces = []
        cuts = 4 if (self.tall // 4) % 128 == 0 else 1
        part = self.tall // cuts
        for cut in range(cuts):
            self.pieces.append(("contract", "c" + str(cut), part, cut * part, self.narrow, 0))
        cuts = 4 if (self.broad // 4) % 128 == 0 else 1
        self.expand_cuts = cuts
        part = self.broad // cuts
        for cut in range(cuts):
            self.pieces.append(("expand", "e" + str(cut), self.short, 0, part, cut * part))
        for name in ("gate", "output", "key", "value", "recept"):
            self.pieces.append((name, name[0], self.short, 0, self.narrow, 0))
        self.orders = {}
        for name, short_name, height, _, _, _ in self.pieces:
            if height % 128 == 0:
                self.orders[short_name] = ORDERS[short_name]
            else:
                self.orders[short_name] = "hly" if name == "expand" else "xylh"
        vmem = pltpu.VMEM
        shapes = {
            "panels": vmem((SLOTS_OF_WEIGHTS, width, width), BF16),
            "both_hidden": vmem((2 * rows, hidden), BF16),
            "grad_expanded": vmem((rows, hidden), BF16),
            "their_expanded": vmem(((self.ch - 1) * rows, self.broad), BF16),
            "both_expand": vmem((self.ch * rows, width), BF16),
            "key": vmem((rows, width), BF16),
            "value": vmem((rows, width), BF16),
            "edges_out": vmem((4, 8, width), F32),
            "edges_in": vmem((4, 8, width), F32),
            "sums_out": vmem((2, 8, width), F32),
            "sums_in": vmem((2, self.ch - 1, 8, width), F32),
            "states": vmem((8, width), F32),
            "finals": vmem((8, width), F32),
            "later": vmem((8, width), F32),
            "factor_ffn": vmem((rows, 128), F32),
            "vectors": vmem((16, width), F32),
            "vector_in": vmem((self.count_vector_slots(), 16, width), F32),
            "vector_parts": vmem((self.seq - 1, 16, self.vector_span), F32),
        }
        for name in ("gate", "output", "key", "value", "recept"):
            shapes["both_" + name] = vmem((2 * rows, width), BF16)
        for name in ("contract", "gate", "output", "key", "value", "recept"):
            shapes["back_" + name] = vmem((2 * rows, half), BF16)
        for index in range(4):
            shapes["rows_" + str(index)] = vmem((rows, width), BF16)
        for name in ("middle", "total", "sigmoid", "num", "den", "unit", "gap"):
            shapes["wide_" + name] = vmem((rows, width), F32)
        copies = 64 + 16 * self.ch
        for name, short_name, height, _, breadth, _ in self.pieces:
            order = self.orders[short_name]
            axes = [axis for axis in AXES if axis in order[1:]]
            lead = tuple(sizes[a] for a in axes)
            shapes["held_" + short_name] = vmem(
                (sizes[order[0]] - 1,) + lead + (height, breadth), BF16
            )
            axes = [axis for axis in AXES if axis in order]
            for stage, axis in enumerate(order):
                axes.remove(axis)
                shape = (sizes[axis] - 1,) + tuple(sizes[a] for a in axes) + (height, breadth)
                shapes["landing_" + short_name + str(stage)] = vmem(shape, BF16)
                copies += sizes[axis] - 1
        copies += self.count_vector_slots() + self.seq
        shapes["sends"] = pltpu.SemaphoreType.DMA((copies,))
        shapes["receives"] = pltpu.SemaphoreType.DMA((copies,))
        shapes["panel_sems"] = pltpu.SemaphoreType.DMA((SLOTS_OF_WEIGHTS,))
        self.shapes = shapes

    def count_vector_slots(self):
        axes = "kx" if self.vector_span < self.width else "kxylh"
        return sum(self.sizes[axis] - 1 for axis in axes)


INPUTS = (
    "tokens",
    "grad_out",
    "lengths",
    "init_num",
    "init_den",
    "w_key",
    "w_value",
    "w_recept",
    "w_output",
    "w_expand",
    "w_contract",
    "w_gate",
    "gain_mix",
    "bias_mix",
    "gain_ffn",
    "bias_ffn",
    "mix_key",
    "mix_value",
    "mix_recept",
    "blend_key",
    "blend_gate",
    "time_decay",
    "time_first",
)
OUTPUTS = (
    "mixed_out",
    "grad_tokens",
    "final",
    "grad_key",
    "grad_value",
    "grad_recept",
    "grad_output",
    "grad_expand",
    "grad_contract",
    "grad_gate",
    "vectors",
)
VECTORS = (
    "gain_mix",
    "bias_mix",
    "gain_ffn",
    "bias_ffn",
    "mix_key",
    "mix_value",
    "mix_recept",
    "blend_key",
    "blend_gate",
    "time_decay",
    "time_first",
)


class Panels:
    def __init__(self, sources, ref, sems):
        self.sources, self.ref, self.sems = sources, ref, sems
        self.used = 0
        for index in range(min(SLOTS_OF_WEIGHTS, len(sources))):
            self.copy(index).start()

    def copy(self, index):
        slot = index % SLOTS_OF_WEIGHTS
        return pltpu.make_async_copy(self.sources[index], self.ref.at[slot], self.sems.at[slot])

    def take(self):
        self.copy(self.used).wait()
        return self.ref.at[self.used % SLOTS_OF_WEIGHTS]

    def release(self):
        index = self.used + SLOTS_OF_WEIGHTS
        if index < len(self.sources):
            self.copy(index).start()
        self.used += 1


def layer_kernel(plan, *all_refs):
    inputs = dict(zip(INPUTS, all_refs))
    outputs = dict(zip(OUTPUTS, all_refs[len(INPUTS) :]))
    held = dict(zip(plan.shapes, all_refs[len(INPUTS) + len(OUTPUTS) :]))
    sizes = plan.sizes
    place = coordinates()
    ch_at = lax.axis_index("ch")
    seq_at = lax.axis_index("seq")
    slots, length, width, rows = plan.slots, plan.length, plan.width, plan.rows
    hidden, ch_size = plan.hidden, plan.ch
    panel_count = hidden // width
    tokens, grad_out, lengths = inputs["tokens"], inputs["grad_out"], inputs["lengths"]
    first_rows = slice(0, rows)
    last_rows = slice(rows, 2 * rows)

    w_expand, w_contract = inputs["w_expand"], inputs["w_contract"]

    def expand_panel(index):
        return w_expand.at[:, pl.ds(index * width, width)]

    def contract_panel(index):
        return w_contract.at[pl.ds(index * width, width), :]

    order = [inputs["w_key"], inputs["w_value"], inputs["w_recept"], inputs["w_output"]]
    for index in range(panel_count):
        order += [expand_panel(index), contract_panel(index)]
    order += [inputs["w_gate"]]
    order += [contract_panel(index) for index in range(panel_count)]
    order += [expand_panel(index) for index in range(panel_count)]
    order += [inputs["w_gate"], inputs["w_output"]]
    order += [inputs["w_key"], inputs["w_value"], inputs["w_recept"]]
    panels = Panels(order, held["panels"], held["panel_sems"])

    barrier = pltpu.get_barrier_semaphore()
    greeted = 0
    for step in range(1, ch_size):
        pl.semaphore_signal(
            barrier,
            inc=1,
            device_id=(seq_at, lax.rem(ch_at + step, ch_size)),
            device_id_type=MESH,
        )
        greeted += 1
    for step in range(1, plan.seq):
        pl.semaphore_signal(
            barrier,
            inc=1,
            device_id=(lax.rem(seq_at + step, plan.seq), ch_at),
            device_id_type=MESH,
        )
        greeted += 1
    copies = Copies(held["sends"], held["receives"])
    partner = device_at({**place, "k": 1 - place["k"]})
    after = (seq_at, lax.rem(ch_at + 1, ch_size))
    before = (seq_at, lax.rem(ch_at + ch_size - 1, ch_size))

    filled_here = [
        jnp.clip(lengths[slot] - ch_at * length, 0, length) for slot in range(slots)
    ]
    vectors = held["vectors"]
    vectors[...] = jnp.zeros_like(vectors)

    def add_vector(name, value):
        at = VECTORS.index(name)
        vectors[at : at + 1, :] += jnp.sum(value, axis=0, keepdims=True)

    def normalize(value):
        center = value - jnp.mean(value, axis=-1, keepdims=True)
        factor = lax.rsqrt(jnp.mean(center * center, axis=-1, keepdims=True) + EPS)
        return center * factor, factor

    def blend(current, earlier, weights):
        return current * weights + earlier * (1.0 - weights)

    def tiles_of(slot, index):
        return pl.ds(pl.multiple_of(slot * length + index * TILE, TILE), TILE)

    row_in_tile = lax.broadcasted_iota(jnp.int32, (TILE, width), 0)

    def shift_down(value, carry):
        return jnp.where(row_in_tile == 0, carry, pltpu.roll(value, 1, 0))

    def shift_up(value, carry):
        return jnp.where(row_in_tile == TILE - 1, carry, pltpu.roll(value, TILE - 1, 0))

    steps_in_slot = length // TILE

    def matmul(left, panel, how, use, left_columns=None):
        def step(index, carry):
            columns = pl.ds(pl.multiple_of(index * MATMUL_WIDE, MATMUL_WIDE), MATMUL_WIDE)
            right = panel[:, columns] if how is NN else panel[columns, :]
            source = left[...] if left_columns is None else left[:, left_columns]
            use(columns, dot(source, right, how))
            return carry

        lax.fori_loop(0, width // MATMUL_WIDE, step, 0)

    def counts(slot, shape, offset):
        at = lax.broadcasted_iota(jnp.int32, shape, 0) + offset
        earlier = jnp.minimum(at, filled_here[slot]).astype(F32)
        upto = jnp.minimum(at + 1, filled_here[slot]).astype(F32)
        return earlier, upto, at < filled_here[slot]

    def tall_mask(columns):
        at = lax.broadcasted_iota(jnp.int32, (rows, columns), 0)
        inside = at < filled_here[0]
        for slot in range(1, slots):
            shifted = at - slot * length
            inside = inside | ((shifted >= 0) & (shifted < filled_here[slot]))
        return inside

    edges_out, edges_in = held["edges_out"], held["edges_in"]
    edges_out[...] = jnp.zeros_like(edges_out)
    for slot in range(slots):
        last = tokens[slot * length + length - 16 : slot * length + length, :].astype(F32)
        edges_out[0, slot : slot + 1, :] = last[15:, :]
    pl.semaphore_wait(barrier, greeted)
    edge_copy = copies.start(edges_out.at[0], edges_in.at[0], after)

    gain_mix, bias_mix = inputs["gain_mix"], inputs["bias_mix"]
    keep_edge = jnp.where(ch_at > 0, 1.0, 0.0)
    keep_next = jnp.where(ch_at < ch_size - 1, 1.0, 0.0)

    mixes = [inputs["mix_key"], inputs["mix_value"], inputs["mix_recept"]]
    both_mix = [held["both_key"], held["both_value"], held["both_recept"]]

    def last_row_before(slot, index):
        return pl.ds(pl.multiple_of(slot * length + index * TILE - 16, 16), 16)

    def mix_tile(slot, index, carry):
        spot = tiles_of(slot, index)
        unit, _ = normalize(tokens[spot, :].astype(F32))
        normed = unit * gain_mix[...] + bias_mix[...]
        earlier = shift_down(normed, carry)
        for weights, target in zip(mixes, both_mix):
            target[spot, :] = blend(normed, earlier, weights[...]).astype(BF16)

    def mix_carry(slot, index):
        unit, _ = normalize(tokens[last_row_before(slot, index), :].astype(F32))
        return (unit * gain_mix[...] + bias_mix[...])[15:, :]

    for slot in range(slots):

        def mix_step(index, carry, slot=slot):
            mix_tile(slot, index, mix_carry(slot, index))
            return carry

        lax.fori_loop(1, steps_in_slot, mix_step, 0)
    edge_copy.wait()
    edge_unit, _ = normalize(edges_in[0])
    edges_in[0] = (edge_unit * gain_mix[...] + bias_mix[...]) * keep_edge
    for slot in range(slots):
        mix_tile(slot, 0, edges_in[0, slot : slot + 1, :])
    exchanges = {}
    for name in ("key", "value", "recept"):
        ref = held["both_" + name]
        exchanges[name] = [
            copies.start(ref.at[pl.ds(0, rows), :], ref.at[pl.ds(rows, rows), :], partner)
        ]

    key_ref, value_ref = held["key"], held["value"]
    wide = {
        name: held["wide_" + name]
        for name in ("middle", "total", "sigmoid", "num", "den", "unit", "gap")
    }

    def own(name):
        return held["both_" + name].at[pl.ds(0, rows), :]

    def store_key(columns, product):
        key_ref[:, columns] = product.astype(BF16)

    def store_value(columns, product):
        value_ref[:, columns] = product.astype(BF16)

    matmul(own("key"), panels.take(), NN, store_key)
    panels.release()
    matmul(own("value"), panels.take(), NN, store_value)
    panels.release()

    time_decay, time_first = inputs["time_decay"], inputs["time_first"]
    square = (length, 3 * length)
    at_row = lax.broadcasted_iota(jnp.int32, square, 0)
    at_column = lax.rem(lax.broadcasted_iota(jnp.int32, square, 1), length)
    lower = jnp.where(at_column < at_row, 1.0, 0.0).astype(BF16)
    upper = jnp.where(at_column > at_row, 1.0, 0.0).astype(BF16)

    def triangle(matrix, value):
        high = value.astype(BF16)
        rest = value - high.astype(F32)
        middle = rest.astype(BF16)
        low = (rest - middle.astype(F32)).astype(BF16)
        return dot(matrix, jnp.concatenate([high, middle, low], axis=0), NN)

    sums_out, sums_in = held["sums_out"], held["sums_in"]
    sums_out[...] = jnp.zeros_like(sums_out)
    for slot in range(slots):

        def local_step(index, carry, slot=slot):
            columns = pl.ds(pl.multiple_of(index * WIDE, WIDE), WIDE)
            spot = pl.ds(slot * length, length)
            rate = jnp.exp(time_decay[:, columns])
            earlier, upto, filled = counts(slot, (length, WIDE), 0)
            stop = rate * filled_here[slot].astype(F32)
            keys = key_ref[spot, columns].astype(F32)
            weight = jnp.where(filled, jnp.exp(rate * upto - stop) * jnp.exp(keys), 0.0)
            payload = weight * value_ref[spot, columns].astype(F32)
            raised = jnp.exp(stop - rate * earlier)
            wide["num"][spot, columns] = raised * triangle(lower, payload)
            wide["den"][spot, columns] = raised * triangle(lower, weight)
            sums_out[0, slot : slot + 1, columns] = jnp.sum(payload, axis=0, keepdims=True)
            at = slots + slot
            sums_out[0, at : at + 1, columns] = jnp.sum(weight, axis=0, keepdims=True)
            return carry

        lax.fori_loop(0, width // WIDE, local_step, 0)

    def share(which):
        return [
            copies.start(
                sums_out.at[which],
                sums_in.at[which, step - 1],
                (seq_at, lax.rem(ch_at + step, ch_size)),
            )
            for step in range(1, ch_size)
        ]

    sum_copies = share(0)

    def store_sigmoid(columns, product):
        wide["sigmoid"][:, columns] = jax.nn.sigmoid(product)

    matmul(own("recept"), panels.take(), NN, store_sigmoid)
    panels.release()
    for copy in sum_copies:
        copy.wait()

    rate_row = jnp.exp(time_decay[...])
    states, finals = held["states"], held["finals"]
    states[...] = jnp.zeros_like(states)
    finals[...] = jnp.zeros_like(finals)
    for slot in range(slots):
        size = lengths[slot]
        reached = jnp.minimum(size, ch_at * length)
        for pair, initial in enumerate((inputs["init_num"], inputs["init_den"])):
            at = pair * slots + slot
            start_row = initial[slot : slot + 1, :]
            state = jnp.exp(-rate_row * reached.astype(F32)) * start_row
            final = jnp.exp(-rate_row * size.astype(F32)) * start_row
            for step in range(ch_size):
                source = lax.rem(ch_at + ch_size - step, ch_size)
                done = jnp.minimum(size, (source + 1) * length)
                term = (
                    sums_out[0, at : at + 1, :]
                    if step == 0
                    else sums_in[0, step - 1, at : at + 1, :]
                )
                final = final + jnp.exp(-rate_row * (size - done).astype(F32)) * term
                if step:
                    gone = jnp.maximum(reached - done, 0).astype(F32)
                    state = state + jnp.where(source < ch_at, jnp.exp(-rate_row * gone) * term, 0.0)
            states[at : at + 1, :] = state
            finals[at : at + 1, :] = final
    own_columns = pl.ds(pl.multiple_of(ch_at * plan.narrow, plan.narrow), plan.narrow)
    outputs["final"][...] = finals[:, own_columns]

    both_output = held["both_output"]
    for slot in range(slots):

        def wkv_step(index, carry, slot=slot):
            spot = tiles_of(slot, index)
            earlier, _, _ = counts(slot, (TILE, width), index * TILE)
            faded = jnp.exp(-rate_row * earlier)
            num = wide["num"][spot, :] + faded * states[slot : slot + 1, :]
            den = wide["den"][spot, :] + faded * states[slots + slot : slots + slot + 1, :]
            wide["num"][spot, :] = num
            wide["den"][spot, :] = den
            bonus = jnp.exp(time_first[...] + key_ref[spot, :].astype(F32))
            wkv = (num + bonus * value_ref[spot, :].astype(F32)) / (den + bonus)
            sent = wkv.astype(BF16).astype(F32)
            both_output[spot, :] = (wide["sigmoid"][spot, :] * sent).astype(BF16)
            return carry

        lax.fori_loop(0, steps_in_slot, wkv_step, 0)
    exchanges["output"] = [
        copies.start(
            both_output.at[pl.ds(0, rows), :], both_output.at[pl.ds(rows, rows), :], partner
        )
    ]

    def store_middle(columns, product):
        wide["middle"][:, columns] = tokens[:, columns].astype(F32) + product

    matmul(own("output"), panels.take(), NN, store_middle)
    panels.release()

    gain_ffn, bias_ffn = inputs["gain_ffn"], inputs["bias_ffn"]
    factor_ffn = held["factor_ffn"]
    for slot in range(slots):
        last = wide["middle"][slot * length + length - 8 : slot * length + length, :]
        unit, _ = normalize(last)
        edges_out[1, slot : slot + 1, :] = (unit * gain_ffn[...] + bias_ffn[...])[7:, :]
    edge_copy = copies.start(edges_out.at[1], edges_in.at[1], after)

    def unit_step(index, carry):
        spot = pl.ds(pl.multiple_of(index * TILE, TILE), TILE)
        unit, factor = normalize(wide["middle"][spot, :])
        wide["unit"][spot, :] = unit
        factor_ffn[spot, :] = jnp.broadcast_to(factor, (TILE, 128))
        return carry

    lax.fori_loop(0, rows // TILE, unit_step, 0)
    blends = [inputs["blend_key"], inputs["blend_gate"]]
    both_blend = [held["both_expand"], held["both_gate"]]

    def blend_tile(slot, index, carry):
        spot = tiles_of(slot, index)
        normed = wide["unit"][spot, :] * gain_ffn[...] + bias_ffn[...]
        earlier = shift_down(normed, carry)
        wide["gap"][spot, :] = normed - earlier
        for weights, target in zip(blends, both_blend):
            target[spot, :] = blend(normed, earlier, weights[...]).astype(BF16)

    for slot in range(slots):

        def blend_step(index, carry, slot=slot):
            last = wide["unit"][last_row_before(slot, index), :][15:, :]
            blend_tile(slot, index, last * gain_ffn[...] + bias_ffn[...])
            return carry

        lax.fori_loop(1, steps_in_slot, blend_step, 0)
    edge_copy.wait()
    for slot in range(slots):
        blend_tile(slot, 0, edges_in[1, slot : slot + 1, :] * keep_edge)
    both_expand, both_gate = held["both_expand"], held["both_gate"]

    def block_of(ref, index):
        return ref.at[pl.ds(index * rows, rows), :]

    exchanges["expand"] = [
        copies.start(block_of(both_expand, 0), block_of(both_expand, 1), partner)
    ]
    across = []
    for step in range(1, sizes["x"]):
        there = device_at(moved(place, sizes, "x", step))
        across.append(
            copies.start(block_of(both_expand, 0), block_of(both_expand, 2 * step), there)
        )
    exchanges["gate"] = [copies.start(block_of(both_gate, 0), block_of(both_gate, 1), partner)]

    both_hidden = held["both_hidden"]
    exchanges["hidden"] = []
    for index in range(panel_count):

        def store_hidden(columns, product, index=index):
            positive = jnp.maximum(product, 0.0)
            start = pl.multiple_of(columns.start + index * width, MATMUL_WIDE)
            both_hidden[first_rows, pl.ds(start, MATMUL_WIDE)] = (positive * positive).astype(BF16)

        matmul(own("expand"), panels.take(), NN, store_hidden)
        panels.release()
        part = pl.ds(index * width, width)
        exchanges["hidden"].append(
            copies.start(
                both_hidden.at[pl.ds(0, rows), part],
                both_hidden.at[pl.ds(rows, rows), part],
                partner,
            )
        )

        def add_contracted(columns, product, index=index):
            if index:
                product = product + wide["total"][:, columns]
            wide["total"][:, columns] = product

        matmul(both_hidden.at[pl.ds(0, rows), part], panels.take(), NN, add_contracted)
        panels.release()

    grad_contracted, grad_logit = held["rows_0"], held["rows_1"]

    def finish_forward(columns, product):
        gate = jax.nn.sigmoid(product)
        contracted = wide["total"][:, columns]
        inside = tall_mask(MATMUL_WIDE)
        mixed = wide["middle"][:, columns] + gate * contracted
        outputs["mixed_out"][:, columns] = jnp.where(inside, mixed, 0.0).astype(BF16)
        grad = jnp.where(inside, grad_out[:, columns].astype(F32), 0.0)
        grad_contracted[:, columns] = (grad * gate).astype(BF16)
        grad_logit[:, columns] = (grad * contracted * gate * (1.0 - gate)).astype(BF16)

    matmul(own("gate"), panels.take(), NN, finish_forward)
    panels.release()

    def hand_over(name, source):
        target = held["back_" + name]
        part = plan.narrow
        exchanges["back_" + name] = []
        for x_at in range(sizes["x"]):
            theirs = pl.multiple_of((x_at * 2 + 1 - place["k"]) * part, part)
            mine = pl.multiple_of((x_at * 2 + place["k"]) * part, part)
            spot = pl.ds(x_at * part, part)
            exchanges["back_" + name].append(
                copies.start(
                    source.at[:, pl.ds(theirs, part)],
                    target.at[pl.ds(rows, rows), spot],
                    partner,
                )
            )
            target[first_rows, spot] = source[:, pl.ds(mine, part)]

    def settle(*wanted):
        for name in wanted:
            for copy in exchanges.pop(name):
                copy.wait()

    grad_expanded, their_expanded = held["grad_expanded"], held["their_expanded"]

    def maker(piece):
        name, short_name, height, row_cut, breadth, column_cut = piece
        first = plan.orders[short_name][0]
        left = held["both_" + ("hidden" if name == "contract" else name)]
        row_step = plan.tall if name == "contract" else plan.short
        if name == "expand":
            rights = (
                (first_rows, grad_expanded, lambda at: ch_at * plan.broad + column_cut),
                (slice(rows, ch_size * rows), their_expanded, lambda at: column_cut),
            )
        else:
            rights = ((slice(None), held["back_" + name], lambda at: at * plan.narrow),)
        kept = [a for a in AXES if a in plan.orders[short_name] and a != first]

        def along(axis, coordinate):
            return [coordinate] if axis == first else range(sizes[axis])

        def make(coordinate, emit):
            places = [(l, y) for l in along("l", coordinate) for y in along("y", coordinate)]
            columns = [0] if name == "expand" else along("x", coordinate)

            def step(h, carry):
                starts = [((h * 2 + l) * 2 + y) * row_step + row_cut for l, y in places]
                spans = [(start, height) for start in starts]
                if row_step == height and first in "xlh":
                    spans = [(starts[0], len(starts) * height)]
                value = None
                for part, right, column_of in rights:
                    a = [
                        left[part, pl.ds(pl.multiple_of(start, math.gcd(span, 512)), span)]
                        for start, span in spans
                    ]
                    b = [
                        right[:, pl.ds(pl.multiple_of(column_of(x), breadth), breadth)]
                        for x in columns
                    ]
                    a = jnp.concatenate(a, axis=1) if len(a) > 1 else a[0]
                    b = jnp.concatenate(b, axis=1) if len(b) > 1 else b[0]
                    product = dot(a, b, TN)
                    value = product if value is None else value + product
                for index, (l, y) in enumerate(places):
                    rows_of = value[index * height : (index + 1) * height, :]
                    for x in columns:
                        at = 0 if first == "x" else x
                        block = rows_of[:, at * breadth : (at + 1) * breadth]
                        where = {"h": h, "l": l, "y": y, "x": x}
                        emit(tuple(where[a] for a in kept), block)
                return carry

            if first == "h":
                step(coordinate, 0)
            else:
                lax.fori_loop(0, sizes["h"], step, 0)

        return make

    pieces = {}
    for piece in plan.pieces:
        name, short_name, height, row_cut, breadth, column_cut = piece
        order_of = plan.orders[short_name]
        out_ref = outputs["grad_" + name].at[
            pl.ds(row_cut, height), pl.ds(column_cut, breadth)
        ]
        landings = [held["landing_" + short_name + str(stage)] for stage in range(len(order_of))]
        pieces[short_name] = Piece(
            maker(piece),
            order_of,
            sizes,
            place,
            copies,
            held["held_" + short_name],
            landings,
            out_ref,
        )

    def start_pieces(prefix):
        for short_name, piece in pieces.items():
            if short_name.startswith(prefix):
                piece.start()

    vector_in = held["vector_in"]
    vector_parts = held["vector_parts"]
    span = plan.vector_span
    scattered = span < width
    vector_queue = {"left": list("kxs" if scattered else "kxylh"), "open": [], "slot": 0}

    def part_of(index):
        return vectors.at[:, pl.ds(pl.multiple_of(index * span, span), span)]

    def start_vectors():
        axis = vector_queue["left"].pop(0)
        if axis == "s":
            for step in range(1, plan.seq):
                there = lax.rem(seq_at + step, plan.seq)
                target = vector_parts.at[step - 1]
                copy = copies.start(part_of(there), target, (there, ch_at))
                vector_queue["open"].append((copy, None))
            return
        for step in range(1, sizes[axis]):
            there = device_at(moved(place, sizes, axis, step))
            copy = copies.start(vectors, vector_in.at[vector_queue["slot"]], there)
            vector_queue["open"].append((copy, vector_queue["slot"]))
            vector_queue["slot"] += 1

    def pump_vectors():
        found, vector_queue["open"] = vector_queue["open"], []
        for copy, _ in found:
            copy.wait()
        for _, slot in found:
            if slot is not None:
                vectors[...] += vector_in[slot]
        if vector_queue["left"]:
            start_vectors()
        elif found:
            total = part_of(seq_at)[...] if scattered else vectors[...]
            for step in range(plan.seq - 1 if scattered else 0):
                total = total + vector_parts[step]
            outputs["vectors"][...] = total

    def pump(point, finish_mix=None):
        for short_name in PUMPS[point]:
            if short_name == "!":
                finish_mix()
                continue
            if short_name[0] == "E":
                if short_name in exchanges:
                    start_expand(int(short_name[1:]))
                continue
            if short_name == "*":
                pump_vectors()
                continue
            piece = pieces.get(short_name)
            if piece is not None and piece.copies:
                piece.advance()

    hand_over("contract", grad_contracted)
    hand_over("gate", grad_logit)
    settle("hidden", "back_contract")
    start_pieces("c")

    for index in range(panel_count):

        def store_expanded(columns, product, index=index):
            start = pl.multiple_of(columns.start + index * width, MATMUL_WIDE)
            spot = pl.ds(start, MATMUL_WIDE)
            positive = jnp.sqrt(both_hidden[first_rows, spot].astype(F32))
            grad_expanded[:, spot] = (product * 2.0 * positive).astype(BF16)

        matmul(grad_contracted, panels.take(), NT, store_expanded)
        panels.release()
    for step, copy in enumerate(across, 1):
        copy.wait()
        exchanges["expand"].append(
            copies.start(
                block_of(both_expand, 2 * step), block_of(both_expand, 2 * step + 1), partner
            )
        )

    def send_expanded(cut):
        if cut >= plan.expand_cuts:
            return
        part = plan.broad // plan.expand_cuts
        found = exchanges["E" + str(cut)] = []
        targets = [({**place, "k": 1 - place["k"]}, 0)]
        for step in range(1, sizes["x"]):
            there = moved(place, sizes, "x", step)
            targets.append((there, 2 * step - 1))
            targets.append(({**there, "k": 1 - place["k"]}, 2 * step))
        for there, slot in targets:
            start = (there["x"] * 2 + there["k"]) * plan.broad + cut * part
            found.append(
                copies.start(
                    grad_expanded.at[:, pl.ds(pl.multiple_of(start, part), part)],
                    their_expanded.at[pl.ds(slot * rows, rows), pl.ds(cut * part, part)],
                    device_at(there),
                )
            )

    def start_expand(cut):
        if "expand" in exchanges:
            settle("expand")
        settle("E" + str(cut))
        pieces["e" + str(cut)].start()

    send_expanded(0)
    pump(0)
    for index in range(panel_count):

        def add_expand(columns, product, index=index):
            if index:
                product = product + wide["total"][:, columns]
            wide["total"][:, columns] = product

        matmul(
            grad_expanded,
            panels.take(),
            NT,
            add_expand,
            left_columns=pl.ds(index * width, width),
        )
        panels.release()

    def store_gate(columns, product):
        wide["middle"][:, columns] = product

    matmul(grad_logit, panels.take(), NT, store_gate)
    panels.release()

    for slot in range(slots):
        spot = slice(slot * length, slot * length + 8)
        edge = wide["total"][spot, :] * (1.0 - blends[0][...])
        edge = edge + wide["middle"][spot, :] * (1.0 - blends[1][...])
        edges_out[2, slot : slot + 1, :] = edge[:1, :]
    edge_copy = copies.start(edges_out.at[2], edges_in.at[2], before)
    send_expanded(1)
    settle("gate", "back_gate")
    start_pieces("g")
    pump(1)
    grad_branch = held["rows_2"]

    def first_row_after(slot, index):
        return pl.ds(pl.multiple_of(slot * length + (index + 1) * TILE, 8), 8)

    def ffn_back_earlier(spot):
        earlier = wide["total"][spot, :] * (1.0 - blends[0][...])
        return earlier + wide["middle"][spot, :] * (1.0 - blends[1][...])

    def ffn_back_tile(slot, index, carry):
        spot = tiles_of(slot, index)
        in_expand, in_gate = wide["total"][spot, :], wide["middle"][spot, :]
        gap = wide["gap"][spot, :]
        unit = wide["unit"][spot, :]
        add_vector("blend_key", in_expand * gap)
        add_vector("blend_gate", in_gate * gap)
        earlier = ffn_back_earlier(spot)
        grad_normed = in_expand * blends[0][...] + in_gate * blends[1][...]
        grad_normed = grad_normed + shift_up(earlier, carry)
        add_vector("gain_ffn", grad_normed * unit)
        add_vector("bias_ffn", grad_normed)
        scaled = grad_normed * gain_ffn[...]
        centered = scaled - jnp.mean(scaled, axis=-1, keepdims=True)
        centered = centered - unit * jnp.mean(scaled * unit, axis=-1, keepdims=True)
        _, _, filled = counts(slot, (TILE, width), index * TILE)
        grad = jnp.where(filled, grad_out[spot, :].astype(F32), 0.0)
        grad = grad + factor_ffn[spot, :1] * centered
        wide["total"][spot, :] = grad
        grad_branch[spot, :] = grad.astype(BF16)

    for slot in range(slots):

        def ffn_back_step(index, carry, slot=slot):
            ffn_back_tile(slot, index, ffn_back_earlier(first_row_after(slot, index))[:1, :])
            return carry

        lax.fori_loop(0, steps_in_slot - 1, ffn_back_step, 0)
    edge_copy.wait()
    for slot in range(slots):
        ffn_back_tile(slot, steps_in_slot - 1, edges_in[2, slot : slot + 1, :] * keep_next)

    hand_over("output", grad_branch)
    pump(2)
    grad_recept = held["rows_3"]

    def gated_back(columns, product):
        gate = wide["sigmoid"][:, columns]
        bonus = jnp.exp(time_first[:, columns] + key_ref[:, columns].astype(F32))
        norm = wide["den"][:, columns] + bonus
        wkv = (wide["num"][:, columns] + bonus * value_ref[:, columns].astype(F32)) / norm
        sent = wkv.astype(BF16).astype(F32)
        grad_wkv = (product * gate).astype(BF16).astype(F32)
        grad_recept[:, columns] = (product * sent * gate * (1.0 - gate)).astype(BF16)
        upper_part = grad_wkv / norm
        wide["middle"][:, columns] = upper_part
        wide["gap"][:, columns] = -upper_part * wkv

    matmul(grad_branch, panels.take(), NT, gated_back)
    panels.release()
    hand_over("recept", grad_recept)
    pump(3)

    for slot in range(slots):

        def adjoint_step(index, carry, slot=slot):
            columns = pl.ds(pl.multiple_of(index * WIDE, WIDE), WIDE)
            spot = pl.ds(slot * length, length)
            rate = jnp.exp(time_decay[:, columns])
            earlier, upto, _ = counts(slot, (length, WIDE), 0)
            faded = jnp.exp(-rate * earlier)
            raised = jnp.exp(rate * upto)
            for pair, (source, target) in enumerate((("middle", "sigmoid"), ("gap", "unit"))):
                terms = faded * wide[source][spot, columns]
                wide[target][spot, columns] = raised * triangle(upper, terms)
                at = pair * slots + slot
                sums_out[1, at : at + 1, columns] = jnp.sum(terms, axis=0, keepdims=True)
            return carry

        lax.fori_loop(0, width // WIDE, adjoint_step, 0)
    sum_copies = share(1)
    send_expanded(2)
    send_expanded(3)
    settle("output", "back_output")
    start_pieces("o")
    settle("recept", "back_recept")
    start_pieces("r")
    pump(4)
    for copy in sum_copies:
        copy.wait()
    later = held["later"]
    later[...] = jnp.zeros_like(later)
    for slot in range(slots):
        size = lengths[slot]
        done = jnp.minimum(size, (ch_at + 1) * length)
        for pair in range(2):
            at = pair * slots + slot
            total = jnp.zeros((1, width), F32)
            for step in range(1, ch_size):
                source = lax.rem(ch_at + ch_size - step, ch_size)
                reached = jnp.minimum(size, source * length)
                gone = jnp.maximum(reached - done, 0).astype(F32)
                term = sums_in[1, step - 1, at : at + 1, :]
                total = total + jnp.where(source > ch_at, jnp.exp(-rate_row * gone) * term, 0.0)
            later[at : at + 1, :] = total

    grad_key, grad_value = held["rows_0"], held["rows_1"]
    for slot in range(slots):

        def wkv_back_step(index, carry, slot=slot):
            spot = tiles_of(slot, index)
            _, upto, filled = counts(slot, (TILE, width), index * TILE)
            left = filled_here[slot].astype(F32) - upto
            faded = jnp.exp(-rate_row * left)
            adj_num = wide["sigmoid"][spot, :] + faded * later[slot : slot + 1, :]
            adj_den = wide["unit"][spot, :] + faded * later[slots + slot : slots + slot + 1, :]
            keys, values = key_ref[spot, :].astype(F32), value_ref[spot, :].astype(F32)
            bonus = jnp.exp(time_first[...] + keys)
            weight = jnp.where(filled, jnp.exp(keys), 0.0)
            upper_part, lower_part = wide["middle"][spot, :], wide["gap"][spot, :]
            direct = (upper_part * values + lower_part) * bonus
            grad_value[spot, :] = (upper_part * bonus + weight * adj_num).astype(BF16)
            grad_key[spot, :] = (direct + weight * (adj_num * values + adj_den)).astype(BF16)
            add_vector("time_first", direct)
            decay = adj_num * wide["num"][spot, :] + adj_den * wide["den"][spot, :]
            add_vector("time_decay", jnp.where(filled, decay, 0.0))
            return carry

        lax.fori_loop(0, steps_in_slot, wkv_back_step, 0)
    decay_at = VECTORS.index("time_decay")
    vectors[decay_at : decay_at + 1, :] *= -rate_row * jnp.exp(-rate_row)

    hand_over("key", grad_key)
    hand_over("value", grad_value)
    pump(5)

    def keeper(name):
        def keep(columns, product):
            wide[name][:, columns] = product

        return keep

    for source, name in ((grad_key, "sigmoid"), (grad_value, "unit"), (grad_recept, "gap")):
        matmul(source, panels.take(), NT, keeper(name))
        panels.release()
    in_names = ("sigmoid", "unit", "gap")
    for slot in range(slots):
        spot = slice(slot * length, slot * length + 8)
        edge = jnp.zeros((8, width), F32)
        for name, weights in zip(in_names, mixes):
            edge = edge + wide[name][spot, :] * (1.0 - weights[...])
        edges_out[3, slot : slot + 1, :] = edge[:1, :]
    edge_copy = copies.start(edges_out.at[3], edges_in.at[3], before)
    for name in ("key", "value"):
        settle(name, "back_" + name)
        start_pieces(name[0])
    pump(6)

    in_carry = [edges_in[0, slot : slot + 1, :] for slot in range(slots)]
    vector_names = ("mix_key", "mix_value", "mix_recept")

    def mix_back_earlier(spot):
        earlier = wide[in_names[0]][spot, :] * (1.0 - mixes[0][...])
        for name, weights in zip(in_names[1:], mixes[1:]):
            earlier = earlier + wide[name][spot, :] * (1.0 - weights[...])
        return earlier

    def mix_back_tile(slot, index, before_row, after_row):
        spot = tiles_of(slot, index)
        unit, factor = normalize(tokens[spot, :].astype(F32))
        normed = unit * gain_mix[...] + bias_mix[...]
        gap = normed - shift_down(normed, before_row)
        grad_normed = shift_up(mix_back_earlier(spot), after_row)
        for name, weights, vector in zip(in_names, mixes, vector_names):
            grad = wide[name][spot, :]
            add_vector(vector, grad * gap)
            grad_normed = grad_normed + grad * weights[...]
        add_vector("gain_mix", grad_normed * unit)
        add_vector("bias_mix", grad_normed)
        scaled = grad_normed * gain_mix[...]
        centered = scaled - jnp.mean(scaled, axis=-1, keepdims=True)
        centered = centered - unit * jnp.mean(scaled * unit, axis=-1, keepdims=True)
        grad = wide["total"][spot, :] + factor * centered
        outputs["grad_tokens"][spot, :] = grad.astype(BF16)

    def next_row(slot, index):
        return mix_back_earlier(first_row_after(slot, index))[:1, :]

    last_tile = steps_in_slot - 1
    for slot in range(slots):

        def mix_back_step(index, carry, slot=slot):
            mix_back_tile(slot, index, mix_carry(slot, index), next_row(slot, index))
            return carry

        lax.fori_loop(1, last_tile, mix_back_step, 0)
        if last_tile:
            mix_back_tile(slot, 0, in_carry[slot], next_row(slot, 0))
    def finish_mix():
        edge_copy.wait()
        for slot in range(slots):
            after_row = edges_in[3, slot : slot + 1, :] * keep_next
            before_row = mix_carry(slot, last_tile) if last_tile else in_carry[slot]
            mix_back_tile(slot, last_tile, before_row, after_row)
        start_vectors()

    pump(7, finish_mix)
    for cut in range(plan.expand_cuts):
        if "E" + str(cut) in exchanges:
            start_expand(cut)
    while any(piece.copies for piece in pieces.values()):
        for piece in pieces.values():
            if piece.copies:
                piece.advance()
    while vector_queue["open"]:
        pump_vectors()


LARGE = tuple(name for name in OUTPUTS if name not in ("final", "vectors"))


def place_outputs(plan, *refs):
    count = len(LARGE)
    refs = list(refs)

    def take(number):
        return [refs.pop(0) for _ in range(number)]

    sources, (final, vectors) = take(count), take(2)
    targets, finals, parts = take(count), take(2), take(len(VECTORS))
    buffers, (sems,) = take(count), take(1)
    loads, stores = [], []
    for index in range(count):
        loads.append(pltpu.make_async_copy(sources[index], buffers[index], sems.at[0, index]))
        stores.append(pltpu.make_async_copy(buffers[index], targets[index], sems.at[1, index]))
        loads[-1].start()
    slots = plan.slots
    for index, target in enumerate(finals):
        target[...] = final[index * slots : (index + 1) * slots, :]
    part = plan.width // (plan.seq * plan.ch)
    at = lax.axis_index("ch") * part
    span = plan.vector_span
    if span == plan.width:
        at = at + lax.axis_index("seq") * plan.short
    turned = pltpu.roll(vectors[...], lax.rem(span - at, span), 1)
    for index, target in enumerate(parts):
        target[...] = turned[index, :part]
    for load, store in zip(loads, stores):
        load.wait()
        store.start()
    for store in stores:
        store.wait()


def body(*arguments):
    values = dict(zip(INPUTS, arguments))
    plan = Plan(values["tokens"], values["w_expand"])
    rows, width = plan.rows, plan.width
    operands, specs = [], []
    for name in INPUTS:
        value = values[name]
        space = pltpu.VMEM
        if name in ("tokens", "grad_out"):
            value = value.reshape(rows, width)
        elif name == "lengths":
            space = pltpu.SMEM
        elif name.startswith("w_"):
            space = pl.ANY
        elif value.ndim == 1:
            value = value.reshape(1, width)
        operands.append(value)
        specs.append(pl.BlockSpec(memory_space=space))
    outs = {
        "mixed_out": ((rows, width), BF16),
        "grad_tokens": ((rows, width), BF16),
        "final": ((8, plan.narrow), F32),
        "grad_key": ((plan.short, plan.narrow), F32),
        "grad_value": ((plan.short, plan.narrow), F32),
        "grad_recept": ((plan.short, plan.narrow), F32),
        "grad_output": ((plan.short, plan.narrow), F32),
        "grad_expand": ((plan.short, plan.broad), F32),
        "grad_contract": ((plan.tall, plan.narrow), F32),
        "grad_gate": ((plan.short, plan.narrow), F32),
        "vectors": ((16, plan.vector_span), F32),
    }
    results = pl.pallas_call(
        functools.partial(layer_kernel, plan),
        out_shape=[jax.ShapeDtypeStruct(*outs[name]) for name in OUTPUTS],
        in_specs=specs,
        out_specs=[pl.BlockSpec(memory_space=pltpu.VMEM)] * len(OUTPUTS),
        scratch_shapes=list(plan.shapes.values()),
        compiler_params=pltpu.CompilerParams(
            collective_id=0, has_side_effects=True, vmem_limit_bytes=63 * 2**20
        ),
    )(*operands)
    part = width // (plan.seq * plan.ch)
    slots = plan.slots
    got = dict(zip(OUTPUTS, results))
    vmem, hbm = pl.BlockSpec(memory_space=pltpu.VMEM), pl.BlockSpec(memory_space=pl.ANY)
    shapes = [outs[name] for name in LARGE] + [((slots, plan.narrow), F32)] * 2
    shapes += [((part,), F32)] * len(VECTORS)
    results = pl.pallas_call(
        functools.partial(place_outputs, plan),
        out_shape=[jax.ShapeDtypeStruct(*shape) for shape in shapes],
        in_specs=[hbm] * len(LARGE) + [vmem] * 2,
        out_specs=[hbm] * len(LARGE) + [vmem] * (2 + len(VECTORS)),
        scratch_shapes=[pltpu.VMEM(*outs[name]) for name in LARGE]
        + [pltpu.SemaphoreType.DMA((2, len(LARGE)))],
        compiler_params=pltpu.CompilerParams(vmem_limit_bytes=60 * 2**20),
    )(*[got[name] for name in LARGE], got["final"], got["vectors"])
    mixed_out, grad_tokens, *weights = results[: len(LARGE)]
    shape = values["tokens"].shape
    return (
        mixed_out.reshape(shape),
        grad_tokens.reshape(shape),
        *results[len(LARGE) : len(LARGE) + 2],
        *weights,
        *results[len(LARGE) + 2 :],
    )


def solution(mesh):
    split, copied = P("seq", "ch", None), P()
    placed = (split, split, P("seq"), P("seq", None), P("seq", None)) + (copied,) * 18
    both = P("seq", "ch")
    return jax.shard_map(
        body,
        mesh=mesh,
        in_specs=placed,
        out_specs=(split, split) + (both,) * 9 + (P(("seq", "ch")),) * 11,
        check_vma=False,
    )
```

```python
import functools
import math

import jax
import jax.numpy as jnp
from jax import lax
from jax.experimental import pallas as pl
from jax.experimental.pallas import tpu as pltpu
from jax.sharding import PartitionSpec as P

EPS = 1e-05
MESH = pl.DeviceIdType.MESH
AXES = "hlyx"
F32 = jnp.float32
BF16 = jnp.bfloat16
TILE = 64
WIDE = 512
MATMUL_WIDE = 1024
SLOTS_OF_WEIGHTS = 3

ORDERS = {
    "c0": "lyhx",
    "c1": "lxyh",
    "c2": "yxlh",
    "c3": "ylhx",
    "e0": "ylh",
    "e1": "ylh",
    "e2": "ylh",
    "e3": "ylh",
    "g": "lxyh",
    "o": "xylh",
    "k": "xylh",
    "v": "xylh",
    "r": "ylhx",
}
PUMPS = (
    (),
    (),
    (
        "c2", "E0",
    ),
    (
        "c0", "E1",
    ),
    (),
    (
        "c3", "c2",
    ),
    (
        "e0", "E2",
    ),
    (
        "c1", "g", "c0", "E3", "c3", "e1", "c2", "e0", "o", "!", "c0", "*", "r", "c3", "e1", "c2",
        "e2", "e0", "k", "r", "e3", "e1", "e2", "o", "r", "v", "e3", "e2", "k", "c1", "o", "e3",
        "v", "k", "g", "c1", "c0", "o", "*", "v", "c3", "g", "r", "*", "k", "c1", "v", "g",
    ),
)

NN = (((1,), (0,)), ((), ()))
NT = (((1,), (1,)), ((), ()))
TN = (((0,), (0,)), ((), ()))


def dot(left, right, how):
    return lax.dot_general(left, right, how, preferred_element_type=F32)


def axis_sizes():
    seq_size, ch_size = lax.axis_size("seq"), lax.axis_size("ch")
    return {"k": 2, "x": ch_size // 2, "y": 2, "l": 2, "h": seq_size // 4}


def coordinates():
    seq_at, ch_at = lax.axis_index("seq"), lax.axis_index("ch")
    return {
        "h": seq_at // 4,
        "l": seq_at // 2 % 2,
        "y": seq_at % 2,
        "x": ch_at // 2,
        "k": ch_at % 2,
    }


def device_at(place):
    return (place["h"] * 4 + place["l"] * 2 + place["y"], place["x"] * 2 + place["k"])


def moved(place, sizes, axis, step):
    return {**place, axis: lax.rem(place[axis] + step, sizes[axis])}


class Copies:
    def __init__(self, sends, receives):
        self.sends, self.receives, self.used = sends, receives, 0
        self.open = []

    def start(self, source, target, device):
        copy = pltpu.make_async_remote_copy(
            src_ref=source,
            dst_ref=target,
            send_sem=self.sends.at[self.used],
            recv_sem=self.receives.at[self.used],
            device_id=device,
            device_id_type=MESH,
        )
        self.used += 1
        copy.start()
        return copy


class Piece:
    def __init__(self, make, order, sizes, place, copies, held, landings, out_ref):
        self.make, self.order, self.sizes, self.place = make, order, sizes, place
        self.remote, self.held, self.landings, self.out_ref = copies, held, landings, out_ref
        self.axes = [axis for axis in AXES if axis in order]
        self.stage = 0
        self.copies = []

    def start(self):
        axis = self.order[self.stage]
        at = self.axes.index(axis)
        for step in range(1, self.sizes[axis]):
            there = moved(self.place, self.sizes, axis, step)
            if self.stage == 0:

                def keep(where, value, slot=step - 1):
                    self.held[(slot,) + where] = value.astype(BF16)

                self.make(there[axis], keep)
                source = self.held.at[step - 1]
            else:
                source = self.landings[self.stage - 1].at[
                    (0,) + (slice(None),) * at + (there[axis],)
                ]
            self.copies.append(
                self.remote.start(
                    source, self.landings[self.stage].at[step - 1], device_at(there)
                )
            )

    def finish(self):
        axis = self.order[self.stage]
        at = self.axes.index(axis)
        landing = self.landings[self.stage]
        others = self.sizes[axis] - 1
        for copy in self.copies:
            copy.wait()
        self.copies = []
        remaining = [a for a in self.axes if a != axis]
        if self.stage == 0:

            def add(where, value):
                for other in range(others):
                    value = value + landing[(other,) + where].astype(F32)
                landing[(0,) + where] = value.astype(BF16)

            self.make(self.place[axis], add)
        else:
            own = self.landings[self.stage - 1].at[
                (0,) + (slice(None),) * at + (self.place[axis],)
            ]
            lead = tuple(self.sizes[a] for a in remaining)
            rows, columns = landing.shape[-2:]
            tile = math.gcd(rows, max(16, 32768 // columns))
            parts = rows // tile

            def add_tile(index, carry):
                part, rest = index % parts, index // parts
                where = ()
                for size in reversed(lead):
                    where = (rest % size,) + where
                    rest = rest // size
                spot = pl.ds(pl.multiple_of(part * tile, tile), tile)
                where = where + (spot, slice(None))
                total = own[where].astype(F32)
                for other in range(others):
                    total = total + landing[(other,) + where].astype(F32)
                if remaining:
                    landing[(0,) + where] = total.astype(BF16)
                else:
                    self.out_ref[where] = total
                return carry

            lax.fori_loop(0, math.prod(lead) * parts, add_tile, 0)
        self.axes = remaining
        self.stage += 1

    def advance(self):
        self.finish()
        if self.axes:
            self.start()


class Plan:
    def __init__(self, tokens, w_expand):
        self.slots, self.length, self.width = tokens.shape
        self.hidden = w_expand.shape[1]
        self.sizes = sizes = axis_sizes()
        self.seq, self.ch = sizes["h"] * 4, sizes["x"] * 2
        self.rows = self.slots * self.length
        rows, width, hidden = self.rows, self.width, self.hidden
        self.narrow = width // self.ch
        self.broad = hidden // self.ch
        self.short = width // self.seq
        self.tall = hidden // self.seq
        self.vector_span = self.short if self.short % 128 == 0 else width
        half = sizes["x"] * self.narrow
        self.pieces = []
        cuts = 4 if (self.tall // 4) % 128 == 0 else 1
        part = self.tall // cuts
        for cut in range(cuts):
            self.pieces.append(("contract", "c" + str(cut), part, cut * part, self.narrow, 0))
        cuts = 4 if (self.broad // 4) % 128 == 0 else 1
        self.expand_cuts = cuts
        part = self.broad // cuts
        for cut in range(cuts):
            self.pieces.append(("expand", "e" + str(cut), self.short, 0, part, cut * part))
        for name in ("gate", "output", "key", "value", "recept"):
            self.pieces.append((name, name[0], self.short, 0, self.narrow, 0))
        self.orders = {}
        for name, short_name, height, _, _, _ in self.pieces:
            if height % 128 == 0:
                self.orders[short_name] = ORDERS[short_name]
            else:
                self.orders[short_name] = "hly" if name == "expand" else "xylh"
        vmem = pltpu.VMEM
        shapes = {
            "panels": vmem((SLOTS_OF_WEIGHTS, width, width), BF16),
            "both_hidden": vmem((2 * rows, hidden), BF16),
            "grad_expanded": vmem((rows, hidden), BF16),
            "their_expanded": vmem(((self.ch - 1) * rows, self.broad), BF16),
            "both_expand": vmem((self.ch * rows, width), BF16),
            "key": vmem((rows, width), BF16),
            "value": vmem((rows, width), BF16),
            "edges_out": vmem((4, 8, width), F32),
            "edges_in": vmem((4, 8, width), F32),
            "sums_out": vmem((2, 8, width), F32),
            "sums_in": vmem((2, self.ch - 1, 8, width), F32),
            "states": vmem((8, width), F32),
            "finals": vmem((8, width), F32),
            "later": vmem((8, width), F32),
            "factor_ffn": vmem((rows, 128), F32),
            "vectors": vmem((16, width), F32),
            "vector_in": vmem((self.count_vector_slots(), 16, width), F32),
            "vector_parts": vmem((self.seq - 1, 16, self.vector_span), F32),
        }
        for name in ("gate", "output", "key", "value", "recept"):
            shapes["both_" + name] = vmem((2 * rows, width), BF16)
        for name in ("contract", "gate", "output", "key", "value", "recept"):
            shapes["back_" + name] = vmem((2 * rows, half), BF16)
        for index in range(4):
            shapes["rows_" + str(index)] = vmem((rows, width), BF16)
        for name in ("middle", "total", "sigmoid", "num", "den", "unit", "gap"):
            shapes["wide_" + name] = vmem((rows, width), F32)
        copies = 64 + 16 * self.ch
        for name, short_name, height, _, breadth, _ in self.pieces:
            order = self.orders[short_name]
            axes = [axis for axis in AXES if axis in order[1:]]
            lead = tuple(sizes[a] for a in axes)
            shapes["held_" + short_name] = vmem(
                (sizes[order[0]] - 1,) + lead + (height, breadth), BF16
            )
            axes = [axis for axis in AXES if axis in order]
            for stage, axis in enumerate(order):
                axes.remove(axis)
                shape = (sizes[axis] - 1,) + tuple(sizes[a] for a in axes) + (height, breadth)
                shapes["landing_" + short_name + str(stage)] = vmem(shape, BF16)
                copies += sizes[axis] - 1
        copies += self.count_vector_slots() + self.seq
        shapes["sends"] = pltpu.SemaphoreType.DMA((copies,))
        shapes["receives"] = pltpu.SemaphoreType.DMA((copies,))
        shapes["panel_sems"] = pltpu.SemaphoreType.DMA((SLOTS_OF_WEIGHTS,))
        self.shapes = shapes

    def count_vector_slots(self):
        axes = "kx" if self.vector_span < self.width else "kxylh"
        return sum(self.sizes[axis] - 1 for axis in axes)


INPUTS = (
    "tokens",
    "grad_out",
    "lengths",
    "init_num",
    "init_den",
    "w_key",
    "w_value",
    "w_recept",
    "w_output",
    "w_expand",
    "w_contract",
    "w_gate",
    "gain_mix",
    "bias_mix",
    "gain_ffn",
    "bias_ffn",
    "mix_key",
    "mix_value",
    "mix_recept",
    "blend_key",
    "blend_gate",
    "time_decay",
    "time_first",
)
OUTPUTS = (
    "mixed_out",
    "grad_tokens",
    "final",
    "grad_key",
    "grad_value",
    "grad_recept",
    "grad_output",
    "grad_expand",
    "grad_contract",
    "grad_gate",
    "vectors",
)
VECTORS = (
    "gain_mix",
    "bias_mix",
    "gain_ffn",
    "bias_ffn",
    "mix_key",
    "mix_value",
    "mix_recept",
    "blend_key",
    "blend_gate",
    "time_decay",
    "time_first",
)


class Panels:
    def __init__(self, sources, ref, sems):
        self.sources, self.ref, self.sems = sources, ref, sems
        self.used = 0
        for index in range(min(SLOTS_OF_WEIGHTS, len(sources))):
            self.copy(index).start()

    def copy(self, index):
        slot = index % SLOTS_OF_WEIGHTS
        return pltpu.make_async_copy(self.sources[index], self.ref.at[slot], self.sems.at[slot])

    def take(self):
        self.copy(self.used).wait()
        return self.ref.at[self.used % SLOTS_OF_WEIGHTS]

    def release(self):
        index = self.used + SLOTS_OF_WEIGHTS
        if index < len(self.sources):
            self.copy(index).start()
        self.used += 1


def layer_kernel(plan, *all_refs):
    inputs = dict(zip(INPUTS, all_refs))
    outputs = dict(zip(OUTPUTS, all_refs[len(INPUTS) :]))
    held = dict(zip(plan.shapes, all_refs[len(INPUTS) + len(OUTPUTS) :]))
    sizes = plan.sizes
    place = coordinates()
    ch_at = lax.axis_index("ch")
    seq_at = lax.axis_index("seq")
    slots, length, width, rows = plan.slots, plan.length, plan.width, plan.rows
    hidden, ch_size = plan.hidden, plan.ch
    panel_count = hidden // width
    tokens, grad_out, lengths = inputs["tokens"], inputs["grad_out"], inputs["lengths"]
    first_rows = slice(0, rows)
    last_rows = slice(rows, 2 * rows)

    w_expand, w_contract = inputs["w_expand"], inputs["w_contract"]

    def expand_panel(index):
        return w_expand.at[:, pl.ds(index * width, width)]

    def contract_panel(index):
        return w_contract.at[pl.ds(index * width, width), :]

    order = [inputs["w_key"], inputs["w_value"], inputs["w_recept"], inputs["w_output"]]
    for index in range(panel_count):
        order += [expand_panel(index), contract_panel(index)]
    order += [inputs["w_gate"]]
    order += [contract_panel(index) for index in range(panel_count)]
    order += [expand_panel(index) for index in range(panel_count)]
    order += [inputs["w_gate"], inputs["w_output"]]
    order += [inputs["w_key"], inputs["w_value"], inputs["w_recept"]]
    panels = Panels(order, held["panels"], held["panel_sems"])

    barrier = pltpu.get_barrier_semaphore()
    greeted = 0
    for step in range(1, ch_size):
        pl.semaphore_signal(
            barrier,
            inc=1,
            device_id=(seq_at, lax.rem(ch_at + step, ch_size)),
            device_id_type=MESH,
        )
        greeted += 1
    for step in range(1, plan.seq):
        pl.semaphore_signal(
            barrier,
            inc=1,
            device_id=(lax.rem(seq_at + step, plan.seq), ch_at),
            device_id_type=MESH,
        )
        greeted += 1
    copies = Copies(held["sends"], held["receives"])
    partner = device_at({**place, "k": 1 - place["k"]})
    after = (seq_at, lax.rem(ch_at + 1, ch_size))
    before = (seq_at, lax.rem(ch_at + ch_size - 1, ch_size))

    filled_here = [
        jnp.clip(lengths[slot] - ch_at * length, 0, length) for slot in range(slots)
    ]
    vectors = held["vectors"]
    vectors[...] = jnp.zeros_like(vectors)

    def add_vector(name, value):
        at = VECTORS.index(name)
        vectors[at : at + 1, :] += jnp.sum(value, axis=0, keepdims=True)

    def normalize(value):
        center = value - jnp.mean(value, axis=-1, keepdims=True)
        factor = lax.rsqrt(jnp.mean(center * center, axis=-1, keepdims=True) + EPS)
        return center * factor, factor

    def blend(current, earlier, weights):
        return current * weights + earlier * (1.0 - weights)

    def tiles_of(slot, index):
        return pl.ds(pl.multiple_of(slot * length + index * TILE, TILE), TILE)

    row_in_tile = lax.broadcasted_iota(jnp.int32, (TILE, width), 0)

    def shift_down(value, carry):
        return jnp.where(row_in_tile == 0, carry, pltpu.roll(value, 1, 0))

    def shift_up(value, carry):
        return jnp.where(row_in_tile == TILE - 1, carry, pltpu.roll(value, TILE - 1, 0))

    steps_in_slot = length // TILE

    def matmul(left, panel, how, use, left_columns=None):
        def step(index, carry):
            columns = pl.ds(pl.multiple_of(index * MATMUL_WIDE, MATMUL_WIDE), MATMUL_WIDE)
            right = panel[:, columns] if how is NN else panel[columns, :]
            source = left[...] if left_columns is None else left[:, left_columns]
            use(columns, dot(source, right, how))
            return carry

        lax.fori_loop(0, width // MATMUL_WIDE, step, 0)

    def counts(slot, shape, offset):
        at = lax.broadcasted_iota(jnp.int32, shape, 0) + offset
        earlier = jnp.minimum(at, filled_here[slot]).astype(F32)
        upto = jnp.minimum(at + 1, filled_here[slot]).astype(F32)
        return earlier, upto, at < filled_here[slot]

    def tall_mask(columns):
        at = lax.broadcasted_iota(jnp.int32, (rows, columns), 0)
        inside = at < filled_here[0]
        for slot in range(1, slots):
            shifted = at - slot * length
            inside = inside | ((shifted >= 0) & (shifted < filled_here[slot]))
        return inside

    edges_out, edges_in = held["edges_out"], held["edges_in"]
    edges_out[...] = jnp.zeros_like(edges_out)
    for slot in range(slots):
        last = tokens[slot * length + length - 16 : slot * length + length, :].astype(F32)
        edges_out[0, slot : slot + 1, :] = last[15:, :]
    pl.semaphore_wait(barrier, greeted)
    edge_copy = copies.start(edges_out.at[0], edges_in.at[0], after)

    gain_mix, bias_mix = inputs["gain_mix"], inputs["bias_mix"]
    keep_edge = jnp.where(ch_at > 0, 1.0, 0.0)
    keep_next = jnp.where(ch_at < ch_size - 1, 1.0, 0.0)

    mixes = [inputs["mix_key"], inputs["mix_value"], inputs["mix_recept"]]
    both_mix = [held["both_key"], held["both_value"], held["both_recept"]]

    def last_row_before(slot, index):
        return pl.ds(pl.multiple_of(slot * length + index * TILE - 16, 16), 16)

    def mix_tile(slot, index, carry):
        spot = tiles_of(slot, index)
        unit, _ = normalize(tokens[spot, :].astype(F32))
        normed = unit * gain_mix[...] + bias_mix[...]
        earlier = shift_down(normed, carry)
        for weights, target in zip(mixes, both_mix):
            target[spot, :] = blend(normed, earlier, weights[...]).astype(BF16)

    def mix_carry(slot, index):
        unit, _ = normalize(tokens[last_row_before(slot, index), :].astype(F32))
        return (unit * gain_mix[...] + bias_mix[...])[15:, :]

    for slot in range(slots):

        def mix_step(index, carry, slot=slot):
            mix_tile(slot, index, mix_carry(slot, index))
            return carry

        lax.fori_loop(1, steps_in_slot, mix_step, 0)
    edge_copy.wait()
    edge_unit, _ = normalize(edges_in[0])
    edges_in[0] = (edge_unit * gain_mix[...] + bias_mix[...]) * keep_edge
    for slot in range(slots):
        mix_tile(slot, 0, edges_in[0, slot : slot + 1, :])
    exchanges = {}
    for name in ("key", "value", "recept"):
        ref = held["both_" + name]
        exchanges[name] = [
            copies.start(ref.at[pl.ds(0, rows), :], ref.at[pl.ds(rows, rows), :], partner)
        ]

    key_ref, value_ref = held["key"], held["value"]
    wide = {
        name: held["wide_" + name]
        for name in ("middle", "total", "sigmoid", "num", "den", "unit", "gap")
    }

    def own(name):
        return held["both_" + name].at[pl.ds(0, rows), :]

    def store_key(columns, product):
        key_ref[:, columns] = product.astype(BF16)

    def store_value(columns, product):
        value_ref[:, columns] = product.astype(BF16)

    matmul(own("key"), panels.take(), NN, store_key)
    panels.release()
    matmul(own("value"), panels.take(), NN, store_value)
    panels.release()

    time_decay, time_first = inputs["time_decay"], inputs["time_first"]
    square = (length, 3 * length)
    at_row = lax.broadcasted_iota(jnp.int32, square, 0)
    at_column = lax.rem(lax.broadcasted_iota(jnp.int32, square, 1), length)
    lower = jnp.where(at_column < at_row, 1.0, 0.0).astype(BF16)
    upper = jnp.where(at_column > at_row, 1.0, 0.0).astype(BF16)

    def triangle(matrix, value):
        high = value.astype(BF16)
        rest = value - high.astype(F32)
        middle = rest.astype(BF16)
        low = (rest - middle.astype(F32)).astype(BF16)
        return dot(matrix, jnp.concatenate([high, middle, low], axis=0), NN)

    sums_out, sums_in = held["sums_out"], held["sums_in"]
    sums_out[...] = jnp.zeros_like(sums_out)
    for slot in range(slots):

        def local_step(index, carry, slot=slot):
            columns = pl.ds(pl.multiple_of(index * WIDE, WIDE), WIDE)
            spot = pl.ds(slot * length, length)
            rate = jnp.exp(time_decay[:, columns])
            earlier, upto, filled = counts(slot, (length, WIDE), 0)
            stop = rate * filled_here[slot].astype(F32)
            keys = key_ref[spot, columns].astype(F32)
            weight = jnp.where(filled, jnp.exp(rate * upto - stop) * jnp.exp(keys), 0.0)
            payload = weight * value_ref[spot, columns].astype(F32)
            raised = jnp.exp(stop - rate * earlier)
            wide["num"][spot, columns] = raised * triangle(lower, payload)
            wide["den"][spot, columns] = raised * triangle(lower, weight)
            sums_out[0, slot : slot + 1, columns] = jnp.sum(payload, axis=0, keepdims=True)
            at = slots + slot
            sums_out[0, at : at + 1, columns] = jnp.sum(weight, axis=0, keepdims=True)
            return carry

        lax.fori_loop(0, width // WIDE, local_step, 0)

    def share(which):
        return [
            copies.start(
                sums_out.at[which],
                sums_in.at[which, step - 1],
                (seq_at, lax.rem(ch_at + step, ch_size)),
            )
            for step in range(1, ch_size)
        ]

    sum_copies = share(0)

    def store_sigmoid(columns, product):
        wide["sigmoid"][:, columns] = jax.nn.sigmoid(product)

    matmul(own("recept"), panels.take(), NN, store_sigmoid)
    panels.release()
    for copy in sum_copies:
        copy.wait()

    rate_row = jnp.exp(time_decay[...])
    states, finals = held["states"], held["finals"]
    states[...] = jnp.zeros_like(states)
    finals[...] = jnp.zeros_like(finals)
    for slot in range(slots):
        size = lengths[slot]
        reached = jnp.minimum(size, ch_at * length)
        for pair, initial in enumerate((inputs["init_num"], inputs["init_den"])):
            at = pair * slots + slot
            start_row = initial[slot : slot + 1, :]
            state = jnp.exp(-rate_row * reached.astype(F32)) * start_row
            final = jnp.exp(-rate_row * size.astype(F32)) * start_row
            for step in range(ch_size):
                source = lax.rem(ch_at + ch_size - step, ch_size)
                done = jnp.minimum(size, (source + 1) * length)
                term = (
                    sums_out[0, at : at + 1, :]
                    if step == 0
                    else sums_in[0, step - 1, at : at + 1, :]
                )
                final = final + jnp.exp(-rate_row * (size - done).astype(F32)) * term
                if step:
                    gone = jnp.maximum(reached - done, 0).astype(F32)
                    state = state + jnp.where(source < ch_at, jnp.exp(-rate_row * gone) * term, 0.0)
            states[at : at + 1, :] = state
            finals[at : at + 1, :] = final
    own_columns = pl.ds(pl.multiple_of(ch_at * plan.narrow, plan.narrow), plan.narrow)
    outputs["final"][...] = finals[:, own_columns]

    both_output = held["both_output"]
    for slot in range(slots):

        def wkv_step(index, carry, slot=slot):
            spot = tiles_of(slot, index)
            earlier, _, _ = counts(slot, (TILE, width), index * TILE)
            faded = jnp.exp(-rate_row * earlier)
            num = wide["num"][spot, :] + faded * states[slot : slot + 1, :]
            den = wide["den"][spot, :] + faded * states[slots + slot : slots + slot + 1, :]
            wide["num"][spot, :] = num
            wide["den"][spot, :] = den
            bonus = jnp.exp(time_first[...] + key_ref[spot, :].astype(F32))
            wkv = (num + bonus * value_ref[spot, :].astype(F32)) / (den + bonus)
            sent = wkv.astype(BF16).astype(F32)
            both_output[spot, :] = (wide["sigmoid"][spot, :] * sent).astype(BF16)
            return carry

        lax.fori_loop(0, steps_in_slot, wkv_step, 0)
    exchanges["output"] = [
        copies.start(
            both_output.at[pl.ds(0, rows), :], both_output.at[pl.ds(rows, rows), :], partner
        )
    ]

    def store_middle(columns, product):
        wide["middle"][:, columns] = tokens[:, columns].astype(F32) + product

    matmul(own("output"), panels.take(), NN, store_middle)
    panels.release()

    gain_ffn, bias_ffn = inputs["gain_ffn"], inputs["bias_ffn"]
    factor_ffn = held["factor_ffn"]
    for slot in range(slots):
        last = wide["middle"][slot * length + length - 8 : slot * length + length, :]
        unit, _ = normalize(last)
        edges_out[1, slot : slot + 1, :] = (unit * gain_ffn[...] + bias_ffn[...])[7:, :]
    edge_copy = copies.start(edges_out.at[1], edges_in.at[1], after)

    def unit_step(index, carry):
        spot = pl.ds(pl.multiple_of(index * TILE, TILE), TILE)
        unit, factor = normalize(wide["middle"][spot, :])
        wide["unit"][spot, :] = unit
        factor_ffn[spot, :] = jnp.broadcast_to(factor, (TILE, 128))
        return carry

    lax.fori_loop(0, rows // TILE, unit_step, 0)
    blends = [inputs["blend_key"], inputs["blend_gate"]]
    both_blend = [held["both_expand"], held["both_gate"]]

    def blend_tile(slot, index, carry):
        spot = tiles_of(slot, index)
        normed = wide["unit"][spot, :] * gain_ffn[...] + bias_ffn[...]
        earlier = shift_down(normed, carry)
        wide["gap"][spot, :] = normed - earlier
        for weights, target in zip(blends, both_blend):
            target[spot, :] = blend(normed, earlier, weights[...]).astype(BF16)

    for slot in range(slots):

        def blend_step(index, carry, slot=slot):
            last = wide["unit"][last_row_before(slot, index), :][15:, :]
            blend_tile(slot, index, last * gain_ffn[...] + bias_ffn[...])
            return carry

        lax.fori_loop(1, steps_in_slot, blend_step, 0)
    edge_copy.wait()
    for slot in range(slots):
        blend_tile(slot, 0, edges_in[1, slot : slot + 1, :] * keep_edge)
    both_expand, both_gate = held["both_expand"], held["both_gate"]

    def block_of(ref, index):
        return ref.at[pl.ds(index * rows, rows), :]

    exchanges["expand"] = [
        copies.start(block_of(both_expand, 0), block_of(both_expand, 1), partner)
    ]
    across = []
    for step in range(1, sizes["x"]):
        there = device_at(moved(place, sizes, "x", step))
        across.append(
            copies.start(block_of(both_expand, 0), block_of(both_expand, 2 * step), there)
        )
    exchanges["gate"] = [copies.start(block_of(both_gate, 0), block_of(both_gate, 1), partner)]

    both_hidden = held["both_hidden"]
    exchanges["hidden"] = []
    for index in range(panel_count):

        def store_hidden(columns, product, index=index):
            positive = jnp.maximum(product, 0.0)
            start = pl.multiple_of(columns.start + index * width, MATMUL_WIDE)
            both_hidden[first_rows, pl.ds(start, MATMUL_WIDE)] = (positive * positive).astype(BF16)

        matmul(own("expand"), panels.take(), NN, store_hidden)
        panels.release()
        part = pl.ds(index * width, width)
        exchanges["hidden"].append(
            copies.start(
                both_hidden.at[pl.ds(0, rows), part],
                both_hidden.at[pl.ds(rows, rows), part],
                partner,
            )
        )

        def add_contracted(columns, product, index=index):
            if index:
                product = product + wide["total"][:, columns]
            wide["total"][:, columns] = product

        matmul(both_hidden.at[pl.ds(0, rows), part], panels.take(), NN, add_contracted)
        panels.release()

    grad_contracted, grad_logit = held["rows_0"], held["rows_1"]

    def finish_forward(columns, product):
        gate = jax.nn.sigmoid(product)
        contracted = wide["total"][:, columns]
        inside = tall_mask(MATMUL_WIDE)
        mixed = wide["middle"][:, columns] + gate * contracted
        outputs["mixed_out"][:, columns] = jnp.where(inside, mixed, 0.0).astype(BF16)
        grad = jnp.where(inside, grad_out[:, columns].astype(F32), 0.0)
        grad_contracted[:, columns] = (grad * gate).astype(BF16)
        grad_logit[:, columns] = (grad * contracted * gate * (1.0 - gate)).astype(BF16)

    matmul(own("gate"), panels.take(), NN, finish_forward)
    panels.release()

    def hand_over(name, source):
        target = held["back_" + name]
        part = plan.narrow
        exchanges["back_" + name] = []
        for x_at in range(sizes["x"]):
            theirs = pl.multiple_of((x_at * 2 + 1 - place["k"]) * part, part)
            mine = pl.multiple_of((x_at * 2 + place["k"]) * part, part)
            spot = pl.ds(x_at * part, part)
            exchanges["back_" + name].append(
                copies.start(
                    source.at[:, pl.ds(theirs, part)],
                    target.at[pl.ds(rows, rows), spot],
                    partner,
                )
            )
            target[first_rows, spot] = source[:, pl.ds(mine, part)]

    def settle(*wanted):
        for name in wanted:
            for copy in exchanges.pop(name):
                copy.wait()

    grad_expanded, their_expanded = held["grad_expanded"], held["their_expanded"]

    def maker(piece):
        name, short_name, height, row_cut, breadth, column_cut = piece
        first = plan.orders[short_name][0]
        left = held["both_" + ("hidden" if name == "contract" else name)]
        row_step = plan.tall if name == "contract" else plan.short
        if name == "expand":
            rights = (
                (first_rows, grad_expanded, lambda at: ch_at * plan.broad + column_cut),
                (slice(rows, ch_size * rows), their_expanded, lambda at: column_cut),
            )
        else:
            rights = ((slice(None), held["back_" + name], lambda at: at * plan.narrow),)
        kept = [a for a in AXES if a in plan.orders[short_name] and a != first]

        def along(axis, coordinate):
            return [coordinate] if axis == first else range(sizes[axis])

        def make(coordinate, emit):
            places = [(l, y) for l in along("l", coordinate) for y in along("y", coordinate)]
            columns = [0] if name == "expand" else along("x", coordinate)

            def step(h, carry):
                starts = [((h * 2 + l) * 2 + y) * row_step + row_cut for l, y in places]
                spans = [(start, height) for start in starts]
                if row_step == height and first in "xlh":
                    spans = [(starts[0], len(starts) * height)]
                value = None
                for part, right, column_of in rights:
                    a = [
                        left[part, pl.ds(pl.multiple_of(start, math.gcd(span, 512)), span)]
                        for start, span in spans
                    ]
                    b = [
                        right[:, pl.ds(pl.multiple_of(column_of(x), breadth), breadth)]
                        for x in columns
                    ]
                    a = jnp.concatenate(a, axis=1) if len(a) > 1 else a[0]
                    b = jnp.concatenate(b, axis=1) if len(b) > 1 else b[0]
                    product = dot(a, b, TN)
                    value = product if value is None else value + product
                for index, (l, y) in enumerate(places):
                    rows_of = value[index * height : (index + 1) * height, :]
                    for x in columns:
                        at = 0 if first == "x" else x
                        block = rows_of[:, at * breadth : (at + 1) * breadth]
                        where = {"h": h, "l": l, "y": y, "x": x}
                        emit(tuple(where[a] for a in kept), block)
                return carry

            if first == "h":
                step(coordinate, 0)
            else:
                lax.fori_loop(0, sizes["h"], step, 0)

        return make

    pieces = {}
    for piece in plan.pieces:
        name, short_name, height, row_cut, breadth, column_cut = piece
        order_of = plan.orders[short_name]
        out_ref = outputs["grad_" + name].at[
            pl.ds(row_cut, height), pl.ds(column_cut, breadth)
        ]
        landings = [held["landing_" + short_name + str(stage)] for stage in range(len(order_of))]
        pieces[short_name] = Piece(
            maker(piece),
            order_of,
            sizes,
            place,
            copies,
            held["held_" + short_name],
            landings,
            out_ref,
        )

    def start_pieces(prefix):
        for short_name, piece in pieces.items():
            if short_name.startswith(prefix):
                piece.start()

    vector_in = held["vector_in"]
    vector_parts = held["vector_parts"]
    span = plan.vector_span
    scattered = span < width
    vector_queue = {"left": list("kxs" if scattered else "kxylh"), "open": [], "slot": 0}

    def part_of(index):
        return vectors.at[:, pl.ds(pl.multiple_of(index * span, span), span)]

    def start_vectors():
        axis = vector_queue["left"].pop(0)
        if axis == "s":
            for step in range(1, plan.seq):
                there = lax.rem(seq_at + step, plan.seq)
                target = vector_parts.at[step - 1]
                copy = copies.start(part_of(there), target, (there, ch_at))
                vector_queue["open"].append((copy, None))
            return
        for step in range(1, sizes[axis]):
            there = device_at(moved(place, sizes, axis, step))
            copy = copies.start(vectors, vector_in.at[vector_queue["slot"]], there)
            vector_queue["open"].append((copy, vector_queue["slot"]))
            vector_queue["slot"] += 1

    def pump_vectors():
        found, vector_queue["open"] = vector_queue["open"], []
        for copy, _ in found:
            copy.wait()
        for _, slot in found:
            if slot is not None:
                vectors[...] += vector_in[slot]
        if vector_queue["left"]:
            start_vectors()
        elif found:
            total = part_of(seq_at)[...] if scattered else vectors[...]
            for step in range(plan.seq - 1 if scattered else 0):
                total = total + vector_parts[step]
            outputs["vectors"][...] = total

    def pump(point, finish_mix=None):
        for short_name in PUMPS[point]:
            if short_name == "!":
                finish_mix()
                continue
            if short_name[0] == "E":
                if short_name in exchanges:
                    start_expand(int(short_name[1:]))
                continue
            if short_name == "*":
                pump_vectors()
                continue
            piece = pieces.get(short_name)
            if piece is not None and piece.copies:
                piece.advance()

    hand_over("contract", grad_contracted)
    hand_over("gate", grad_logit)
    settle("hidden", "back_contract")
    start_pieces("c")

    for index in range(panel_count):

        def store_expanded(columns, product, index=index):
            start = pl.multiple_of(columns.start + index * width, MATMUL_WIDE)
            spot = pl.ds(start, MATMUL_WIDE)
            positive = jnp.sqrt(both_hidden[first_rows, spot].astype(F32))
            grad_expanded[:, spot] = (product * 2.0 * positive).astype(BF16)

        matmul(grad_contracted, panels.take(), NT, store_expanded)
        panels.release()
    for step, copy in enumerate(across, 1):
        copy.wait()
        exchanges["expand"].append(
            copies.start(
                block_of(both_expand, 2 * step), block_of(both_expand, 2 * step + 1), partner
            )
        )

    def send_expanded(cut):
        if cut >= plan.expand_cuts:
            return
        part = plan.broad // plan.expand_cuts
        found = exchanges["E" + str(cut)] = []
        targets = [({**place, "k": 1 - place["k"]}, 0)]
        for step in range(1, sizes["x"]):
            there = moved(place, sizes, "x", step)
            targets.append((there, 2 * step - 1))
            targets.append(({**there, "k": 1 - place["k"]}, 2 * step))
        for there, slot in targets:
            start = (there["x"] * 2 + there["k"]) * plan.broad + cut * part
            found.append(
                copies.start(
                    grad_expanded.at[:, pl.ds(pl.multiple_of(start, part), part)],
                    their_expanded.at[pl.ds(slot * rows, rows), pl.ds(cut * part, part)],
                    device_at(there),
                )
            )

    def start_expand(cut):
        if "expand" in exchanges:
            settle("expand")
        settle("E" + str(cut))
        pieces["e" + str(cut)].start()

    send_expanded(0)
    pump(0)
    for index in range(panel_count):

        def add_expand(columns, product, index=index):
            if index:
                product = product + wide["total"][:, columns]
            wide["total"][:, columns] = product

        matmul(
            grad_expanded,
            panels.take(),
            NT,
            add_expand,
            left_columns=pl.ds(index * width, width),
        )
        panels.release()

    def store_gate(columns, product):
        wide["middle"][:, columns] = product

    matmul(grad_logit, panels.take(), NT, store_gate)
    panels.release()

    for slot in range(slots):
        spot = slice(slot * length, slot * length + 8)
        edge = wide["total"][spot, :] * (1.0 - blends[0][...])
        edge = edge + wide["middle"][spot, :] * (1.0 - blends[1][...])
        edges_out[2, slot : slot + 1, :] = edge[:1, :]
    edge_copy = copies.start(edges_out.at[2], edges_in.at[2], before)
    send_expanded(1)
    settle("gate", "back_gate")
    start_pieces("g")
    pump(1)
    grad_branch = held["rows_2"]

    def first_row_after(slot, index):
        return pl.ds(pl.multiple_of(slot * length + (index + 1) * TILE, 8), 8)

    def ffn_back_earlier(spot):
        earlier = wide["total"][spot, :] * (1.0 - blends[0][...])
        return earlier + wide["middle"][spot, :] * (1.0 - blends[1][...])

    def ffn_back_tile(slot, index, carry):
        spot = tiles_of(slot, index)
        in_expand, in_gate = wide["total"][spot, :], wide["middle"][spot, :]
        gap = wide["gap"][spot, :]
        unit = wide["unit"][spot, :]
        add_vector("blend_key", in_expand * gap)
        add_vector("blend_gate", in_gate * gap)
        earlier = ffn_back_earlier(spot)
        grad_normed = in_expand * blends[0][...] + in_gate * blends[1][...]
        grad_normed = grad_normed + shift_up(earlier, carry)
        add_vector("gain_ffn", grad_normed * unit)
        add_vector("bias_ffn", grad_normed)
        scaled = grad_normed * gain_ffn[...]
        centered = scaled - jnp.mean(scaled, axis=-1, keepdims=True)
        centered = centered - unit * jnp.mean(scaled * unit, axis=-1, keepdims=True)
        _, _, filled = counts(slot, (TILE, width), index * TILE)
        grad = jnp.where(filled, grad_out[spot, :].astype(F32), 0.0)
        grad = grad + factor_ffn[spot, :1] * centered
        wide["total"][spot, :] = grad
        grad_branch[spot, :] = grad.astype(BF16)

    for slot in range(slots):

        def ffn_back_step(index, carry, slot=slot):
            ffn_back_tile(slot, index, ffn_back_earlier(first_row_after(slot, index))[:1, :])
            return carry

        lax.fori_loop(0, steps_in_slot - 1, ffn_back_step, 0)
    edge_copy.wait()
    for slot in range(slots):
        ffn_back_tile(slot, steps_in_slot - 1, edges_in[2, slot : slot + 1, :] * keep_next)

    hand_over("output", grad_branch)
    pump(2)
    grad_recept = held["rows_3"]

    def gated_back(columns, product):
        gate = wide["sigmoid"][:, columns]
        bonus = jnp.exp(time_first[:, columns] + key_ref[:, columns].astype(F32))
        norm = wide["den"][:, columns] + bonus
        wkv = (wide["num"][:, columns] + bonus * value_ref[:, columns].astype(F32)) / norm
        sent = wkv.astype(BF16).astype(F32)
        grad_wkv = (product * gate).astype(BF16).astype(F32)
        grad_recept[:, columns] = (product * sent * gate * (1.0 - gate)).astype(BF16)
        upper_part = grad_wkv / norm
        wide["middle"][:, columns] = upper_part
        wide["gap"][:, columns] = -upper_part * wkv

    matmul(grad_branch, panels.take(), NT, gated_back)
    panels.release()
    hand_over("recept", grad_recept)
    pump(3)

    for slot in range(slots):

        def adjoint_step(index, carry, slot=slot):
            columns = pl.ds(pl.multiple_of(index * WIDE, WIDE), WIDE)
            spot = pl.ds(slot * length, length)
            rate = jnp.exp(time_decay[:, columns])
            earlier, upto, _ = counts(slot, (length, WIDE), 0)
            faded = jnp.exp(-rate * earlier)
            raised = jnp.exp(rate * upto)
            for pair, (source, target) in enumerate((("middle", "sigmoid"), ("gap", "unit"))):
                terms = faded * wide[source][spot, columns]
                wide[target][spot, columns] = raised * triangle(upper, terms)
                at = pair * slots + slot
                sums_out[1, at : at + 1, columns] = jnp.sum(terms, axis=0, keepdims=True)
            return carry

        lax.fori_loop(0, width // WIDE, adjoint_step, 0)
    sum_copies = share(1)
    send_expanded(2)
    send_expanded(3)
    settle("output", "back_output")
    start_pieces("o")
    settle("recept", "back_recept")
    start_pieces("r")
    pump(4)
    for copy in sum_copies:
        copy.wait()
    later = held["later"]
    later[...] = jnp.zeros_like(later)
    for slot in range(slots):
        size = lengths[slot]
        done = jnp.minimum(size, (ch_at + 1) * length)
        for pair in range(2):
            at = pair * slots + slot
            total = jnp.zeros((1, width), F32)
            for step in range(1, ch_size):
                source = lax.rem(ch_at + ch_size - step, ch_size)
                reached = jnp.minimum(size, source * length)
                gone = jnp.maximum(reached - done, 0).astype(F32)
                term = sums_in[1, step - 1, at : at + 1, :]
                total = total + jnp.where(source > ch_at, jnp.exp(-rate_row * gone) * term, 0.0)
            later[at : at + 1, :] = total

    grad_key, grad_value = held["rows_0"], held["rows_1"]
    for slot in range(slots):

        def wkv_back_step(index, carry, slot=slot):
            spot = tiles_of(slot, index)
            _, upto, filled = counts(slot, (TILE, width), index * TILE)
            left = filled_here[slot].astype(F32) - upto
            faded = jnp.exp(-rate_row * left)
            adj_num = wide["sigmoid"][spot, :] + faded * later[slot : slot + 1, :]
            adj_den = wide["unit"][spot, :] + faded * later[slots + slot : slots + slot + 1, :]
            keys, values = key_ref[spot, :].astype(F32), value_ref[spot, :].astype(F32)
            bonus = jnp.exp(time_first[...] + keys)
            weight = jnp.where(filled, jnp.exp(keys), 0.0)
            upper_part, lower_part = wide["middle"][spot, :], wide["gap"][spot, :]
            direct = (upper_part * values + lower_part) * bonus
            grad_value[spot, :] = (upper_part * bonus + weight * adj_num).astype(BF16)
            grad_key[spot, :] = (direct + weight * (adj_num * values + adj_den)).astype(BF16)
            add_vector("time_first", direct)
            decay = adj_num * wide["num"][spot, :] + adj_den * wide["den"][spot, :]
            add_vector("time_decay", jnp.where(filled, decay, 0.0))
            return carry

        lax.fori_loop(0, steps_in_slot, wkv_back_step, 0)
    decay_at = VECTORS.index("time_decay")
    vectors[decay_at : decay_at + 1, :] *= -rate_row * jnp.exp(-rate_row)

    hand_over("key", grad_key)
    hand_over("value", grad_value)
    pump(5)

    def keeper(name):
        def keep(columns, product):
            wide[name][:, columns] = product

        return keep

    for source, name in ((grad_key, "sigmoid"), (grad_value, "unit"), (grad_recept, "gap")):
        matmul(source, panels.take(), NT, keeper(name))
        panels.release()
    in_names = ("sigmoid", "unit", "gap")
    for slot in range(slots):
        spot = slice(slot * length, slot * length + 8)
        edge = jnp.zeros((8, width), F32)
        for name, weights in zip(in_names, mixes):
            edge = edge + wide[name][spot, :] * (1.0 - weights[...])
        edges_out[3, slot : slot + 1, :] = edge[:1, :]
    edge_copy = copies.start(edges_out.at[3], edges_in.at[3], before)
    for name in ("key", "value"):
        settle(name, "back_" + name)
        start_pieces(name[0])
    pump(6)

    in_carry = [edges_in[0, slot : slot + 1, :] for slot in range(slots)]
    vector_names = ("mix_key", "mix_value", "mix_recept")

    def mix_back_earlier(spot):
        earlier = wide[in_names[0]][spot, :] * (1.0 - mixes[0][...])
        for name, weights in zip(in_names[1:], mixes[1:]):
            earlier = earlier + wide[name][spot, :] * (1.0 - weights[...])
        return earlier

    def mix_back_tile(slot, index, before_row, after_row):
        spot = tiles_of(slot, index)
        unit, factor = normalize(tokens[spot, :].astype(F32))
        normed = unit * gain_mix[...] + bias_mix[...]
        gap = normed - shift_down(normed, before_row)
        grad_normed = shift_up(mix_back_earlier(spot), after_row)
        for name, weights, vector in zip(in_names, mixes, vector_names):
            grad = wide[name][spot, :]
            add_vector(vector, grad * gap)
            grad_normed = grad_normed + grad * weights[...]
        add_vector("gain_mix", grad_normed * unit)
        add_vector("bias_mix", grad_normed)
        scaled = grad_normed * gain_mix[...]
        centered = scaled - jnp.mean(scaled, axis=-1, keepdims=True)
        centered = centered - unit * jnp.mean(scaled * unit, axis=-1, keepdims=True)
        grad = wide["total"][spot, :] + factor * centered
        outputs["grad_tokens"][spot, :] = grad.astype(BF16)

    def next_row(slot, index):
        return mix_back_earlier(first_row_after(slot, index))[:1, :]

    last_tile = steps_in_slot - 1
    for slot in range(slots):

        def mix_back_step(index, carry, slot=slot):
            mix_back_tile(slot, index, mix_carry(slot, index), next_row(slot, index))
            return carry

        lax.fori_loop(1, last_tile, mix_back_step, 0)
        if last_tile:
            mix_back_tile(slot, 0, in_carry[slot], next_row(slot, 0))
    def finish_mix():
        edge_copy.wait()
        for slot in range(slots):
            after_row = edges_in[3, slot : slot + 1, :] * keep_next
            before_row = mix_carry(slot, last_tile) if last_tile else in_carry[slot]
            mix_back_tile(slot, last_tile, before_row, after_row)
        start_vectors()

    pump(7, finish_mix)
    for cut in range(plan.expand_cuts):
        if "E" + str(cut) in exchanges:
            start_expand(cut)
    while any(piece.copies for piece in pieces.values()):
        for piece in pieces.values():
            if piece.copies:
                piece.advance()
    while vector_queue["open"]:
        pump_vectors()


LARGE = tuple(name for name in OUTPUTS if name not in ("final", "vectors"))


def place_outputs(plan, *refs):
    count = len(LARGE)
    refs = list(refs)

    def take(number):
        return [refs.pop(0) for _ in range(number)]

    sources, (final, vectors) = take(count), take(2)
    targets, finals, parts = take(count), take(2), take(len(VECTORS))
    buffers, (sems,) = take(count), take(1)
    loads, stores = [], []
    for index in range(count):
        loads.append(pltpu.make_async_copy(sources[index], buffers[index], sems.at[0, index]))
        stores.append(pltpu.make_async_copy(buffers[index], targets[index], sems.at[1, index]))
        loads[-1].start()
    slots = plan.slots
    for index, target in enumerate(finals):
        target[...] = final[index * slots : (index + 1) * slots, :]
    part = plan.width // (plan.seq * plan.ch)
    at = lax.axis_index("ch") * part
    span = plan.vector_span
    if span == plan.width:
        at = at + lax.axis_index("seq") * plan.short
    turned = pltpu.roll(vectors[...], lax.rem(span - at, span), 1)
    for index, target in enumerate(parts):
        target[...] = turned[index, :part]
    for load, store in zip(loads, stores):
        load.wait()
        store.start()
    for store in stores:
        store.wait()


def body(*arguments):
    values = dict(zip(INPUTS, arguments))
    plan = Plan(values["tokens"], values["w_expand"])
    rows, width = plan.rows, plan.width
    operands, specs = [], []
    for name in INPUTS:
        value = values[name]
        space = pltpu.VMEM
        if name in ("tokens", "grad_out"):
            value = value.reshape(rows, width)
        elif name == "lengths":
            space = pltpu.SMEM
        elif name.startswith("w_"):
            space = pl.ANY
        elif value.ndim == 1:
            value = value.reshape(1, width)
        operands.append(value)
        specs.append(pl.BlockSpec(memory_space=space))
    outs = {
        "mixed_out": ((rows, width), BF16),
        "grad_tokens": ((rows, width), BF16),
        "final": ((8, plan.narrow), F32),
        "grad_key": ((plan.short, plan.narrow), F32),
        "grad_value": ((plan.short, plan.narrow), F32),
        "grad_recept": ((plan.short, plan.narrow), F32),
        "grad_output": ((plan.short, plan.narrow), F32),
        "grad_expand": ((plan.short, plan.broad), F32),
        "grad_contract": ((plan.tall, plan.narrow), F32),
        "grad_gate": ((plan.short, plan.narrow), F32),
        "vectors": ((16, plan.vector_span), F32),
    }
    results = pl.pallas_call(
        functools.partial(layer_kernel, plan),
        out_shape=[jax.ShapeDtypeStruct(*outs[name]) for name in OUTPUTS],
        in_specs=specs,
        out_specs=[pl.BlockSpec(memory_space=pltpu.VMEM)] * len(OUTPUTS),
        scratch_shapes=list(plan.shapes.values()),
        compiler_params=pltpu.CompilerParams(
            collective_id=0, has_side_effects=True, vmem_limit_bytes=63 * 2**20
        ),
    )(*operands)
    part = width // (plan.seq * plan.ch)
    slots = plan.slots
    got = dict(zip(OUTPUTS, results))
    vmem, hbm = pl.BlockSpec(memory_space=pltpu.VMEM), pl.BlockSpec(memory_space=pl.ANY)
    shapes = [outs[name] for name in LARGE] + [((slots, plan.narrow), F32)] * 2
    shapes += [((part,), F32)] * len(VECTORS)
    results = pl.pallas_call(
        functools.partial(place_outputs, plan),
        out_shape=[jax.ShapeDtypeStruct(*shape) for shape in shapes],
        in_specs=[hbm] * len(LARGE) + [vmem] * 2,
        out_specs=[hbm] * len(LARGE) + [vmem] * (2 + len(VECTORS)),
        scratch_shapes=[pltpu.VMEM(*outs[name]) for name in LARGE]
        + [pltpu.SemaphoreType.DMA((2, len(LARGE)))],
        compiler_params=pltpu.CompilerParams(vmem_limit_bytes=60 * 2**20),
    )(*[got[name] for name in LARGE], got["final"], got["vectors"])
    mixed_out, grad_tokens, *weights = results[: len(LARGE)]
    shape = values["tokens"].shape
    return (
        mixed_out.reshape(shape),
        grad_tokens.reshape(shape),
        *results[len(LARGE) : len(LARGE) + 2],
        *weights,
        *results[len(LARGE) + 2 :],
    )


def solution(mesh):
    split, copied = P("seq", "ch", None), P()
    placed = (split, split, P("seq"), P("seq", None), P("seq", None)) + (copied,) * 18
    both = P("seq", "ch")
    return jax.shard_map(
        body,
        mesh=mesh,
        in_specs=placed,
        out_specs=(split, split) + (both,) * 9 + (P(("seq", "ch")),) * 11,
        check_vma=False,
    )
```

```python
import functools
import math

import jax
import jax.numpy as jnp
from jax import lax
from jax.experimental import pallas as pl
from jax.experimental.pallas import tpu as pltpu
from jax.sharding import PartitionSpec as P

EPS = 1e-05
MESH = pl.DeviceIdType.MESH
AXES = "hlyx"
F32 = jnp.float32
BF16 = jnp.bfloat16
TILE = 64
WIDE = 512
MATMUL_WIDE = 1024
SLOTS_OF_WEIGHTS = 3

ORDERS = {
    "c0": "yxlh",
    "c1": "lyhx",
    "c2": "ylhx",
    "c3": "lxyh",
    "e0": "ylh",
    "e1": "ylh",
    "e2": "ylh",
    "e3": "ylh",
    "g": "lxyh",
    "o": "ylhx",
    "k": "xylh",
    "v": "xylh",
    "r": "xylh",
}
PUMPS = (
    (),
    (),
    (
        "c0", "c1", "E0",
    ),
    (),
    (),
    (
        "E1", "c2", "c0",
    ),
    (
        "c3", "c1", "E2",
    ),
    (
        "e0", "g", "E3", "c2", "c0", "o", "c1", "r", "!", "e0", "e1", "*", "c2", "c0", "e2", "o",
        "k", "e0", "e3", "e1", "e2", "r", "o", "v", "e3", "e1", "k", "c3", "e2", "r", "e3", "v",
        "k", "c3", "g", "c1", "r", "*", "v", "c2", "g", "o", "*", "k", "c3", "v", "g",
    ),
)

NN = (((1,), (0,)), ((), ()))
NT = (((1,), (1,)), ((), ()))
TN = (((0,), (0,)), ((), ()))


def dot(left, right, how):
    return lax.dot_general(left, right, how, preferred_element_type=F32)


def axis_sizes():
    seq_size, ch_size = lax.axis_size("seq"), lax.axis_size("ch")
    return {"k": 2, "x": ch_size // 2, "y": 2, "l": 2, "h": seq_size // 4}


def coordinates():
    seq_at, ch_at = lax.axis_index("seq"), lax.axis_index("ch")
    return {
        "h": seq_at // 4,
        "l": seq_at // 2 % 2,
        "y": seq_at % 2,
        "x": ch_at // 2,
        "k": ch_at % 2,
    }


def device_at(place):
    return (place["h"] * 4 + place["l"] * 2 + place["y"], place["x"] * 2 + place["k"])


def moved(place, sizes, axis, step):
    return {**place, axis: lax.rem(place[axis] + step, sizes[axis])}


class Copies:
    def __init__(self, sends, receives):
        self.sends, self.receives, self.used = sends, receives, 0
        self.open = []

    def start(self, source, target, device):
        copy = pltpu.make_async_remote_copy(
            src_ref=source,
            dst_ref=target,
            send_sem=self.sends.at[self.used],
            recv_sem=self.receives.at[self.used],
            device_id=device,
            device_id_type=MESH,
        )
        self.used += 1
        copy.start()
        return copy


class Piece:
    def __init__(self, make, order, sizes, place, copies, held, landings, out_ref):
        self.make, self.order, self.sizes, self.place = make, order, sizes, place
        self.remote, self.held, self.landings, self.out_ref = copies, held, landings, out_ref
        self.axes = [axis for axis in AXES if axis in order]
        self.stage = 0
        self.copies = []

    def start(self):
        axis = self.order[self.stage]
        at = self.axes.index(axis)
        for step in range(1, self.sizes[axis]):
            there = moved(self.place, self.sizes, axis, step)
            if self.stage == 0:

                def keep(where, value, slot=step - 1):
                    self.held[(slot,) + where] = value.astype(BF16)

                self.make(there[axis], keep)
                source = self.held.at[step - 1]
            else:
                source = self.landings[self.stage - 1].at[
                    (0,) + (slice(None),) * at + (there[axis],)
                ]
            self.copies.append(
                self.remote.start(
                    source, self.landings[self.stage].at[step - 1], device_at(there)
                )
            )

    def finish(self):
        axis = self.order[self.stage]
        at = self.axes.index(axis)
        landing = self.landings[self.stage]
        others = self.sizes[axis] - 1
        for copy in self.copies:
            copy.wait()
        self.copies = []
        remaining = [a for a in self.axes if a != axis]
        if self.stage == 0:

            def add(where, value):
                for other in range(others):
                    value = value + landing[(other,) + where].astype(F32)
                landing[(0,) + where] = value.astype(BF16)

            self.make(self.place[axis], add)
        else:
            own = self.landings[self.stage - 1].at[
                (0,) + (slice(None),) * at + (self.place[axis],)
            ]
            lead = tuple(self.sizes[a] for a in remaining)
            rows, columns = landing.shape[-2:]
            tile = math.gcd(rows, max(16, 32768 // columns))
            parts = rows // tile

            def add_tile(index, carry):
                part, rest = index % parts, index // parts
                where = ()
                for size in reversed(lead):
                    where = (rest % size,) + where
                    rest = rest // size
                spot = pl.ds(pl.multiple_of(part * tile, tile), tile)
                where = where + (spot, slice(None))
                total = own[where].astype(F32)
                for other in range(others):
                    total = total + landing[(other,) + where].astype(F32)
                if remaining:
                    landing[(0,) + where] = total.astype(BF16)
                else:
                    self.out_ref[where] = total
                return carry

            lax.fori_loop(0, math.prod(lead) * parts, add_tile, 0)
        self.axes = remaining
        self.stage += 1

    def advance(self):
        self.finish()
        if self.axes:
            self.start()


class Plan:
    def __init__(self, tokens, w_expand):
        self.slots, self.length, self.width = tokens.shape
        self.hidden = w_expand.shape[1]
        self.sizes = sizes = axis_sizes()
        self.seq, self.ch = sizes["h"] * 4, sizes["x"] * 2
        self.rows = self.slots * self.length
        rows, width, hidden = self.rows, self.width, self.hidden
        self.narrow = width // self.ch
        self.broad = hidden // self.ch
        self.short = width // self.seq
        self.tall = hidden // self.seq
        self.vector_span = self.short if self.short % 128 == 0 else width
        half = sizes["x"] * self.narrow
        self.pieces = []
        cuts = 4 if (self.tall // 4) % 128 == 0 else 1
        part = self.tall // cuts
        for cut in range(cuts):
            self.pieces.append(("contract", "c" + str(cut), part, cut * part, self.narrow, 0))
        cuts = 4 if (self.broad // 4) % 128 == 0 else 1
        self.expand_cuts = cuts
        part = self.broad // cuts
        for cut in range(cuts):
            self.pieces.append(("expand", "e" + str(cut), self.short, 0, part, cut * part))
        for name in ("gate", "output", "key", "value", "recept"):
            self.pieces.append((name, name[0], self.short, 0, self.narrow, 0))
        self.orders = {}
        for name, short_name, height, _, _, _ in self.pieces:
            if height % 128 == 0:
                self.orders[short_name] = ORDERS[short_name]
            else:
                self.orders[short_name] = "hly" if name == "expand" else "xylh"
        vmem = pltpu.VMEM
        shapes = {
            "panels": vmem((SLOTS_OF_WEIGHTS, width, width), BF16),
            "both_hidden": vmem((2 * rows, hidden), BF16),
            "grad_expanded": vmem((rows, hidden), BF16),
            "their_expanded": vmem(((self.ch - 1) * rows, self.broad), BF16),
            "both_expand": vmem((self.ch * rows, width), BF16),
            "key": vmem((rows, width), BF16),
            "value": vmem((rows, width), BF16),
            "edges_out": vmem((4, 8, width), F32),
            "edges_in": vmem((4, 8, width), F32),
            "sums_out": vmem((2, 8, width), F32),
            "sums_in": vmem((2, self.ch - 1, 8, width), F32),
            "states": vmem((8, width), F32),
            "finals": vmem((8, width), F32),
            "later": vmem((8, width), F32),
            "factor_ffn": vmem((rows, 128), F32),
            "vectors": vmem((16, width), F32),
            "vector_in": vmem((self.count_vector_slots(), 16, width), F32),
            "vector_parts": vmem((self.seq - 1, 16, self.vector_span), F32),
        }
        for name in ("gate", "output", "key", "value", "recept"):
            shapes["both_" + name] = vmem((2 * rows, width), BF16)
        for name in ("contract", "gate", "output", "key", "value", "recept"):
            shapes["back_" + name] = vmem((2 * rows, half), BF16)
        for index in range(4):
            shapes["rows_" + str(index)] = vmem((rows, width), BF16)
        for name in ("middle", "total", "sigmoid", "num", "den", "unit", "gap"):
            shapes["wide_" + name] = vmem((rows, width), F32)
        copies = 64 + 16 * self.ch
        for name, short_name, height, _, breadth, _ in self.pieces:
            order = self.orders[short_name]
            axes = [axis for axis in AXES if axis in order[1:]]
            lead = tuple(sizes[a] for a in axes)
            shapes["held_" + short_name] = vmem(
                (sizes[order[0]] - 1,) + lead + (height, breadth), BF16
            )
            axes = [axis for axis in AXES if axis in order]
            for stage, axis in enumerate(order):
                axes.remove(axis)
                shape = (sizes[axis] - 1,) + tuple(sizes[a] for a in axes) + (height, breadth)
                shapes["landing_" + short_name + str(stage)] = vmem(shape, BF16)
                copies += sizes[axis] - 1
        copies += self.count_vector_slots() + self.seq
        shapes["sends"] = pltpu.SemaphoreType.DMA((copies,))
        shapes["receives"] = pltpu.SemaphoreType.DMA((copies,))
        shapes["panel_sems"] = pltpu.SemaphoreType.DMA((SLOTS_OF_WEIGHTS,))
        self.shapes = shapes

    def count_vector_slots(self):
        axes = "kx" if self.vector_span < self.width else "kxylh"
        return sum(self.sizes[axis] - 1 for axis in axes)


INPUTS = (
    "tokens",
    "grad_out",
    "lengths",
    "init_num",
    "init_den",
    "w_key",
    "w_value",
    "w_recept",
    "w_output",
    "w_expand",
    "w_contract",
    "w_gate",
    "gain_mix",
    "bias_mix",
    "gain_ffn",
    "bias_ffn",
    "mix_key",
    "mix_value",
    "mix_recept",
    "blend_key",
    "blend_gate",
    "time_decay",
    "time_first",
)
OUTPUTS = (
    "mixed_out",
    "grad_tokens",
    "final",
    "grad_key",
    "grad_value",
    "grad_recept",
    "grad_output",
    "grad_expand",
    "grad_contract",
    "grad_gate",
    "vectors",
)
VECTORS = (
    "gain_mix",
    "bias_mix",
    "gain_ffn",
    "bias_ffn",
    "mix_key",
    "mix_value",
    "mix_recept",
    "blend_key",
    "blend_gate",
    "time_decay",
    "time_first",
)


class Panels:
    def __init__(self, sources, ref, sems):
        self.sources, self.ref, self.sems = sources, ref, sems
        self.used = 0
        for index in range(min(SLOTS_OF_WEIGHTS, len(sources))):
            self.copy(index).start()

    def copy(self, index):
        slot = index % SLOTS_OF_WEIGHTS
        return pltpu.make_async_copy(self.sources[index], self.ref.at[slot], self.sems.at[slot])

    def take(self):
        self.copy(self.used).wait()
        return self.ref.at[self.used % SLOTS_OF_WEIGHTS]

    def release(self):
        index = self.used + SLOTS_OF_WEIGHTS
        if index < len(self.sources):
            self.copy(index).start()
        self.used += 1


def layer_kernel(plan, *all_refs):
    inputs = dict(zip(INPUTS, all_refs))
    outputs = dict(zip(OUTPUTS, all_refs[len(INPUTS) :]))
    held = dict(zip(plan.shapes, all_refs[len(INPUTS) + len(OUTPUTS) :]))
    sizes = plan.sizes
    place = coordinates()
    ch_at = lax.axis_index("ch")
    seq_at = lax.axis_index("seq")
    slots, length, width, rows = plan.slots, plan.length, plan.width, plan.rows
    hidden, ch_size = plan.hidden, plan.ch
    panel_count = hidden // width
    tokens, grad_out, lengths = inputs["tokens"], inputs["grad_out"], inputs["lengths"]
    first_rows = slice(0, rows)
    last_rows = slice(rows, 2 * rows)

    w_expand, w_contract = inputs["w_expand"], inputs["w_contract"]

    def expand_panel(index):
        return w_expand.at[:, pl.ds(index * width, width)]

    def contract_panel(index):
        return w_contract.at[pl.ds(index * width, width), :]

    order = [inputs["w_key"], inputs["w_value"], inputs["w_recept"], inputs["w_output"]]
    for index in range(panel_count):
        order += [expand_panel(index), contract_panel(index)]
    order += [inputs["w_gate"]]
    order += [contract_panel(index) for index in range(panel_count)]
    order += [expand_panel(index) for index in range(panel_count)]
    order += [inputs["w_gate"], inputs["w_output"]]
    order += [inputs["w_key"], inputs["w_value"], inputs["w_recept"]]
    panels = Panels(order, held["panels"], held["panel_sems"])

    barrier = pltpu.get_barrier_semaphore()
    greeted = 0
    for step in range(1, ch_size):
        pl.semaphore_signal(
            barrier,
            inc=1,
            device_id=(seq_at, lax.rem(ch_at + step, ch_size)),
            device_id_type=MESH,
        )
        greeted += 1
    for step in range(1, plan.seq):
        pl.semaphore_signal(
            barrier,
            inc=1,
            device_id=(lax.rem(seq_at + step, plan.seq), ch_at),
            device_id_type=MESH,
        )
        greeted += 1
    copies = Copies(held["sends"], held["receives"])
    partner = device_at({**place, "k": 1 - place["k"]})
    after = (seq_at, lax.rem(ch_at + 1, ch_size))
    before = (seq_at, lax.rem(ch_at + ch_size - 1, ch_size))

    filled_here = [
        jnp.clip(lengths[slot] - ch_at * length, 0, length) for slot in range(slots)
    ]
    vectors = held["vectors"]
    vectors[...] = jnp.zeros_like(vectors)

    def add_vector(name, value):
        at = VECTORS.index(name)
        vectors[at : at + 1, :] += jnp.sum(value, axis=0, keepdims=True)

    def normalize(value):
        center = value - jnp.mean(value, axis=-1, keepdims=True)
        factor = lax.rsqrt(jnp.mean(center * center, axis=-1, keepdims=True) + EPS)
        return center * factor, factor

    def blend(current, earlier, weights):
        return current * weights + earlier * (1.0 - weights)

    def tiles_of(slot, index):
        return pl.ds(pl.multiple_of(slot * length + index * TILE, TILE), TILE)

    row_in_tile = lax.broadcasted_iota(jnp.int32, (TILE, width), 0)

    def shift_down(value, carry):
        return jnp.where(row_in_tile == 0, carry, pltpu.roll(value, 1, 0))

    def shift_up(value, carry):
        return jnp.where(row_in_tile == TILE - 1, carry, pltpu.roll(value, TILE - 1, 0))

    steps_in_slot = length // TILE

    def matmul(left, panel, how, use, left_columns=None):
        def step(index, carry):
            columns = pl.ds(pl.multiple_of(index * MATMUL_WIDE, MATMUL_WIDE), MATMUL_WIDE)
            right = panel[:, columns] if how is NN else panel[columns, :]
            source = left[...] if left_columns is None else left[:, left_columns]
            use(columns, dot(source, right, how))
            return carry

        lax.fori_loop(0, width // MATMUL_WIDE, step, 0)

    def counts(slot, shape, offset):
        at = lax.broadcasted_iota(jnp.int32, shape, 0) + offset
        earlier = jnp.minimum(at, filled_here[slot]).astype(F32)
        upto = jnp.minimum(at + 1, filled_here[slot]).astype(F32)
        return earlier, upto, at < filled_here[slot]

    def tall_mask(columns):
        at = lax.broadcasted_iota(jnp.int32, (rows, columns), 0)
        inside = at < filled_here[0]
        for slot in range(1, slots):
            shifted = at - slot * length
            inside = inside | ((shifted >= 0) & (shifted < filled_here[slot]))
        return inside

    edges_out, edges_in = held["edges_out"], held["edges_in"]
    edges_out[...] = jnp.zeros_like(edges_out)
    for slot in range(slots):
        last = tokens[slot * length + length - 16 : slot * length + length, :].astype(F32)
        edges_out[0, slot : slot + 1, :] = last[15:, :]
    pl.semaphore_wait(barrier, greeted)
    edge_copy = copies.start(edges_out.at[0], edges_in.at[0], after)

    gain_mix, bias_mix = inputs["gain_mix"], inputs["bias_mix"]
    keep_edge = jnp.where(ch_at > 0, 1.0, 0.0)
    keep_next = jnp.where(ch_at < ch_size - 1, 1.0, 0.0)

    mixes = [inputs["mix_key"], inputs["mix_value"], inputs["mix_recept"]]
    both_mix = [held["both_key"], held["both_value"], held["both_recept"]]

    def last_row_before(slot, index):
        return pl.ds(pl.multiple_of(slot * length + index * TILE - 16, 16), 16)

    def mix_tile(slot, index, carry):
        spot = tiles_of(slot, index)
        unit, _ = normalize(tokens[spot, :].astype(F32))
        normed = unit * gain_mix[...] + bias_mix[...]
        earlier = shift_down(normed, carry)
        for weights, target in zip(mixes, both_mix):
            target[spot, :] = blend(normed, earlier, weights[...]).astype(BF16)

    def mix_carry(slot, index):
        unit, _ = normalize(tokens[last_row_before(slot, index), :].astype(F32))
        return (unit * gain_mix[...] + bias_mix[...])[15:, :]

    for slot in range(slots):

        def mix_step(index, carry, slot=slot):
            mix_tile(slot, index, mix_carry(slot, index))
            return carry

        lax.fori_loop(1, steps_in_slot, mix_step, 0)
    edge_copy.wait()
    edge_unit, _ = normalize(edges_in[0])
    edges_in[0] = (edge_unit * gain_mix[...] + bias_mix[...]) * keep_edge
    for slot in range(slots):
        mix_tile(slot, 0, edges_in[0, slot : slot + 1, :])
    exchanges = {}
    for name in ("key", "value", "recept"):
        ref = held["both_" + name]
        exchanges[name] = [
            copies.start(ref.at[pl.ds(0, rows), :], ref.at[pl.ds(rows, rows), :], partner)
        ]

    key_ref, value_ref = held["key"], held["value"]
    wide = {
        name: held["wide_" + name]
        for name in ("middle", "total", "sigmoid", "num", "den", "unit", "gap")
    }

    def own(name):
        return held["both_" + name].at[pl.ds(0, rows), :]

    def store_key(columns, product):
        key_ref[:, columns] = product.astype(BF16)

    def store_value(columns, product):
        value_ref[:, columns] = product.astype(BF16)

    matmul(own("key"), panels.take(), NN, store_key)
    panels.release()
    matmul(own("value"), panels.take(), NN, store_value)
    panels.release()

    time_decay, time_first = inputs["time_decay"], inputs["time_first"]
    square = (length, 3 * length)
    at_row = lax.broadcasted_iota(jnp.int32, square, 0)
    at_column = lax.rem(lax.broadcasted_iota(jnp.int32, square, 1), length)
    lower = jnp.where(at_column < at_row, 1.0, 0.0).astype(BF16)
    upper = jnp.where(at_column > at_row, 1.0, 0.0).astype(BF16)

    def triangle(matrix, value):
        high = value.astype(BF16)
        rest = value - high.astype(F32)
        middle = rest.astype(BF16)
        low = (rest - middle.astype(F32)).astype(BF16)
        return dot(matrix, jnp.concatenate([high, middle, low], axis=0), NN)

    sums_out, sums_in = held["sums_out"], held["sums_in"]
    sums_out[...] = jnp.zeros_like(sums_out)
    for slot in range(slots):

        def local_step(index, carry, slot=slot):
            columns = pl.ds(pl.multiple_of(index * WIDE, WIDE), WIDE)
            spot = pl.ds(slot * length, length)
            rate = jnp.exp(time_decay[:, columns])
            earlier, upto, filled = counts(slot, (length, WIDE), 0)
            stop = rate * filled_here[slot].astype(F32)
            keys = key_ref[spot, columns].astype(F32)
            weight = jnp.where(filled, jnp.exp(rate * upto - stop) * jnp.exp(keys), 0.0)
            payload = weight * value_ref[spot, columns].astype(F32)
            raised = jnp.exp(stop - rate * earlier)
            wide["num"][spot, columns] = raised * triangle(lower, payload)
            wide["den"][spot, columns] = raised * triangle(lower, weight)
            sums_out[0, slot : slot + 1, columns] = jnp.sum(payload, axis=0, keepdims=True)
            at = slots + slot
            sums_out[0, at : at + 1, columns] = jnp.sum(weight, axis=0, keepdims=True)
            return carry

        lax.fori_loop(0, width // WIDE, local_step, 0)

    def share(which):
        return [
            copies.start(
                sums_out.at[which],
                sums_in.at[which, step - 1],
                (seq_at, lax.rem(ch_at + step, ch_size)),
            )
            for step in range(1, ch_size)
        ]

    sum_copies = share(0)

    def store_sigmoid(columns, product):
        wide["sigmoid"][:, columns] = jax.nn.sigmoid(product)

    matmul(own("recept"), panels.take(), NN, store_sigmoid)
    panels.release()
    for copy in sum_copies:
        copy.wait()

    rate_row = jnp.exp(time_decay[...])
    states, finals = held["states"], held["finals"]
    states[...] = jnp.zeros_like(states)
    finals[...] = jnp.zeros_like(finals)
    for slot in range(slots):
        size = lengths[slot]
        reached = jnp.minimum(size, ch_at * length)
        for pair, initial in enumerate((inputs["init_num"], inputs["init_den"])):
            at = pair * slots + slot
            start_row = initial[slot : slot + 1, :]
            state = jnp.exp(-rate_row * reached.astype(F32)) * start_row
            final = jnp.exp(-rate_row * size.astype(F32)) * start_row
            for step in range(ch_size):
                source = lax.rem(ch_at + ch_size - step, ch_size)
                done = jnp.minimum(size, (source + 1) * length)
                term = (
                    sums_out[0, at : at + 1, :]
                    if step == 0
                    else sums_in[0, step - 1, at : at + 1, :]
                )
                final = final + jnp.exp(-rate_row * (size - done).astype(F32)) * term
                if step:
                    gone = jnp.maximum(reached - done, 0).astype(F32)
                    state = state + jnp.where(source < ch_at, jnp.exp(-rate_row * gone) * term, 0.0)
            states[at : at + 1, :] = state
            finals[at : at + 1, :] = final
    own_columns = pl.ds(pl.multiple_of(ch_at * plan.narrow, plan.narrow), plan.narrow)
    outputs["final"][...] = finals[:, own_columns]

    both_output = held["both_output"]
    for slot in range(slots):

        def wkv_step(index, carry, slot=slot):
            spot = tiles_of(slot, index)
            earlier, _, _ = counts(slot, (TILE, width), index * TILE)
            faded = jnp.exp(-rate_row * earlier)
            num = wide["num"][spot, :] + faded * states[slot : slot + 1, :]
            den = wide["den"][spot, :] + faded * states[slots + slot : slots + slot + 1, :]
            wide["num"][spot, :] = num
            wide["den"][spot, :] = den
            bonus = jnp.exp(time_first[...] + key_ref[spot, :].astype(F32))
            wkv = (num + bonus * value_ref[spot, :].astype(F32)) / (den + bonus)
            sent = wkv.astype(BF16).astype(F32)
            both_output[spot, :] = (wide["sigmoid"][spot, :] * sent).astype(BF16)
            return carry

        lax.fori_loop(0, steps_in_slot, wkv_step, 0)
    exchanges["output"] = [
        copies.start(
            both_output.at[pl.ds(0, rows), :], both_output.at[pl.ds(rows, rows), :], partner
        )
    ]

    def store_middle(columns, product):
        wide["middle"][:, columns] = tokens[:, columns].astype(F32) + product

    matmul(own("output"), panels.take(), NN, store_middle)
    panels.release()

    gain_ffn, bias_ffn = inputs["gain_ffn"], inputs["bias_ffn"]
    factor_ffn = held["factor_ffn"]
    for slot in range(slots):
        last = wide["middle"][slot * length + length - 8 : slot * length + length, :]
        unit, _ = normalize(last)
        edges_out[1, slot : slot + 1, :] = (unit * gain_ffn[...] + bias_ffn[...])[7:, :]
    edge_copy = copies.start(edges_out.at[1], edges_in.at[1], after)

    def unit_step(index, carry):
        spot = pl.ds(pl.multiple_of(index * TILE, TILE), TILE)
        unit, factor = normalize(wide["middle"][spot, :])
        wide["unit"][spot, :] = unit
        factor_ffn[spot, :] = jnp.broadcast_to(factor, (TILE, 128))
        return carry

    lax.fori_loop(0, rows // TILE, unit_step, 0)
    blends = [inputs["blend_key"], inputs["blend_gate"]]
    both_blend = [held["both_expand"], held["both_gate"]]

    def blend_tile(slot, index, carry):
        spot = tiles_of(slot, index)
        normed = wide["unit"][spot, :] * gain_ffn[...] + bias_ffn[...]
        earlier = shift_down(normed, carry)
        wide["gap"][spot, :] = normed - earlier
        for weights, target in zip(blends, both_blend):
            target[spot, :] = blend(normed, earlier, weights[...]).astype(BF16)

    for slot in range(slots):

        def blend_step(index, carry, slot=slot):
            last = wide["unit"][last_row_before(slot, index), :][15:, :]
            blend_tile(slot, index, last * gain_ffn[...] + bias_ffn[...])
            return carry

        lax.fori_loop(1, steps_in_slot, blend_step, 0)
    edge_copy.wait()
    for slot in range(slots):
        blend_tile(slot, 0, edges_in[1, slot : slot + 1, :] * keep_edge)
    both_expand, both_gate = held["both_expand"], held["both_gate"]

    def block_of(ref, index):
        return ref.at[pl.ds(index * rows, rows), :]

    exchanges["expand"] = [
        copies.start(block_of(both_expand, 0), block_of(both_expand, 1), partner)
    ]
    across = []
    for step in range(1, sizes["x"]):
        there = device_at(moved(place, sizes, "x", step))
        across.append(
            copies.start(block_of(both_expand, 0), block_of(both_expand, 2 * step), there)
        )
    exchanges["gate"] = [copies.start(block_of(both_gate, 0), block_of(both_gate, 1), partner)]

    both_hidden = held["both_hidden"]
    exchanges["hidden"] = []
    for index in range(panel_count):

        def store_hidden(columns, product, index=index):
            positive = jnp.maximum(product, 0.0)
            start = pl.multiple_of(columns.start + index * width, MATMUL_WIDE)
            both_hidden[first_rows, pl.ds(start, MATMUL_WIDE)] = (positive * positive).astype(BF16)

        matmul(own("expand"), panels.take(), NN, store_hidden)
        panels.release()
        part = pl.ds(index * width, width)
        exchanges["hidden"].append(
            copies.start(
                both_hidden.at[pl.ds(0, rows), part],
                both_hidden.at[pl.ds(rows, rows), part],
                partner,
            )
        )

        def add_contracted(columns, product, index=index):
            if index:
                product = product + wide["total"][:, columns]
            wide["total"][:, columns] = product

        matmul(both_hidden.at[pl.ds(0, rows), part], panels.take(), NN, add_contracted)
        panels.release()

    grad_contracted, grad_logit = held["rows_0"], held["rows_1"]

    def finish_forward(columns, product):
        gate = jax.nn.sigmoid(product)
        contracted = wide["total"][:, columns]
        inside = tall_mask(MATMUL_WIDE)
        mixed = wide["middle"][:, columns] + gate * contracted
        outputs["mixed_out"][:, columns] = jnp.where(inside, mixed, 0.0).astype(BF16)
        grad = jnp.where(inside, grad_out[:, columns].astype(F32), 0.0)
        grad_contracted[:, columns] = (grad * gate).astype(BF16)
        grad_logit[:, columns] = (grad * contracted * gate * (1.0 - gate)).astype(BF16)

    matmul(own("gate"), panels.take(), NN, finish_forward)
    panels.release()

    def hand_over(name, source):
        target = held["back_" + name]
        part = plan.narrow
        exchanges["back_" + name] = []
        for x_at in range(sizes["x"]):
            theirs = pl.multiple_of((x_at * 2 + 1 - place["k"]) * part, part)
            mine = pl.multiple_of((x_at * 2 + place["k"]) * part, part)
            spot = pl.ds(x_at * part, part)
            exchanges["back_" + name].append(
                copies.start(
                    source.at[:, pl.ds(theirs, part)],
                    target.at[pl.ds(rows, rows), spot],
                    partner,
                )
            )
            target[first_rows, spot] = source[:, pl.ds(mine, part)]

    def settle(*wanted):
        for name in wanted:
            for copy in exchanges.pop(name):
                copy.wait()

    grad_expanded, their_expanded = held["grad_expanded"], held["their_expanded"]

    def maker(piece):
        name, short_name, height, row_cut, breadth, column_cut = piece
        first = plan.orders[short_name][0]
        left = held["both_" + ("hidden" if name == "contract" else name)]
        row_step = plan.tall if name == "contract" else plan.short
        if name == "expand":
            rights = (
                (first_rows, grad_expanded, lambda at: ch_at * plan.broad + column_cut),
                (slice(rows, ch_size * rows), their_expanded, lambda at: column_cut),
            )
        else:
            rights = ((slice(None), held["back_" + name], lambda at: at * plan.narrow),)
        kept = [a for a in AXES if a in plan.orders[short_name] and a != first]

        def along(axis, coordinate):
            return [coordinate] if axis == first else range(sizes[axis])

        def make(coordinate, emit):
            places = [(l, y) for l in along("l", coordinate) for y in along("y", coordinate)]
            columns = [0] if name == "expand" else along("x", coordinate)

            def step(h, carry):
                starts = [((h * 2 + l) * 2 + y) * row_step + row_cut for l, y in places]
                spans = [(start, height) for start in starts]
                if row_step == height and first in "xlh":
                    spans = [(starts[0], len(starts) * height)]
                value = None
                for part, right, column_of in rights:
                    a = [
                        left[part, pl.ds(pl.multiple_of(start, math.gcd(span, 512)), span)]
                        for start, span in spans
                    ]
                    b = [
                        right[:, pl.ds(pl.multiple_of(column_of(x), breadth), breadth)]
                        for x in columns
                    ]
                    a = jnp.concatenate(a, axis=1) if len(a) > 1 else a[0]
                    b = jnp.concatenate(b, axis=1) if len(b) > 1 else b[0]
                    product = dot(a, b, TN)
                    value = product if value is None else value + product
                for index, (l, y) in enumerate(places):
                    rows_of = value[index * height : (index + 1) * height, :]
                    for x in columns:
                        at = 0 if first == "x" else x
                        block = rows_of[:, at * breadth : (at + 1) * breadth]
                        where = {"h": h, "l": l, "y": y, "x": x}
                        emit(tuple(where[a] for a in kept), block)
                return carry

            if first == "h":
                step(coordinate, 0)
            else:
                lax.fori_loop(0, sizes["h"], step, 0)

        return make

    pieces = {}
    for piece in plan.pieces:
        name, short_name, height, row_cut, breadth, column_cut = piece
        order_of = plan.orders[short_name]
        out_ref = outputs["grad_" + name].at[
            pl.ds(row_cut, height), pl.ds(column_cut, breadth)
        ]
        landings = [held["landing_" + short_name + str(stage)] for stage in range(len(order_of))]
        pieces[short_name] = Piece(
            maker(piece),
            order_of,
            sizes,
            place,
            copies,
            held["held_" + short_name],
            landings,
            out_ref,
        )

    def start_pieces(prefix):
        for short_name, piece in pieces.items():
            if short_name.startswith(prefix):
                piece.start()

    vector_in = held["vector_in"]
    vector_parts = held["vector_parts"]
    span = plan.vector_span
    scattered = span < width
    vector_queue = {"left": list("kxs" if scattered else "kxylh"), "open": [], "slot": 0}

    def part_of(index):
        return vectors.at[:, pl.ds(pl.multiple_of(index * span, span), span)]

    def start_vectors():
        axis = vector_queue["left"].pop(0)
        if axis == "s":
            for step in range(1, plan.seq):
                there = lax.rem(seq_at + step, plan.seq)
                target = vector_parts.at[step - 1]
                copy = copies.start(part_of(there), target, (there, ch_at))
                vector_queue["open"].append((copy, None))
            return
        for step in range(1, sizes[axis]):
            there = device_at(moved(place, sizes, axis, step))
            copy = copies.start(vectors, vector_in.at[vector_queue["slot"]], there)
            vector_queue["open"].append((copy, vector_queue["slot"]))
            vector_queue["slot"] += 1

    def pump_vectors():
        found, vector_queue["open"] = vector_queue["open"], []
        for copy, _ in found:
            copy.wait()
        for _, slot in found:
            if slot is not None:
                vectors[...] += vector_in[slot]
        if vector_queue["left"]:
            start_vectors()
        elif found:
            total = part_of(seq_at)[...] if scattered else vectors[...]
            for step in range(plan.seq - 1 if scattered else 0):
                total = total + vector_parts[step]
            outputs["vectors"][...] = total

    def pump(point, finish_mix=None):
        for short_name in PUMPS[point]:
            if short_name == "!":
                finish_mix()
                continue
            if short_name[0] == "E":
                if short_name in exchanges:
                    start_expand(int(short_name[1:]))
                continue
            if short_name == "*":
                pump_vectors()
                continue
            piece = pieces.get(short_name)
            if piece is not None and piece.copies:
                piece.advance()

    hand_over("contract", grad_contracted)
    hand_over("gate", grad_logit)
    for index in range(panel_count):

        def store_expanded(columns, product, index=index):
            start = pl.multiple_of(columns.start + index * width, MATMUL_WIDE)
            spot = pl.ds(start, MATMUL_WIDE)
            positive = jnp.sqrt(both_hidden[first_rows, spot].astype(F32))
            grad_expanded[:, spot] = (product * 2.0 * positive).astype(BF16)

        matmul(grad_contracted, panels.take(), NT, store_expanded)
        panels.release()
        if index == 0:
            settle("hidden", "back_contract")
            start_pieces("c")
    for step, copy in enumerate(across, 1):
        copy.wait()
        exchanges["expand"].append(
            copies.start(
                block_of(both_expand, 2 * step), block_of(both_expand, 2 * step + 1), partner
            )
        )

    def send_expanded(cut):
        if cut >= plan.expand_cuts:
            return
        part = plan.broad // plan.expand_cuts
        found = exchanges["E" + str(cut)] = []
        targets = [({**place, "k": 1 - place["k"]}, 0)]
        for step in range(1, sizes["x"]):
            there = moved(place, sizes, "x", step)
            targets.append((there, 2 * step - 1))
            targets.append(({**there, "k": 1 - place["k"]}, 2 * step))
        for there, slot in targets:
            start = (there["x"] * 2 + there["k"]) * plan.broad + cut * part
            found.append(
                copies.start(
                    grad_expanded.at[:, pl.ds(pl.multiple_of(start, part), part)],
                    their_expanded.at[pl.ds(slot * rows, rows), pl.ds(cut * part, part)],
                    device_at(there),
                )
            )

    def start_expand(cut):
        if "expand" in exchanges:
            settle("expand")
        settle("E" + str(cut))
        pieces["e" + str(cut)].start()

    send_expanded(0)
    pump(0)
    for index in range(panel_count):

        def add_expand(columns, product, index=index):
            if index:
                product = product + wide["total"][:, columns]
            wide["total"][:, columns] = product

        matmul(
            grad_expanded,
            panels.take(),
            NT,
            add_expand,
            left_columns=pl.ds(index * width, width),
        )
        panels.release()

    def store_gate(columns, product):
        wide["middle"][:, columns] = product

    matmul(grad_logit, panels.take(), NT, store_gate)
    panels.release()

    for slot in range(slots):
        spot = slice(slot * length, slot * length + 8)
        edge = wide["total"][spot, :] * (1.0 - blends[0][...])
        edge = edge + wide["middle"][spot, :] * (1.0 - blends[1][...])
        edges_out[2, slot : slot + 1, :] = edge[:1, :]
    edge_copy = copies.start(edges_out.at[2], edges_in.at[2], before)
    send_expanded(1)
    settle("gate", "back_gate")
    start_pieces("g")
    pump(1)
    grad_branch = held["rows_2"]

    def first_row_after(slot, index):
        return pl.ds(pl.multiple_of(slot * length + (index + 1) * TILE, 8), 8)

    def ffn_back_earlier(spot):
        earlier = wide["total"][spot, :] * (1.0 - blends[0][...])
        return earlier + wide["middle"][spot, :] * (1.0 - blends[1][...])

    def ffn_back_tile(slot, index, carry):
        spot = tiles_of(slot, index)
        in_expand, in_gate = wide["total"][spot, :], wide["middle"][spot, :]
        gap = wide["gap"][spot, :]
        unit = wide["unit"][spot, :]
        add_vector("blend_key", in_expand * gap)
        add_vector("blend_gate", in_gate * gap)
        earlier = ffn_back_earlier(spot)
        grad_normed = in_expand * blends[0][...] + in_gate * blends[1][...]
        grad_normed = grad_normed + shift_up(earlier, carry)
        add_vector("gain_ffn", grad_normed * unit)
        add_vector("bias_ffn", grad_normed)
        scaled = grad_normed * gain_ffn[...]
        centered = scaled - jnp.mean(scaled, axis=-1, keepdims=True)
        centered = centered - unit * jnp.mean(scaled * unit, axis=-1, keepdims=True)
        _, _, filled = counts(slot, (TILE, width), index * TILE)
        grad = jnp.where(filled, grad_out[spot, :].astype(F32), 0.0)
        grad = grad + factor_ffn[spot, :1] * centered
        wide["total"][spot, :] = grad
        grad_branch[spot, :] = grad.astype(BF16)

    for slot in range(slots):

        def ffn_back_step(index, carry, slot=slot):
            ffn_back_tile(slot, index, ffn_back_earlier(first_row_after(slot, index))[:1, :])
            return carry

        lax.fori_loop(0, steps_in_slot - 1, ffn_back_step, 0)
    edge_copy.wait()
    for slot in range(slots):
        ffn_back_tile(slot, steps_in_slot - 1, edges_in[2, slot : slot + 1, :] * keep_next)

    hand_over("output", grad_branch)
    pump(2)
    grad_recept = held["rows_3"]

    def gated_back(columns, product):
        gate = wide["sigmoid"][:, columns]
        bonus = jnp.exp(time_first[:, columns] + key_ref[:, columns].astype(F32))
        norm = wide["den"][:, columns] + bonus
        wkv = (wide["num"][:, columns] + bonus * value_ref[:, columns].astype(F32)) / norm
        sent = wkv.astype(BF16).astype(F32)
        grad_wkv = (product * gate).astype(BF16).astype(F32)
        grad_recept[:, columns] = (product * sent * gate * (1.0 - gate)).astype(BF16)
        upper_part = grad_wkv / norm
        wide["middle"][:, columns] = upper_part
        wide["gap"][:, columns] = -upper_part * wkv

    matmul(grad_branch, panels.take(), NT, gated_back)
    panels.release()
    hand_over("recept", grad_recept)
    pump(3)

    for slot in range(slots):

        def adjoint_step(index, carry, slot=slot):
            columns = pl.ds(pl.multiple_of(index * WIDE, WIDE), WIDE)
            spot = pl.ds(slot * length, length)
            rate = jnp.exp(time_decay[:, columns])
            earlier, upto, _ = counts(slot, (length, WIDE), 0)
            faded = jnp.exp(-rate * earlier)
            raised = jnp.exp(rate * upto)
            for pair, (source, target) in enumerate((("middle", "sigmoid"), ("gap", "unit"))):
                terms = faded * wide[source][spot, columns]
                wide[target][spot, columns] = raised * triangle(upper, terms)
                at = pair * slots + slot
                sums_out[1, at : at + 1, columns] = jnp.sum(terms, axis=0, keepdims=True)
            return carry

        lax.fori_loop(0, width // WIDE, adjoint_step, 0)
    sum_copies = share(1)
    send_expanded(2)
    send_expanded(3)
    settle("output", "back_output")
    start_pieces("o")
    settle("recept", "back_recept")
    start_pieces("r")
    pump(4)
    for copy in sum_copies:
        copy.wait()
    later = held["later"]
    later[...] = jnp.zeros_like(later)
    for slot in range(slots):
        size = lengths[slot]
        done = jnp.minimum(size, (ch_at + 1) * length)
        for pair in range(2):
            at = pair * slots + slot
            total = jnp.zeros((1, width), F32)
            for step in range(1, ch_size):
                source = lax.rem(ch_at + ch_size - step, ch_size)
                reached = jnp.minimum(size, source * length)
                gone = jnp.maximum(reached - done, 0).astype(F32)
                term = sums_in[1, step - 1, at : at + 1, :]
                total = total + jnp.where(source > ch_at, jnp.exp(-rate_row * gone) * term, 0.0)
            later[at : at + 1, :] = total

    grad_key, grad_value = held["rows_0"], held["rows_1"]
    for slot in range(slots):

        def wkv_back_step(index, carry, slot=slot):
            spot = tiles_of(slot, index)
            _, upto, filled = counts(slot, (TILE, width), index * TILE)
            left = filled_here[slot].astype(F32) - upto
            faded = jnp.exp(-rate_row * left)
            adj_num = wide["sigmoid"][spot, :] + faded * later[slot : slot + 1, :]
            adj_den = wide["unit"][spot, :] + faded * later[slots + slot : slots + slot + 1, :]
            keys, values = key_ref[spot, :].astype(F32), value_ref[spot, :].astype(F32)
            bonus = jnp.exp(time_first[...] + keys)
            weight = jnp.where(filled, jnp.exp(keys), 0.0)
            upper_part, lower_part = wide["middle"][spot, :], wide["gap"][spot, :]
            direct = (upper_part * values + lower_part) * bonus
            grad_value[spot, :] = (upper_part * bonus + weight * adj_num).astype(BF16)
            grad_key[spot, :] = (direct + weight * (adj_num * values + adj_den)).astype(BF16)
            add_vector("time_first", direct)
            decay = adj_num * wide["num"][spot, :] + adj_den * wide["den"][spot, :]
            add_vector("time_decay", jnp.where(filled, decay, 0.0))
            return carry

        lax.fori_loop(0, steps_in_slot, wkv_back_step, 0)
    decay_at = VECTORS.index("time_decay")
    vectors[decay_at : decay_at + 1, :] *= -rate_row * jnp.exp(-rate_row)

    hand_over("key", grad_key)
    hand_over("value", grad_value)
    pump(5)

    def keeper(name):
        def keep(columns, product):
            wide[name][:, columns] = product

        return keep

    for source, name in ((grad_key, "sigmoid"), (grad_value, "unit"), (grad_recept, "gap")):
        matmul(source, panels.take(), NT, keeper(name))
        panels.release()
    in_names = ("sigmoid", "unit", "gap")
    for slot in range(slots):
        spot = slice(slot * length, slot * length + 8)
        edge = jnp.zeros((8, width), F32)
        for name, weights in zip(in_names, mixes):
            edge = edge + wide[name][spot, :] * (1.0 - weights[...])
        edges_out[3, slot : slot + 1, :] = edge[:1, :]
    edge_copy = copies.start(edges_out.at[3], edges_in.at[3], before)
    for name in ("key", "value"):
        settle(name, "back_" + name)
        start_pieces(name[0])
    pump(6)

    in_carry = [edges_in[0, slot : slot + 1, :] for slot in range(slots)]
    vector_names = ("mix_key", "mix_value", "mix_recept")

    def mix_back_earlier(spot):
        earlier = wide[in_names[0]][spot, :] * (1.0 - mixes[0][...])
        for name, weights in zip(in_names[1:], mixes[1:]):
            earlier = earlier + wide[name][spot, :] * (1.0 - weights[...])
        return earlier

    def mix_back_tile(slot, index, before_row, after_row):
        spot = tiles_of(slot, index)
        unit, factor = normalize(tokens[spot, :].astype(F32))
        normed = unit * gain_mix[...] + bias_mix[...]
        gap = normed - shift_down(normed, before_row)
        grad_normed = shift_up(mix_back_earlier(spot), after_row)
        for name, weights, vector in zip(in_names, mixes, vector_names):
            grad = wide[name][spot, :]
            add_vector(vector, grad * gap)
            grad_normed = grad_normed + grad * weights[...]
        add_vector("gain_mix", grad_normed * unit)
        add_vector("bias_mix", grad_normed)
        scaled = grad_normed * gain_mix[...]
        centered = scaled - jnp.mean(scaled, axis=-1, keepdims=True)
        centered = centered - unit * jnp.mean(scaled * unit, axis=-1, keepdims=True)
        grad = wide["total"][spot, :] + factor * centered
        outputs["grad_tokens"][spot, :] = grad.astype(BF16)

    def next_row(slot, index):
        return mix_back_earlier(first_row_after(slot, index))[:1, :]

    last_tile = steps_in_slot - 1
    for slot in range(slots):

        def mix_back_step(index, carry, slot=slot):
            mix_back_tile(slot, index, mix_carry(slot, index), next_row(slot, index))
            return carry

        lax.fori_loop(1, last_tile, mix_back_step, 0)
        if last_tile:
            mix_back_tile(slot, 0, in_carry[slot], next_row(slot, 0))
    def finish_mix():
        edge_copy.wait()
        for slot in range(slots):
            after_row = edges_in[3, slot : slot + 1, :] * keep_next
            before_row = mix_carry(slot, last_tile) if last_tile else in_carry[slot]
            mix_back_tile(slot, last_tile, before_row, after_row)
        start_vectors()

    pump(7, finish_mix)
    for cut in range(plan.expand_cuts):
        if "E" + str(cut) in exchanges:
            start_expand(cut)
    while any(piece.copies for piece in pieces.values()):
        for piece in pieces.values():
            if piece.copies:
                piece.advance()
    while vector_queue["open"]:
        pump_vectors()


LARGE = tuple(name for name in OUTPUTS if name not in ("final", "vectors"))


def place_outputs(plan, *refs):
    count = len(LARGE)
    refs = list(refs)

    def take(number):
        return [refs.pop(0) for _ in range(number)]

    sources, (final, vectors) = take(count), take(2)
    targets, finals, parts = take(count), take(2), take(len(VECTORS))
    buffers, (sems,) = take(count), take(1)
    loads, stores = [], []
    for index in range(count):
        loads.append(pltpu.make_async_copy(sources[index], buffers[index], sems.at[0, index]))
        stores.append(pltpu.make_async_copy(buffers[index], targets[index], sems.at[1, index]))
        loads[-1].start()
    slots = plan.slots
    for index, target in enumerate(finals):
        target[...] = final[index * slots : (index + 1) * slots, :]
    part = plan.width // (plan.seq * plan.ch)
    at = lax.axis_index("ch") * part
    span = plan.vector_span
    if span == plan.width:
        at = at + lax.axis_index("seq") * plan.short
    turned = pltpu.roll(vectors[...], lax.rem(span - at, span), 1)
    for index, target in enumerate(parts):
        target[...] = turned[index, :part]
    for load, store in zip(loads, stores):
        load.wait()
        store.start()
    for store in stores:
        store.wait()


def body(*arguments):
    values = dict(zip(INPUTS, arguments))
    plan = Plan(values["tokens"], values["w_expand"])
    rows, width = plan.rows, plan.width
    operands, specs = [], []
    for name in INPUTS:
        value = values[name]
        space = pltpu.VMEM
        if name in ("tokens", "grad_out"):
            value = value.reshape(rows, width)
        elif name == "lengths":
            space = pltpu.SMEM
        elif name.startswith("w_"):
            space = pl.ANY
        elif value.ndim == 1:
            value = value.reshape(1, width)
        operands.append(value)
        specs.append(pl.BlockSpec(memory_space=space))
    outs = {
        "mixed_out": ((rows, width), BF16),
        "grad_tokens": ((rows, width), BF16),
        "final": ((8, plan.narrow), F32),
        "grad_key": ((plan.short, plan.narrow), F32),
        "grad_value": ((plan.short, plan.narrow), F32),
        "grad_recept": ((plan.short, plan.narrow), F32),
        "grad_output": ((plan.short, plan.narrow), F32),
        "grad_expand": ((plan.short, plan.broad), F32),
        "grad_contract": ((plan.tall, plan.narrow), F32),
        "grad_gate": ((plan.short, plan.narrow), F32),
        "vectors": ((16, plan.vector_span), F32),
    }
    results = pl.pallas_call(
        functools.partial(layer_kernel, plan),
        out_shape=[jax.ShapeDtypeStruct(*outs[name]) for name in OUTPUTS],
        in_specs=specs,
        out_specs=[pl.BlockSpec(memory_space=pltpu.VMEM)] * len(OUTPUTS),
        scratch_shapes=list(plan.shapes.values()),
        compiler_params=pltpu.CompilerParams(
            collective_id=0, has_side_effects=True, vmem_limit_bytes=63 * 2**20
        ),
    )(*operands)
    part = width // (plan.seq * plan.ch)
    slots = plan.slots
    got = dict(zip(OUTPUTS, results))
    vmem, hbm = pl.BlockSpec(memory_space=pltpu.VMEM), pl.BlockSpec(memory_space=pl.ANY)
    shapes = [outs[name] for name in LARGE] + [((slots, plan.narrow), F32)] * 2
    shapes += [((part,), F32)] * len(VECTORS)
    results = pl.pallas_call(
        functools.partial(place_outputs, plan),
        out_shape=[jax.ShapeDtypeStruct(*shape) for shape in shapes],
        in_specs=[hbm] * len(LARGE) + [vmem] * 2,
        out_specs=[hbm] * len(LARGE) + [vmem] * (2 + len(VECTORS)),
        scratch_shapes=[pltpu.VMEM(*outs[name]) for name in LARGE]
        + [pltpu.SemaphoreType.DMA((2, len(LARGE)))],
        compiler_params=pltpu.CompilerParams(vmem_limit_bytes=60 * 2**20),
    )(*[got[name] for name in LARGE], got["final"], got["vectors"])
    mixed_out, grad_tokens, *weights = results[: len(LARGE)]
    shape = values["tokens"].shape
    return (
        mixed_out.reshape(shape),
        grad_tokens.reshape(shape),
        *results[len(LARGE) : len(LARGE) + 2],
        *weights,
        *results[len(LARGE) + 2 :],
    )


def solution(mesh):
    split, copied = P("seq", "ch", None), P()
    placed = (split, split, P("seq"), P("seq", None), P("seq", None)) + (copied,) * 18
    both = P("seq", "ch")
    return jax.shard_map(
        body,
        mesh=mesh,
        in_specs=placed,
        out_specs=(split, split) + (both,) * 9 + (P(("seq", "ch")),) * 11,
        check_vma=False,
    )
```

```python
import functools
import math

import jax
import jax.numpy as jnp
from jax import lax
from jax.experimental import pallas as pl
from jax.experimental.pallas import tpu as pltpu
from jax.sharding import PartitionSpec as P

EPS = 1e-05
MESH = pl.DeviceIdType.MESH
AXES = "hlyx"
F32 = jnp.float32
BF16 = jnp.bfloat16
TILE = 64
WIDE = 512
MATMUL_WIDE = 1024
SLOTS_OF_WEIGHTS = 3

ORDERS = {
    "c0": "yxlh",
    "c1": "lyhx",
    "c2": "ylhx",
    "c3": "lxyh",
    "e0": "ylh",
    "e1": "ylh",
    "e2": "ylh",
    "e3": "ylh",
    "g": "lxyh",
    "o": "ylhx",
    "k": "xylh",
    "v": "xylh",
    "r": "xylh",
}
PUMPS = (
    (),
    (),
    (
        "c0", "c1", "E0",
    ),
    (),
    (),
    (
        "E1", "c2", "c0",
    ),
    (
        "c3", "c1", "E2",
    ),
    (
        "e0", "g", "E3", "c2", "c0", "o", "c1", "r", "!", "e0", "e1", "*", "c2", "c0", "e2", "o",
        "k", "e0", "e3", "e1", "e2", "r", "o", "v", "e3", "e1", "k", "c3", "e2", "r", "e3", "v",
        "k", "c3", "g", "c1", "r", "*", "v", "c2", "g", "o", "*", "k", "c3", "v", "g",
    ),
)

NN = (((1,), (0,)), ((), ()))
NT = (((1,), (1,)), ((), ()))
TN = (((0,), (0,)), ((), ()))


def dot(left, right, how):
    return lax.dot_general(left, right, how, preferred_element_type=F32)


def axis_sizes():
    seq_size, ch_size = lax.axis_size("seq"), lax.axis_size("ch")
    return {"k": 2, "x": ch_size // 2, "y": 2, "l": 2, "h": seq_size // 4}


def coordinates():
    seq_at, ch_at = lax.axis_index("seq"), lax.axis_index("ch")
    return {
        "h": seq_at // 4,
        "l": seq_at // 2 % 2,
        "y": seq_at % 2,
        "x": ch_at // 2,
        "k": ch_at % 2,
    }


def device_at(place):
    return (place["h"] * 4 + place["l"] * 2 + place["y"], place["x"] * 2 + place["k"])


def moved(place, sizes, axis, step):
    return {**place, axis: lax.rem(place[axis] + step, sizes[axis])}


class Copies:
    def __init__(self, sends, receives):
        self.sends, self.receives, self.used = sends, receives, 0
        self.open = []

    def start(self, source, target, device):
        copy = pltpu.make_async_remote_copy(
            src_ref=source,
            dst_ref=target,
            send_sem=self.sends.at[self.used],
            recv_sem=self.receives.at[self.used],
            device_id=device,
            device_id_type=MESH,
        )
        self.used += 1
        copy.start()
        return copy


class Piece:
    def __init__(self, make, order, sizes, place, copies, held, landings, out_ref):
        self.make, self.order, self.sizes, self.place = make, order, sizes, place
        self.remote, self.held, self.landings, self.out_ref = copies, held, landings, out_ref
        self.axes = [axis for axis in AXES if axis in order]
        self.stage = 0
        self.copies = []

    def start(self):
        axis = self.order[self.stage]
        at = self.axes.index(axis)
        for step in range(1, self.sizes[axis]):
            there = moved(self.place, self.sizes, axis, step)
            if self.stage == 0:

                def keep(where, value, slot=step - 1):
                    self.held[(slot,) + where] = value.astype(BF16)

                self.make(there[axis], keep)
                source = self.held.at[step - 1]
            else:
                source = self.landings[self.stage - 1].at[
                    (0,) + (slice(None),) * at + (there[axis],)
                ]
            self.copies.append(
                self.remote.start(
                    source, self.landings[self.stage].at[step - 1], device_at(there)
                )
            )

    def finish(self):
        axis = self.order[self.stage]
        at = self.axes.index(axis)
        landing = self.landings[self.stage]
        others = self.sizes[axis] - 1
        for copy in self.copies:
            copy.wait()
        self.copies = []
        remaining = [a for a in self.axes if a != axis]
        if self.stage == 0:

            def add(where, value):
                for other in range(others):
                    value = value + landing[(other,) + where].astype(F32)
                landing[(0,) + where] = value.astype(BF16)

            self.make(self.place[axis], add)
        else:
            own = self.landings[self.stage - 1].at[
                (0,) + (slice(None),) * at + (self.place[axis],)
            ]
            lead = tuple(self.sizes[a] for a in remaining)
            rows, columns = landing.shape[-2:]
            tile = math.gcd(rows, max(16, 32768 // columns))
            parts = rows // tile

            def add_tile(index, carry):
                part, rest = index % parts, index // parts
                where = ()
                for size in reversed(lead):
                    where = (rest % size,) + where
                    rest = rest // size
                spot = pl.ds(pl.multiple_of(part * tile, tile), tile)
                where = where + (spot, slice(None))
                total = own[where].astype(F32)
                for other in range(others):
                    total = total + landing[(other,) + where].astype(F32)
                if remaining:
                    landing[(0,) + where] = total.astype(BF16)
                else:
                    self.out_ref[where] = total
                return carry

            lax.fori_loop(0, math.prod(lead) * parts, add_tile, 0)
        self.axes = remaining
        self.stage += 1

    def advance(self):
        self.finish()
        if self.axes:
            self.start()


class Plan:
    def __init__(self, tokens, w_expand):
        self.slots, self.length, self.width = tokens.shape
        self.hidden = w_expand.shape[1]
        self.sizes = sizes = axis_sizes()
        self.seq, self.ch = sizes["h"] * 4, sizes["x"] * 2
        self.rows = self.slots * self.length
        rows, width, hidden = self.rows, self.width, self.hidden
        self.narrow = width // self.ch
        self.broad = hidden // self.ch
        self.short = width // self.seq
        self.tall = hidden // self.seq
        self.vector_span = self.short if self.short % 128 == 0 else width
        half = sizes["x"] * self.narrow
        self.pieces = []
        cuts = 4 if (self.tall // 4) % 128 == 0 else 1
        part = self.tall // cuts
        for cut in range(cuts):
            self.pieces.append(("contract", "c" + str(cut), part, cut * part, self.narrow, 0))
        cuts = 4 if (self.broad // 4) % 128 == 0 else 1
        self.expand_cuts = cuts
        part = self.broad // cuts
        for cut in range(cuts):
            self.pieces.append(("expand", "e" + str(cut), self.short, 0, part, cut * part))
        for name in ("gate", "output", "key", "value", "recept"):
            self.pieces.append((name, name[0], self.short, 0, self.narrow, 0))
        self.orders = {}
        for name, short_name, height, _, _, _ in self.pieces:
            if height % 128 == 0:
                self.orders[short_name] = ORDERS[short_name]
            else:
                self.orders[short_name] = "hly" if name == "expand" else "xylh"
        vmem = pltpu.VMEM
        shapes = {
            "panels": vmem((SLOTS_OF_WEIGHTS, width, width), BF16),
            "both_hidden": vmem((2 * rows, hidden), BF16),
            "grad_expanded": vmem((rows, hidden), BF16),
            "their_expanded": vmem(((self.ch - 1) * rows, self.broad), BF16),
            "both_expand": vmem((self.ch * rows, width), BF16),
            "key": vmem((rows, width), BF16),
            "value": vmem((rows, width), BF16),
            "edges_out": vmem((4, 8, width), F32),
            "edges_in": vmem((4, 8, width), F32),
            "sums_out": vmem((2, 8, width), F32),
            "sums_in": vmem((2, self.ch - 1, 8, width), F32),
            "states": vmem((8, width), F32),
            "finals": vmem((8, width), F32),
            "later": vmem((8, width), F32),
            "factor_ffn": vmem((rows, 128), F32),
            "vectors": vmem((16, width), F32),
            "vector_in": vmem((self.count_vector_slots(), 16, width), F32),
            "vector_parts": vmem((self.seq - 1, 16, self.vector_span), F32),
        }
        for name in ("gate", "output", "key", "value", "recept"):
            shapes["both_" + name] = vmem((2 * rows, width), BF16)
        for name in ("contract", "gate", "output", "key", "value", "recept"):
            shapes["back_" + name] = vmem((2 * rows, half), BF16)
        for index in range(4):
            shapes["rows_" + str(index)] = vmem((rows, width), BF16)
        for name in ("middle", "total", "sigmoid", "num", "den", "unit", "gap"):
            shapes["wide_" + name] = vmem((rows, width), F32)
        copies = 64 + 16 * self.ch
        for name, short_name, height, _, breadth, _ in self.pieces:
            order = self.orders[short_name]
            axes = [axis for axis in AXES if axis in order[1:]]
            lead = tuple(sizes[a] for a in axes)
            shapes["held_" + short_name] = vmem(
                (sizes[order[0]] - 1,) + lead + (height, breadth), BF16
            )
            axes = [axis for axis in AXES if axis in order]
            for stage, axis in enumerate(order):
                axes.remove(axis)
                shape = (sizes[axis] - 1,) + tuple(sizes[a] for a in axes) + (height, breadth)
                shapes["landing_" + short_name + str(stage)] = vmem(shape, BF16)
                copies += sizes[axis] - 1
        copies += self.count_vector_slots() + self.seq
        shapes["sends"] = pltpu.SemaphoreType.DMA((copies,))
        shapes["receives"] = pltpu.SemaphoreType.DMA((copies,))
        shapes["panel_sems"] = pltpu.SemaphoreType.DMA((SLOTS_OF_WEIGHTS,))
        self.shapes = shapes

    def count_vector_slots(self):
        axes = "kx" if self.vector_span < self.width else "kxylh"
        return sum(self.sizes[axis] - 1 for axis in axes)


INPUTS = (
    "tokens",
    "grad_out",
    "lengths",
    "init_num",
    "init_den",
    "w_key",
    "w_value",
    "w_recept",
    "w_output",
    "w_expand",
    "w_contract",
    "w_gate",
    "gain_mix",
    "bias_mix",
    "gain_ffn",
    "bias_ffn",
    "mix_key",
    "mix_value",
    "mix_recept",
    "blend_key",
    "blend_gate",
    "time_decay",
    "time_first",
)
OUTPUTS = (
    "mixed_out",
    "grad_tokens",
    "final",
    "grad_key",
    "grad_value",
    "grad_recept",
    "grad_output",
    "grad_expand",
    "grad_contract",
    "grad_gate",
    "vectors",
)
VECTORS = (
    "gain_mix",
    "bias_mix",
    "gain_ffn",
    "bias_ffn",
    "mix_key",
    "mix_value",
    "mix_recept",
    "blend_key",
    "blend_gate",
    "time_decay",
    "time_first",
)


class Panels:
    def __init__(self, sources, ref, sems):
        self.sources, self.ref, self.sems = sources, ref, sems
        self.used = 0
        for index in range(min(SLOTS_OF_WEIGHTS, len(sources))):
            self.copy(index).start()

    def copy(self, index):
        slot = index % SLOTS_OF_WEIGHTS
        return pltpu.make_async_copy(self.sources[index], self.ref.at[slot], self.sems.at[slot])

    def take(self):
        self.copy(self.used).wait()
        return self.ref.at[self.used % SLOTS_OF_WEIGHTS]

    def release(self):
        index = self.used + SLOTS_OF_WEIGHTS
        if index < len(self.sources):
            self.copy(index).start()
        self.used += 1


def layer_kernel(plan, *all_refs):
    inputs = dict(zip(INPUTS, all_refs))
    outputs = dict(zip(OUTPUTS, all_refs[len(INPUTS) :]))
    held = dict(zip(plan.shapes, all_refs[len(INPUTS) + len(OUTPUTS) :]))
    sizes = plan.sizes
    place = coordinates()
    ch_at = lax.axis_index("ch")
    seq_at = lax.axis_index("seq")
    slots, length, width, rows = plan.slots, plan.length, plan.width, plan.rows
    hidden, ch_size = plan.hidden, plan.ch
    panel_count = hidden // width
    tokens, grad_out, lengths = inputs["tokens"], inputs["grad_out"], inputs["lengths"]
    first_rows = slice(0, rows)
    last_rows = slice(rows, 2 * rows)

    w_expand, w_contract = inputs["w_expand"], inputs["w_contract"]

    def expand_panel(index):
        return w_expand.at[:, pl.ds(index * width, width)]

    def contract_panel(index):
        return w_contract.at[pl.ds(index * width, width), :]

    order = [inputs["w_key"], inputs["w_value"], inputs["w_recept"], inputs["w_output"]]
    for index in range(panel_count):
        order += [expand_panel(index), contract_panel(index)]
    order += [inputs["w_gate"]]
    order += [contract_panel(index) for index in range(panel_count)]
    order += [expand_panel(index) for index in range(panel_count)]
    order += [inputs["w_gate"], inputs["w_output"]]
    order += [inputs["w_key"], inputs["w_value"], inputs["w_recept"]]
    panels = Panels(order, held["panels"], held["panel_sems"])

    barrier = pltpu.get_barrier_semaphore()
    greeted = 0
    for step in range(1, ch_size):
        pl.semaphore_signal(
            barrier,
            inc=1,
            device_id=(seq_at, lax.rem(ch_at + step, ch_size)),
            device_id_type=MESH,
        )
        greeted += 1
    for step in range(1, plan.seq):
        pl.semaphore_signal(
            barrier,
            inc=1,
            device_id=(lax.rem(seq_at + step, plan.seq), ch_at),
            device_id_type=MESH,
        )
        greeted += 1
    copies = Copies(held["sends"], held["receives"])
    partner = device_at({**place, "k": 1 - place["k"]})
    after = (seq_at, lax.rem(ch_at + 1, ch_size))
    before = (seq_at, lax.rem(ch_at + ch_size - 1, ch_size))

    filled_here = [
        jnp.clip(lengths[slot] - ch_at * length, 0, length) for slot in range(slots)
    ]
    vectors = held["vectors"]
    vectors[...] = jnp.zeros_like(vectors)

    def add_vector(name, value):
        at = VECTORS.index(name)
        vectors[at : at + 1, :] += jnp.sum(value, axis=0, keepdims=True)

    def normalize(value):
        center = value - jnp.mean(value, axis=-1, keepdims=True)
        factor = lax.rsqrt(jnp.mean(center * center, axis=-1, keepdims=True) + EPS)
        return center * factor, factor

    def blend(current, earlier, weights):
        return current * weights + earlier * (1.0 - weights)

    def tiles_of(slot, index):
        return pl.ds(pl.multiple_of(slot * length + index * TILE, TILE), TILE)

    row_in_tile = lax.broadcasted_iota(jnp.int32, (TILE, width), 0)

    def shift_down(value, carry):
        return jnp.where(row_in_tile == 0, carry, pltpu.roll(value, 1, 0))

    def shift_up(value, carry):
        return jnp.where(row_in_tile == TILE - 1, carry, pltpu.roll(value, TILE - 1, 0))

    steps_in_slot = length // TILE

    def matmul(left, panel, how, use, left_columns=None):
        def step(index, carry):
            columns = pl.ds(pl.multiple_of(index * MATMUL_WIDE, MATMUL_WIDE), MATMUL_WIDE)
            right = panel[:, columns] if how is NN else panel[columns, :]
            source = left[...] if left_columns is None else left[:, left_columns]
            use(columns, dot(source, right, how))
            return carry

        lax.fori_loop(0, width // MATMUL_WIDE, step, 0)

    def counts(slot, shape, offset):
        at = lax.broadcasted_iota(jnp.int32, shape, 0) + offset
        earlier = jnp.minimum(at, filled_here[slot]).astype(F32)
        upto = jnp.minimum(at + 1, filled_here[slot]).astype(F32)
        return earlier, upto, at < filled_here[slot]

    def tall_mask(columns):
        at = lax.broadcasted_iota(jnp.int32, (rows, columns), 0)
        inside = at < filled_here[0]
        for slot in range(1, slots):
            shifted = at - slot * length
            inside = inside | ((shifted >= 0) & (shifted < filled_here[slot]))
        return inside

    edges_out, edges_in = held["edges_out"], held["edges_in"]
    edges_out[...] = jnp.zeros_like(edges_out)
    for slot in range(slots):
        last = tokens[slot * length + length - 16 : slot * length + length, :].astype(F32)
        edges_out[0, slot : slot + 1, :] = last[15:, :]
    pl.semaphore_wait(barrier, greeted)
    edge_copy = copies.start(edges_out.at[0], edges_in.at[0], after)

    gain_mix, bias_mix = inputs["gain_mix"], inputs["bias_mix"]
    keep_edge = jnp.where(ch_at > 0, 1.0, 0.0)
    keep_next = jnp.where(ch_at < ch_size - 1, 1.0, 0.0)

    mixes = [inputs["mix_key"], inputs["mix_value"], inputs["mix_recept"]]
    both_mix = [held["both_key"], held["both_value"], held["both_recept"]]

    def last_row_before(slot, index):
        return pl.ds(pl.multiple_of(slot * length + index * TILE - 16, 16), 16)

    def mix_tile(slot, index, carry):
        spot = tiles_of(slot, index)
        unit, _ = normalize(tokens[spot, :].astype(F32))
        normed = unit * gain_mix[...] + bias_mix[...]
        earlier = shift_down(normed, carry)
        for weights, target in zip(mixes, both_mix):
            target[spot, :] = blend(normed, earlier, weights[...]).astype(BF16)

    def mix_carry(slot, index):
        unit, _ = normalize(tokens[last_row_before(slot, index), :].astype(F32))
        return (unit * gain_mix[...] + bias_mix[...])[15:, :]

    for slot in range(slots):

        def mix_step(index, carry, slot=slot):
            mix_tile(slot, index, mix_carry(slot, index))
            return carry

        lax.fori_loop(1, steps_in_slot, mix_step, 0)
    edge_copy.wait()
    edge_unit, _ = normalize(edges_in[0])
    edges_in[0] = (edge_unit * gain_mix[...] + bias_mix[...]) * keep_edge
    for slot in range(slots):
        mix_tile(slot, 0, edges_in[0, slot : slot + 1, :])
    exchanges = {}
    for name in ("key", "value", "recept"):
        ref = held["both_" + name]
        exchanges[name] = [
            copies.start(ref.at[pl.ds(0, rows), :], ref.at[pl.ds(rows, rows), :], partner)
        ]

    key_ref, value_ref = held["key"], held["value"]
    wide = {
        name: held["wide_" + name]
        for name in ("middle", "total", "sigmoid", "num", "den", "unit", "gap")
    }

    def own(name):
        return held["both_" + name].at[pl.ds(0, rows), :]

    def store_key(columns, product):
        key_ref[:, columns] = product.astype(BF16)

    def store_value(columns, product):
        value_ref[:, columns] = product.astype(BF16)

    matmul(own("key"), panels.take(), NN, store_key)
    panels.release()
    matmul(own("value"), panels.take(), NN, store_value)
    panels.release()

    time_decay, time_first = inputs["time_decay"], inputs["time_first"]
    square = (length, 3 * length)
    at_row = lax.broadcasted_iota(jnp.int32, square, 0)
    at_column = lax.rem(lax.broadcasted_iota(jnp.int32, square, 1), length)
    lower = jnp.where(at_column < at_row, 1.0, 0.0).astype(BF16)
    upper = jnp.where(at_column > at_row, 1.0, 0.0).astype(BF16)

    def triangle(matrix, value):
        high = value.astype(BF16)
        rest = value - high.astype(F32)
        middle = rest.astype(BF16)
        low = (rest - middle.astype(F32)).astype(BF16)
        return dot(matrix, jnp.concatenate([high, middle, low], axis=0), NN)

    sums_out, sums_in = held["sums_out"], held["sums_in"]
    sums_out[...] = jnp.zeros_like(sums_out)
    for slot in range(slots):

        def local_step(index, carry, slot=slot):
            columns = pl.ds(pl.multiple_of(index * WIDE, WIDE), WIDE)
            spot = pl.ds(slot * length, length)
            rate = jnp.exp(time_decay[:, columns])
            earlier, upto, filled = counts(slot, (length, WIDE), 0)
            stop = rate * filled_here[slot].astype(F32)
            keys = key_ref[spot, columns].astype(F32)
            weight = jnp.where(filled, jnp.exp(rate * upto - stop) * jnp.exp(keys), 0.0)
            payload = weight * value_ref[spot, columns].astype(F32)
            raised = jnp.exp(stop - rate * earlier)
            wide["num"][spot, columns] = raised * triangle(lower, payload)
            wide["den"][spot, columns] = raised * triangle(lower, weight)
            sums_out[0, slot : slot + 1, columns] = jnp.sum(payload, axis=0, keepdims=True)
            at = slots + slot
            sums_out[0, at : at + 1, columns] = jnp.sum(weight, axis=0, keepdims=True)
            return carry

        lax.fori_loop(0, width // WIDE, local_step, 0)

    def share(which):
        return [
            copies.start(
                sums_out.at[which],
                sums_in.at[which, step - 1],
                (seq_at, lax.rem(ch_at + step, ch_size)),
            )
            for step in range(1, ch_size)
        ]

    sum_copies = share(0)

    def store_sigmoid(columns, product):
        wide["sigmoid"][:, columns] = jax.nn.sigmoid(product)

    matmul(own("recept"), panels.take(), NN, store_sigmoid)
    panels.release()
    for copy in sum_copies:
        copy.wait()

    rate_row = jnp.exp(time_decay[...])
    states, finals = held["states"], held["finals"]
    states[...] = jnp.zeros_like(states)
    finals[...] = jnp.zeros_like(finals)
    for slot in range(slots):
        size = lengths[slot]
        reached = jnp.minimum(size, ch_at * length)
        for pair, initial in enumerate((inputs["init_num"], inputs["init_den"])):
            at = pair * slots + slot
            start_row = initial[slot : slot + 1, :]
            state = jnp.exp(-rate_row * reached.astype(F32)) * start_row
            final = jnp.exp(-rate_row * size.astype(F32)) * start_row
            for step in range(ch_size):
                source = lax.rem(ch_at + ch_size - step, ch_size)
                done = jnp.minimum(size, (source + 1) * length)
                term = (
                    sums_out[0, at : at + 1, :]
                    if step == 0
                    else sums_in[0, step - 1, at : at + 1, :]
                )
                final = final + jnp.exp(-rate_row * (size - done).astype(F32)) * term
                if step:
                    gone = jnp.maximum(reached - done, 0).astype(F32)
                    state = state + jnp.where(source < ch_at, jnp.exp(-rate_row * gone) * term, 0.0)
            states[at : at + 1, :] = state
            finals[at : at + 1, :] = final
    own_columns = pl.ds(pl.multiple_of(ch_at * plan.narrow, plan.narrow), plan.narrow)
    outputs["final"][...] = finals[:, own_columns]

    both_output = held["both_output"]
    for slot in range(slots):

        def wkv_step(index, carry, slot=slot):
            spot = tiles_of(slot, index)
            earlier, _, _ = counts(slot, (TILE, width), index * TILE)
            faded = jnp.exp(-rate_row * earlier)
            num = wide["num"][spot, :] + faded * states[slot : slot + 1, :]
            den = wide["den"][spot, :] + faded * states[slots + slot : slots + slot + 1, :]
            wide["num"][spot, :] = num
            wide["den"][spot, :] = den
            bonus = jnp.exp(time_first[...] + key_ref[spot, :].astype(F32))
            wkv = (num + bonus * value_ref[spot, :].astype(F32)) / (den + bonus)
            sent = wkv.astype(BF16).astype(F32)
            both_output[spot, :] = (wide["sigmoid"][spot, :] * sent).astype(BF16)
            return carry

        lax.fori_loop(0, steps_in_slot, wkv_step, 0)
    exchanges["output"] = [
        copies.start(
            both_output.at[pl.ds(0, rows), :], both_output.at[pl.ds(rows, rows), :], partner
        )
    ]

    def store_middle(columns, product):
        wide["middle"][:, columns] = tokens[:, columns].astype(F32) + product

    matmul(own("output"), panels.take(), NN, store_middle)
    panels.release()

    gain_ffn, bias_ffn = inputs["gain_ffn"], inputs["bias_ffn"]
    factor_ffn = held["factor_ffn"]
    for slot in range(slots):
        last = wide["middle"][slot * length + length - 8 : slot * length + length, :]
        unit, _ = normalize(last)
        edges_out[1, slot : slot + 1, :] = (unit * gain_ffn[...] + bias_ffn[...])[7:, :]
    edge_copy = copies.start(edges_out.at[1], edges_in.at[1], after)

    def unit_step(index, carry):
        spot = pl.ds(pl.multiple_of(index * TILE, TILE), TILE)
        unit, factor = normalize(wide["middle"][spot, :])
        wide["unit"][spot, :] = unit
        factor_ffn[spot, :] = jnp.broadcast_to(factor, (TILE, 128))
        return carry

    lax.fori_loop(0, rows // TILE, unit_step, 0)
    blends = [inputs["blend_key"], inputs["blend_gate"]]
    both_blend = [held["both_expand"], held["both_gate"]]

    def blend_tile(slot, index, carry):
        spot = tiles_of(slot, index)
        normed = wide["unit"][spot, :] * gain_ffn[...] + bias_ffn[...]
        earlier = shift_down(normed, carry)
        wide["gap"][spot, :] = normed - earlier
        for weights, target in zip(blends, both_blend):
            target[spot, :] = blend(normed, earlier, weights[...]).astype(BF16)

    for slot in range(slots):

        def blend_step(index, carry, slot=slot):
            last = wide["unit"][last_row_before(slot, index), :][15:, :]
            blend_tile(slot, index, last * gain_ffn[...] + bias_ffn[...])
            return carry

        lax.fori_loop(1, steps_in_slot, blend_step, 0)
    edge_copy.wait()
    for slot in range(slots):
        blend_tile(slot, 0, edges_in[1, slot : slot + 1, :] * keep_edge)
    both_expand, both_gate = held["both_expand"], held["both_gate"]

    def block_of(ref, index):
        return ref.at[pl.ds(index * rows, rows), :]

    exchanges["expand"] = [
        copies.start(block_of(both_expand, 0), block_of(both_expand, 1), partner)
    ]
    across = []
    for step in range(1, sizes["x"]):
        there = device_at(moved(place, sizes, "x", step))
        across.append(
            copies.start(block_of(both_expand, 0), block_of(both_expand, 2 * step), there)
        )
    exchanges["gate"] = [copies.start(block_of(both_gate, 0), block_of(both_gate, 1), partner)]

    both_hidden = held["both_hidden"]
    exchanges["hidden"] = []
    for index in range(panel_count):

        def store_hidden(columns, product, index=index):
            positive = jnp.maximum(product, 0.0)
            start = pl.multiple_of(columns.start + index * width, MATMUL_WIDE)
            both_hidden[first_rows, pl.ds(start, MATMUL_WIDE)] = (positive * positive).astype(BF16)

        matmul(own("expand"), panels.take(), NN, store_hidden)
        panels.release()
        part = pl.ds(index * width, width)
        exchanges["hidden"].append(
            copies.start(
                both_hidden.at[pl.ds(0, rows), part],
                both_hidden.at[pl.ds(rows, rows), part],
                partner,
            )
        )

        def add_contracted(columns, product, index=index):
            if index:
                product = product + wide["total"][:, columns]
            wide["total"][:, columns] = product

        matmul(both_hidden.at[pl.ds(0, rows), part], panels.take(), NN, add_contracted)
        panels.release()

    grad_contracted, grad_logit = held["rows_0"], held["rows_1"]

    def finish_forward(columns, product):
        gate = jax.nn.sigmoid(product)
        contracted = wide["total"][:, columns]
        inside = tall_mask(MATMUL_WIDE)
        mixed = wide["middle"][:, columns] + gate * contracted
        outputs["mixed_out"][:, columns] = jnp.where(inside, mixed, 0.0).astype(BF16)
        grad = jnp.where(inside, grad_out[:, columns].astype(F32), 0.0)
        grad_contracted[:, columns] = (grad * gate).astype(BF16)
        grad_logit[:, columns] = (grad * contracted * gate * (1.0 - gate)).astype(BF16)

    matmul(own("gate"), panels.take(), NN, finish_forward)
    panels.release()

    def hand_over(name, source):
        target = held["back_" + name]
        part = plan.narrow
        exchanges["back_" + name] = []
        for x_at in range(sizes["x"]):
            theirs = pl.multiple_of((x_at * 2 + 1 - place["k"]) * part, part)
            mine = pl.multiple_of((x_at * 2 + place["k"]) * part, part)
            spot = pl.ds(x_at * part, part)
            exchanges["back_" + name].append(
                copies.start(
                    source.at[:, pl.ds(theirs, part)],
                    target.at[pl.ds(rows, rows), spot],
                    partner,
                )
            )
            target[first_rows, spot] = source[:, pl.ds(mine, part)]

    def settle(*wanted):
        for name in wanted:
            for copy in exchanges.pop(name):
                copy.wait()

    grad_expanded, their_expanded = held["grad_expanded"], held["their_expanded"]

    def maker(piece):
        name, short_name, height, row_cut, breadth, column_cut = piece
        first = plan.orders[short_name][0]
        left = held["both_" + ("hidden" if name == "contract" else name)]
        row_step = plan.tall if name == "contract" else plan.short
        if name == "expand":
            rights = (
                (first_rows, grad_expanded, lambda at: ch_at * plan.broad + column_cut),
                (slice(rows, ch_size * rows), their_expanded, lambda at: column_cut),
            )
        else:
            rights = ((slice(None), held["back_" + name], lambda at: at * plan.narrow),)
        kept = [a for a in AXES if a in plan.orders[short_name] and a != first]

        def along(axis, coordinate):
            return [coordinate] if axis == first else range(sizes[axis])

        def make(coordinate, emit):
            places = [(l, y) for l in along("l", coordinate) for y in along("y", coordinate)]
            columns = [0] if name == "expand" else along("x", coordinate)

            def step(h, carry):
                starts = [((h * 2 + l) * 2 + y) * row_step + row_cut for l, y in places]
                spans = [(start, height) for start in starts]
                if row_step == height and first in "xlh":
                    spans = [(starts[0], len(starts) * height)]
                value = None
                for part, right, column_of in rights:
                    a = [
                        left[part, pl.ds(pl.multiple_of(start, math.gcd(span, 512)), span)]
                        for start, span in spans
                    ]
                    b = [
                        right[:, pl.ds(pl.multiple_of(column_of(x), breadth), breadth)]
                        for x in columns
                    ]
                    a = jnp.concatenate(a, axis=1) if len(a) > 1 else a[0]
                    b = jnp.concatenate(b, axis=1) if len(b) > 1 else b[0]
                    product = dot(a, b, TN)
                    value = product if value is None else value + product
                for index, (l, y) in enumerate(places):
                    rows_of = value[index * height : (index + 1) * height, :]
                    for x in columns:
                        at = 0 if first == "x" else x
                        block = rows_of[:, at * breadth : (at + 1) * breadth]
                        where = {"h": h, "l": l, "y": y, "x": x}
                        emit(tuple(where[a] for a in kept), block)
                return carry

            if first == "h":
                step(coordinate, 0)
            else:
                lax.fori_loop(0, sizes["h"], step, 0)

        return make

    pieces = {}
    for piece in plan.pieces:
        name, short_name, height, row_cut, breadth, column_cut = piece
        order_of = plan.orders[short_name]
        out_ref = outputs["grad_" + name].at[
            pl.ds(row_cut, height), pl.ds(column_cut, breadth)
        ]
        landings = [held["landing_" + short_name + str(stage)] for stage in range(len(order_of))]
        pieces[short_name] = Piece(
            maker(piece),
            order_of,
            sizes,
            place,
            copies,
            held["held_" + short_name],
            landings,
            out_ref,
        )

    def start_pieces(prefix):
        for short_name, piece in pieces.items():
            if short_name.startswith(prefix):
                piece.start()

    vector_in = held["vector_in"]
    vector_parts = held["vector_parts"]
    span = plan.vector_span
    scattered = span < width
    vector_queue = {"left": list("kxs" if scattered else "kxylh"), "open": [], "slot": 0}

    def part_of(index):
        return vectors.at[:, pl.ds(pl.multiple_of(index * span, span), span)]

    def start_vectors():
        axis = vector_queue["left"].pop(0)
        if axis == "s":
            for step in range(1, plan.seq):
                there = lax.rem(seq_at + step, plan.seq)
                target = vector_parts.at[step - 1]
                copy = copies.start(part_of(there), target, (there, ch_at))
                vector_queue["open"].append((copy, None))
            return
        for step in range(1, sizes[axis]):
            there = device_at(moved(place, sizes, axis, step))
            copy = copies.start(vectors, vector_in.at[vector_queue["slot"]], there)
            vector_queue["open"].append((copy, vector_queue["slot"]))
            vector_queue["slot"] += 1

    def pump_vectors():
        found, vector_queue["open"] = vector_queue["open"], []
        for copy, _ in found:
            copy.wait()
        for _, slot in found:
            if slot is not None:
                vectors[...] += vector_in[slot]
        if vector_queue["left"]:
            start_vectors()
        elif found:
            total = part_of(seq_at)[...] if scattered else vectors[...]
            for step in range(plan.seq - 1 if scattered else 0):
                total = total + vector_parts[step]
            outputs["vectors"][...] = total

    def pump(point, finish_mix=None):
        for short_name in PUMPS[point]:
            if short_name == "!":
                finish_mix()
                continue
            if short_name[0] == "E":
                if short_name in exchanges:
                    start_expand(int(short_name[1:]))
                continue
            if short_name == "*":
                pump_vectors()
                continue
            piece = pieces.get(short_name)
            if piece is not None and piece.copies:
                piece.advance()

    hand_over("contract", grad_contracted)
    hand_over("gate", grad_logit)
    for index in range(panel_count):

        def store_expanded(columns, product, index=index):
            start = pl.multiple_of(columns.start + index * width, MATMUL_WIDE)
            spot = pl.ds(start, MATMUL_WIDE)
            positive = jnp.sqrt(both_hidden[first_rows, spot].astype(F32))
            grad_expanded[:, spot] = (product * 2.0 * positive).astype(BF16)

        matmul(grad_contracted, panels.take(), NT, store_expanded)
        panels.release()
        if index == 0:
            settle("hidden", "back_contract")
            start_pieces("c")
    for step, copy in enumerate(across, 1):
        copy.wait()
        exchanges["expand"].append(
            copies.start(
                block_of(both_expand, 2 * step), block_of(both_expand, 2 * step + 1), partner
            )
        )

    def send_expanded(cut):
        if cut >= plan.expand_cuts:
            return
        part = plan.broad // plan.expand_cuts
        found = exchanges["E" + str(cut)] = []
        targets = [({**place, "k": 1 - place["k"]}, 0)]
        for step in range(1, sizes["x"]):
            there = moved(place, sizes, "x", step)
            targets.append((there, 2 * step - 1))
            targets.append(({**there, "k": 1 - place["k"]}, 2 * step))
        for there, slot in targets:
            start = (there["x"] * 2 + there["k"]) * plan.broad + cut * part
            found.append(
                copies.start(
                    grad_expanded.at[:, pl.ds(pl.multiple_of(start, part), part)],
                    their_expanded.at[pl.ds(slot * rows, rows), pl.ds(cut * part, part)],
                    device_at(there),
                )
            )

    def start_expand(cut):
        if "expand" in exchanges:
            settle("expand")
        settle("E" + str(cut))
        pieces["e" + str(cut)].start()

    send_expanded(0)
    pump(0)
    for index in range(panel_count):

        def add_expand(columns, product, index=index):
            if index:
                product = product + wide["total"][:, columns]
            wide["total"][:, columns] = product

        matmul(
            grad_expanded,
            panels.take(),
            NT,
            add_expand,
            left_columns=pl.ds(index * width, width),
        )
        panels.release()

    def store_gate(columns, product):
        wide["middle"][:, columns] = product

    matmul(grad_logit, panels.take(), NT, store_gate)
    panels.release()

    for slot in range(slots):
        spot = slice(slot * length, slot * length + 8)
        edge = wide["total"][spot, :] * (1.0 - blends[0][...])
        edge = edge + wide["middle"][spot, :] * (1.0 - blends[1][...])
        edges_out[2, slot : slot + 1, :] = edge[:1, :]
    edge_copy = copies.start(edges_out.at[2], edges_in.at[2], before)
    send_expanded(1)
    settle("gate", "back_gate")
    start_pieces("g")
    pump(1)
    grad_branch = held["rows_2"]

    def first_row_after(slot, index):
        return pl.ds(pl.multiple_of(slot * length + (index + 1) * TILE, 8), 8)

    def ffn_back_earlier(spot):
        earlier = wide["total"][spot, :] * (1.0 - blends[0][...])
        return earlier + wide["middle"][spot, :] * (1.0 - blends[1][...])

    def ffn_back_tile(slot, index, carry):
        spot = tiles_of(slot, index)
        in_expand, in_gate = wide["total"][spot, :], wide["middle"][spot, :]
        gap = wide["gap"][spot, :]
        unit = wide["unit"][spot, :]
        add_vector("blend_key", in_expand * gap)
        add_vector("blend_gate", in_gate * gap)
        earlier = ffn_back_earlier(spot)
        grad_normed = in_expand * blends[0][...] + in_gate * blends[1][...]
        grad_normed = grad_normed + shift_up(earlier, carry)
        add_vector("gain_ffn", grad_normed * unit)
        add_vector("bias_ffn", grad_normed)
        scaled = grad_normed * gain_ffn[...]
        centered = scaled - jnp.mean(scaled, axis=-1, keepdims=True)
        centered = centered - unit * jnp.mean(scaled * unit, axis=-1, keepdims=True)
        _, _, filled = counts(slot, (TILE, width), index * TILE)
        grad = jnp.where(filled, grad_out[spot, :].astype(F32), 0.0)
        grad = grad + factor_ffn[spot, :1] * centered
        wide["total"][spot, :] = grad
        grad_branch[spot, :] = grad.astype(BF16)

    for slot in range(slots):

        def ffn_back_step(index, carry, slot=slot):
            ffn_back_tile(slot, index, ffn_back_earlier(first_row_after(slot, index))[:1, :])
            return carry

        lax.fori_loop(0, steps_in_slot - 1, ffn_back_step, 0)
    edge_copy.wait()
    for slot in range(slots):
        ffn_back_tile(slot, steps_in_slot - 1, edges_in[2, slot : slot + 1, :] * keep_next)

    hand_over("output", grad_branch)
    pump(2)
    grad_recept = held["rows_3"]

    def gated_back(columns, product):
        gate = wide["sigmoid"][:, columns]
        bonus = jnp.exp(time_first[:, columns] + key_ref[:, columns].astype(F32))
        norm = wide["den"][:, columns] + bonus
        wkv = (wide["num"][:, columns] + bonus * value_ref[:, columns].astype(F32)) / norm
        sent = wkv.astype(BF16).astype(F32)
        grad_wkv = (product * gate).astype(BF16).astype(F32)
        grad_recept[:, columns] = (product * sent * gate * (1.0 - gate)).astype(BF16)
        upper_part = grad_wkv / norm
        wide["middle"][:, columns] = upper_part
        wide["gap"][:, columns] = -upper_part * wkv

    matmul(grad_branch, panels.take(), NT, gated_back)
    panels.release()
    hand_over("recept", grad_recept)
    pump(3)

    for slot in range(slots):

        def adjoint_step(index, carry, slot=slot):
            columns = pl.ds(pl.multiple_of(index * WIDE, WIDE), WIDE)
            spot = pl.ds(slot * length, length)
            rate = jnp.exp(time_decay[:, columns])
            earlier, upto, _ = counts(slot, (length, WIDE), 0)
            faded = jnp.exp(-rate * earlier)
            raised = jnp.exp(rate * upto)
            for pair, (source, target) in enumerate((("middle", "sigmoid"), ("gap", "unit"))):
                terms = faded * wide[source][spot, columns]
                wide[target][spot, columns] = raised * triangle(upper, terms)
                at = pair * slots + slot
                sums_out[1, at : at + 1, columns] = jnp.sum(terms, axis=0, keepdims=True)
            return carry

        lax.fori_loop(0, width // WIDE, adjoint_step, 0)
    sum_copies = share(1)
    send_expanded(2)
    send_expanded(3)
    settle("output", "back_output")
    start_pieces("o")
    settle("recept", "back_recept")
    start_pieces("r")
    pump(4)
    for copy in sum_copies:
        copy.wait()
    later = held["later"]
    later[...] = jnp.zeros_like(later)
    for slot in range(slots):
        size = lengths[slot]
        done = jnp.minimum(size, (ch_at + 1) * length)
        for pair in range(2):
            at = pair * slots + slot
            total = jnp.zeros((1, width), F32)
            for step in range(1, ch_size):
                source = lax.rem(ch_at + ch_size - step, ch_size)
                reached = jnp.minimum(size, source * length)
                gone = jnp.maximum(reached - done, 0).astype(F32)
                term = sums_in[1, step - 1, at : at + 1, :]
                total = total + jnp.where(source > ch_at, jnp.exp(-rate_row * gone) * term, 0.0)
            later[at : at + 1, :] = total

    grad_key, grad_value = held["rows_0"], held["rows_1"]
    for slot in range(slots):

        def wkv_back_step(index, carry, slot=slot):
            spot = tiles_of(slot, index)
            _, upto, filled = counts(slot, (TILE, width), index * TILE)
            left = filled_here[slot].astype(F32) - upto
            faded = jnp.exp(-rate_row * left)
            adj_num = wide["sigmoid"][spot, :] + faded * later[slot : slot + 1, :]
            adj_den = wide["unit"][spot, :] + faded * later[slots + slot : slots + slot + 1, :]
            keys, values = key_ref[spot, :].astype(F32), value_ref[spot, :].astype(F32)
            bonus = jnp.exp(time_first[...] + keys)
            weight = jnp.where(filled, jnp.exp(keys), 0.0)
            upper_part, lower_part = wide["middle"][spot, :], wide["gap"][spot, :]
            direct = (upper_part * values + lower_part) * bonus
            grad_value[spot, :] = (upper_part * bonus + weight * adj_num).astype(BF16)
            grad_key[spot, :] = (direct + weight * (adj_num * values + adj_den)).astype(BF16)
            add_vector("time_first", direct)
            decay = adj_num * wide["num"][spot, :] + adj_den * wide["den"][spot, :]
            add_vector("time_decay", jnp.where(filled, decay, 0.0))
            return carry

        lax.fori_loop(0, steps_in_slot, wkv_back_step, 0)
    decay_at = VECTORS.index("time_decay")
    vectors[decay_at : decay_at + 1, :] *= -rate_row * jnp.exp(-rate_row)

    hand_over("key", grad_key)
    hand_over("value", grad_value)
    pump(5)

    def keeper(name):
        def keep(columns, product):
            wide[name][:, columns] = product

        return keep

    for source, name in ((grad_key, "sigmoid"), (grad_value, "unit"), (grad_recept, "gap")):
        matmul(source, panels.take(), NT, keeper(name))
        panels.release()
    in_names = ("sigmoid", "unit", "gap")
    for slot in range(slots):
        spot = slice(slot * length, slot * length + 8)
        edge = jnp.zeros((8, width), F32)
        for name, weights in zip(in_names, mixes):
            edge = edge + wide[name][spot, :] * (1.0 - weights[...])
        edges_out[3, slot : slot + 1, :] = edge[:1, :]
    edge_copy = copies.start(edges_out.at[3], edges_in.at[3], before)
    for name in ("key", "value"):
        settle(name, "back_" + name)
        start_pieces(name[0])
    pump(6)

    in_carry = [edges_in[0, slot : slot + 1, :] for slot in range(slots)]
    vector_names = ("mix_key", "mix_value", "mix_recept")

    def mix_back_earlier(spot):
        earlier = wide[in_names[0]][spot, :] * (1.0 - mixes[0][...])
        for name, weights in zip(in_names[1:], mixes[1:]):
            earlier = earlier + wide[name][spot, :] * (1.0 - weights[...])
        return earlier

    def mix_back_tile(slot, index, before_row, after_row):
        spot = tiles_of(slot, index)
        unit, factor = normalize(tokens[spot, :].astype(F32))
        normed = unit * gain_mix[...] + bias_mix[...]
        gap = normed - shift_down(normed, before_row)
        grad_normed = shift_up(mix_back_earlier(spot), after_row)
        for name, weights, vector in zip(in_names, mixes, vector_names):
            grad = wide[name][spot, :]
            add_vector(vector, grad * gap)
            grad_normed = grad_normed + grad * weights[...]
        add_vector("gain_mix", grad_normed * unit)
        add_vector("bias_mix", grad_normed)
        scaled = grad_normed * gain_mix[...]
        centered = scaled - jnp.mean(scaled, axis=-1, keepdims=True)
        centered = centered - unit * jnp.mean(scaled * unit, axis=-1, keepdims=True)
        grad = wide["total"][spot, :] + factor * centered
        outputs["grad_tokens"][spot, :] = grad.astype(BF16)

    def next_row(slot, index):
        return mix_back_earlier(first_row_after(slot, index))[:1, :]

    last_tile = steps_in_slot - 1
    for slot in range(slots):

        def mix_back_step(index, carry, slot=slot):
            mix_back_tile(slot, index, mix_carry(slot, index), next_row(slot, index))
            return carry

        lax.fori_loop(1, last_tile, mix_back_step, 0)
        if last_tile:
            mix_back_tile(slot, 0, in_carry[slot], next_row(slot, 0))
    def finish_mix():
        edge_copy.wait()
        for slot in range(slots):
            after_row = edges_in[3, slot : slot + 1, :] * keep_next
            before_row = mix_carry(slot, last_tile) if last_tile else in_carry[slot]
            mix_back_tile(slot, last_tile, before_row, after_row)
        start_vectors()

    pump(7, finish_mix)
    for cut in range(plan.expand_cuts):
        if "E" + str(cut) in exchanges:
            start_expand(cut)
    while any(piece.copies for piece in pieces.values()):
        for piece in pieces.values():
            if piece.copies:
                piece.advance()
    while vector_queue["open"]:
        pump_vectors()


LARGE = tuple(name for name in OUTPUTS if name not in ("final", "vectors"))


def place_outputs(plan, *refs):
    count = len(LARGE)
    refs = list(refs)

    def take(number):
        return [refs.pop(0) for _ in range(number)]

    sources, (final, vectors) = take(count), take(2)
    targets, finals, parts = take(count), take(2), take(len(VECTORS))
    slots = plan.slots
    for index, target in enumerate(finals):
        target[...] = final[index * slots : (index + 1) * slots, :]
    part = plan.width // (plan.seq * plan.ch)
    at = lax.axis_index("ch") * part
    span = plan.vector_span
    if span == plan.width:
        at = at + lax.axis_index("seq") * plan.short
    turned = pltpu.roll(vectors[...], lax.rem(span - at, span), 1)
    for index, target in enumerate(parts):
        target[...] = turned[index, :part]
    for source, target in zip(sources, targets):
        target[...] = source[...]


def body(*arguments):
    values = dict(zip(INPUTS, arguments))
    plan = Plan(values["tokens"], values["w_expand"])
    rows, width = plan.rows, plan.width
    operands, specs = [], []
    for name in INPUTS:
        value = values[name]
        space = pltpu.VMEM
        if name in ("tokens", "grad_out"):
            value = value.reshape(rows, width)
        elif name == "lengths":
            space = pltpu.SMEM
        elif name.startswith("w_"):
            space = pl.ANY
        elif value.ndim == 1:
            value = value.reshape(1, width)
        operands.append(value)
        specs.append(pl.BlockSpec(memory_space=space))
    outs = {
        "mixed_out": ((rows, width), BF16),
        "grad_tokens": ((rows, width), BF16),
        "final": ((8, plan.narrow), F32),
        "grad_key": ((plan.short, plan.narrow), F32),
        "grad_value": ((plan.short, plan.narrow), F32),
        "grad_recept": ((plan.short, plan.narrow), F32),
        "grad_output": ((plan.short, plan.narrow), F32),
        "grad_expand": ((plan.short, plan.broad), F32),
        "grad_contract": ((plan.tall, plan.narrow), F32),
        "grad_gate": ((plan.short, plan.narrow), F32),
        "vectors": ((16, plan.vector_span), F32),
    }
    results = pl.pallas_call(
        functools.partial(layer_kernel, plan),
        out_shape=[jax.ShapeDtypeStruct(*outs[name]) for name in OUTPUTS],
        in_specs=specs,
        out_specs=[pl.BlockSpec(memory_space=pltpu.VMEM)] * len(OUTPUTS),
        scratch_shapes=list(plan.shapes.values()),
        compiler_params=pltpu.CompilerParams(
            collective_id=0, has_side_effects=True, vmem_limit_bytes=63 * 2**20
        ),
    )(*operands)
    part = width // (plan.seq * plan.ch)
    slots = plan.slots
    got = dict(zip(OUTPUTS, results))
    vmem = pl.BlockSpec(memory_space=pltpu.VMEM)
    shapes = [outs[name] for name in LARGE] + [((slots, plan.narrow), F32)] * 2
    shapes += [((part,), F32)] * len(VECTORS)
    results = pl.pallas_call(
        functools.partial(place_outputs, plan),
        out_shape=[jax.ShapeDtypeStruct(*shape) for shape in shapes],
        in_specs=[vmem] * (len(LARGE) + 2),
        out_specs=[vmem] * len(shapes),
        compiler_params=pltpu.CompilerParams(vmem_limit_bytes=60 * 2**20),
    )(*[got[name] for name in LARGE], got["final"], got["vectors"])
    mixed_out, grad_tokens, *weights = results[: len(LARGE)]
    shape = values["tokens"].shape
    return (
        mixed_out.reshape(shape),
        grad_tokens.reshape(shape),
        *results[len(LARGE) : len(LARGE) + 2],
        *weights,
        *results[len(LARGE) + 2 :],
    )


def solution(mesh):
    split, copied = P("seq", "ch", None), P()
    placed = (split, split, P("seq"), P("seq", None), P("seq", None)) + (copied,) * 18
    both = P("seq", "ch")
    return jax.shard_map(
        body,
        mesh=mesh,
        in_specs=placed,
        out_specs=(split, split) + (both,) * 9 + (P(("seq", "ch")),) * 11,
        check_vma=False,
    )
```
